32 devices in a mesh: section: 2 (over y), dp: 16 (over z, x, core).
Axes of the slice: x: 2, y: 2, z: 4, core: 2. Of those that a mesh axis runs over, the one named last changes fastest.
Arguments:
- tokens: bfloat16 [2, 32768, 512], P('section', 'dp'), may hold values from -6 to 6
- cotangent: bfloat16 [2, 32768, 512], P('section', 'dp'), may hold values from -6 to 6
- lengths: int32 [2, 64], P(None, 'dp'), may hold values from 256 to 512, as said below
- owners: int32 [2, 9], P('section'), may hold values from 0 to 15, as said below
- master_sq: float32 [2, 16, 6, 512, 512], P('section', 'dp'), may hold values from -1.06066017 to 1.06066017, as said below
- mom1_sq: float32 [2, 16, 6, 512, 512], P('section', 'dp'), may hold values from -256 to 256
- mom2_sq: float32 [2, 16, 6, 512, 512], P('section', 'dp'), may hold values from 983.04 to 8192
- master_vec: float32 [2, 16, 11, 512], P('section', 'dp'), may hold values from -0.9 to 1.75, as said below
- mom1_vec: float32 [2, 16, 11, 512], P('section', 'dp'), may hold values from -256 to 256
- mom2_vec: float32 [2, 16, 11, 512], P('section', 'dp'), may hold values from 983.04 to 8192
Outputs:
- hidden: bfloat16 [2, 32768, 512], P('section', 'dp')
- d_tokens: float32 [2, 32768, 512], P('section', 'dp')
- new_master_sq: float32 [2, 16, 6, 512, 512], P('section', 'dp')
- new_mom1_sq: float32 [2, 16, 6, 512, 512], P('section', 'dp')
- new_mom2_sq: float32 [2, 16, 6, 512, 512], P('section', 'dp')
- new_master_vec: float32 [2, 16, 11, 512], P('section', 'dp')
- new_mom1_vec: float32 [2, 16, 11, 512], P('section', 'dp')
- new_mom2_vec: float32 [2, 16, 11, 512], P('section', 'dp')
The draws below stay inside these ranges and needn't reach their ends.
Inputs may be any that keep to these rules, and one draw needn't show every extreme that they name: `lengths`: positions from the length to 512 are padding; each row has a block of exactly 512. `owners`: the matrix units that one device owns fill at most 6 slots; in each section some device fills all 6. `master_sq`: slots that hold no unit by slot_map are not read. `master_vec`: only the owner's pack is read.
All inputs are finite; a program needn't handle non-finite values.
Results may differ from the reference program's by a relative error of at most 0.012.
Values may be sent and summed in bfloat16 or wider, within the bound.
A program may use at most 448 MiB of HBM per device.

```python
import math
import jax
import jax.numpy as jnp
import numpy as np
from jax import lax

D = 512
HEADS = 8
FF = 2048
P_SIZE = 512
BLK_DEV = 4
STEP = 5
VROWS = 11
CAP = 6
BLOCKS = 64
TOKENS = 32768
N_DP = 16


def unit_tables_drawn(owner_row):
    ratio_units = FF // D
    tensor_sizes = np.array([1] * 6 + [ratio_units, ratio_units], dtype=np.int32)
    tensor_of = np.repeat(np.arange(8), tensor_sizes)
    first_unit = np.concatenate([np.zeros(1, np.int32), np.cumsum(tensor_sizes)[:-1]]).astype(np.int32)
    owned_by = owner_row[:8]
    earlier = (owned_by[:, None] == owned_by[None, :]) & jnp.asarray(np.arange(8)[None, :] < np.arange(8)[:, None])
    prior_units = jnp.sum(jnp.where(earlier, jnp.asarray(tensor_sizes)[None, :], 0), axis=1).astype(jnp.int32)
    unit_owner = owned_by[tensor_of]
    unit_slot = prior_units[tensor_of] + jnp.asarray(np.arange(tensor_of.shape[0]) - first_unit[tensor_of], dtype=jnp.int32)
    return (unit_owner, unit_slot)


def owner_table(key):
    section_rows = []
    for section_index in range(2):
        section_key = jax.random.fold_in(key, 101 + section_index)
        devices = jax.random.permutation(jax.random.fold_in(section_key, 1), N_DP)[:4].astype(jnp.int32)
        squares = jax.random.permutation(jax.random.fold_in(section_key, 2), 6)
        places = jnp.stack([devices[0], devices[0], devices[2], devices[2], devices[3], devices[1]])
        matrices = jnp.zeros(8, jnp.int32).at[squares].set(places).at[6].set(devices[0]).at[7].set(devices[1])
        vector_owner = jax.random.randint(jax.random.fold_in(section_key, 3), (1,), 0, N_DP).astype(jnp.int32)
        section_rows.append(jnp.concatenate([matrices, vector_owner]))
    return jnp.stack(section_rows)


def slot_scales(owner_grid):
    ratio_units = FF // D
    tensor_sizes = np.array([1] * 6 + [ratio_units, ratio_units], dtype=np.int32)
    result = []
    for section_index in range(2):
        unit_owner, unit_slot = unit_tables_drawn(owner_grid[section_index])
        factors = np.ones(8, np.float32)
        factors[3] = 8.0
        if section_index == 1:
            factors[5] = 8.0
        factors[7] = (D / FF) ** 0.5
        unit_factor = jnp.asarray(np.repeat(factors, tensor_sizes))
        slot_hits = (unit_owner[None, None, :] == jnp.arange(N_DP, dtype=jnp.int32)[:, None, None]) & (unit_slot[None, None, :] == jnp.arange(CAP, dtype=jnp.int32)[None, :, None])
        slot_scale = jnp.sum(jnp.where(slot_hits, unit_factor, 0.0), axis=-1) + 1.0 - jnp.any(slot_hits, axis=-1).astype(jnp.float32)
        result.append(slot_scale)
    return jnp.stack(result)


def draw_owners(key, part):
    return owner_table(key)


def draw_master_sq(key, part):
    drawn_key = jax.random.fold_in(key, 7)
    scales = slot_scales(owner_table(key))
    shape = (2, N_DP, CAP, D, D)
    raw_noise = jax.random.truncated_normal(drawn_key, -3.0, 3.0, shape, jnp.float32)
    return raw_noise * scales[..., None, None] * D ** (-0.5)


def draw_master_vec(key, part):
    drawn_key = jax.random.fold_in(key, 9)
    shape = (2, N_DP, VROWS, D)
    raw_noise = jax.random.truncated_normal(drawn_key, -3.0, 3.0, shape, jnp.float32)
    row_index = jnp.arange(VROWS)[:, None]
    return jnp.where(row_index < 3, 1.0 + 0.25 * raw_noise, 0.3 * raw_noise)


def draw_lengths(key, part):
    drawn_key = jax.random.fold_in(key, 5)
    picked = jax.random.randint(jax.random.fold_in(drawn_key, 1), (2, BLOCKS), P_SIZE // 2, P_SIZE + 1)
    full_block = jax.random.randint(jax.random.fold_in(drawn_key, 2), (2, 1), 0, BLOCKS)
    return jnp.where(jnp.arange(BLOCKS)[None, :] == full_block, P_SIZE, picked).astype(jnp.int32)


def block_levels(key, dims, pieces, least, largest):
    level, own = 1.0, jax.random.fold_in(key, 6)
    for dim, blocks in pieces:
        steps = jnp.exp(jax.random.uniform(jax.random.fold_in(own, dim), (blocks,), jnp.float32, least / len(pieces), largest / len(pieces)))
        level = level * jnp.repeat(steps, dims[dim] // blocks).reshape([-1 if axis == dim else 1 for axis in range(len(dims))])
    return level


def gaussian(own_key, extent, scale, bound, shards=(), kind=jnp.bfloat16):
    level = block_levels(own_key, extent, shards, -0.22, 0.18) if shards else 1.0
    drawn = jax.random.normal(own_key, extent, jnp.float32) * scale * level
    return jnp.minimum(jnp.maximum(drawn, -bound), bound).astype(kind)


def setup_inputs(seed: int = 0) -> dict:
    splits = jax.random.split(jax.random.key(seed), 11)
    return {
        "tokens": gaussian(splits[0], (2, TOKENS, D), 1.0, 6.0, ((0, 2), (1, 16))),
        "cotangent": gaussian(splits[1], (2, TOKENS, D), 1.0, 6.0, ((0, 2), (1, 16))),
        "lengths": draw_lengths(jax.random.fold_in(splits[10], 71), 0),
        "owners": draw_owners(jax.random.fold_in(splits[10], 71), 0),
        "master_sq": draw_master_sq(jax.random.fold_in(splits[10], 71), 0),
        "mom1_sq": gaussian(splits[5], (2, N_DP, CAP, D, D), (0.25 * TOKENS ** 0.5), 256.0, ((0, 2), (1, 16)), jnp.float32),
        "mom2_sq": jnp.clip(jnp.exp(math.log(8192.0) - 2.1202636 * jax.random.uniform(splits[6], (2, N_DP, CAP, D, D), jnp.float32) ** block_levels(splits[6], (2, N_DP, CAP, D, D), ((0, 2), (1, 16)), -0.2, 0.2)), 983.04, 8192.0),
        "master_vec": draw_master_vec(jax.random.fold_in(splits[10], 71), 0),
        "mom1_vec": gaussian(splits[8], (2, N_DP, VROWS, D), (0.25 * TOKENS ** 0.5), 256.0, ((0, 2), (1, 16)), jnp.float32),
        "mom2_vec": jnp.clip(jnp.exp(math.log(8192.0) - 2.1202636 * jax.random.uniform(splits[9], (2, N_DP, VROWS, D), jnp.float32) ** block_levels(splits[9], (2, N_DP, VROWS, D), ((0, 2), (1, 16)), -0.2, 0.2)), 983.04, 8192.0),
    }


@jax.custom_vjp
def low(v):
    return lax.optimization_barrier(v.astype(jnp.bfloat16)).astype(jnp.float32)

@jax.custom_vjp
def low_back(v):
    return v

def low_keep(v):
    return (low(v), None)

def low_pass(kept, grad):
    return (grad,)

def back_keep(v):
    return (v, None)

def back_low(kept, grad):
    return (low(grad),)
low.defvjp(low_keep, low_pass)
low_back.defvjp(back_keep, back_low)
highest = lax.Precision.HIGHEST
matrix_rate = 0.04
vector_rate = 0.25
matrix_decay = 0.01

def rounded(value):
    return low(low_back(value))

def dense_product(left, right):
    return jnp.dot(left, right, precision=highest)

def normalize(value, gain, shift):
    centred = value - lax.optimization_barrier(jnp.mean(value, axis=-1, keepdims=True))
    spread = lax.optimization_barrier(jnp.mean(centred * centred, axis=-1, keepdims=True))
    return centred * lax.rsqrt(spread + 1e-05) * gain + shift

def attention(queries, keys_in, values_in, allowed):
    block_count, block_rows, model_width = queries.shape
    head_size = model_width // HEADS
    query_heads = queries.reshape(block_count, block_rows, HEADS, head_size)
    key_heads = keys_in.reshape(block_count, keys_in.shape[1], HEADS, head_size)
    value_heads = values_in.reshape(block_count, values_in.shape[1], HEADS, head_size)
    scores = jnp.einsum('bqhd,bkhd->bhqk', query_heads, key_heads, precision=highest) * head_size ** (-0.5)
    scores = low_back(scores)
    scores = jnp.where(allowed[:, None], scores, -1000000000.0)
    row_max = lax.optimization_barrier(jnp.max(scores, axis=-1, keepdims=True))
    exponent = jnp.exp(scores - row_max)
    softmax_weights = low(exponent / lax.optimization_barrier(jnp.sum(exponent, axis=-1, keepdims=True)))
    attended = jnp.einsum('bhqk,bkhd->bqhd', softmax_weights, value_heads, precision=highest)
    return rounded(attended.reshape(block_count, block_rows, model_width))

def self_branch(source, squares, allowed, block_count):
    entry_rounded = low(source)
    queries = rounded(dense_product(entry_rounded, squares[0]))
    keys_made = rounded(dense_product(entry_rounded, squares[1]))
    values_made = rounded(dense_product(entry_rounded, squares[2]))
    block_shape = (block_count, -1, source.shape[-1])
    attended = attention(queries.reshape(block_shape), keys_made.reshape(block_shape), values_made.reshape(block_shape), allowed)
    return low_back(dense_product(attended.reshape(source.shape), squares[3]))

def feed_forward(source, up_matrix, down_matrix, vector):
    pre_active = low_back(dense_product(low(source), up_matrix) + vector[7:].reshape(-1))
    active = low(jax.nn.gelu(pre_active, approximate=True))
    return low_back(dense_product(active, down_matrix) + vector[6])

def encoder(source_tokens, squares, up_matrix, down_matrix, vector, allowed, block_count):
    entry_norm = normalize(source_tokens, vector[0], vector[3])
    settled = normalize(entry_norm + self_branch(entry_norm, squares, allowed, block_count), vector[1], vector[4])
    memory = normalize(settled + feed_forward(settled, up_matrix, down_matrix, vector), vector[2], vector[5])
    source = low(memory)
    return (memory, rounded(dense_product(source, squares[4])), rounded(dense_product(source, squares[5])))

def decoder_lower(source_tokens, squares, vector, allowed, block_count):
    return normalize(source_tokens + self_branch(source_tokens, squares, allowed, block_count), vector[0], vector[3])

def decoder_upper(lower_out, keys_in, values_in, squares, up_matrix, down_matrix, vector, allowed, block_count):
    queries = rounded(dense_product(low(lower_out), squares[4]))
    block_shape = (block_count, -1, lower_out.shape[-1])
    attended = attention(queries.reshape(block_shape), keys_in.reshape(block_shape), values_in.reshape(block_shape), allowed)
    crossed = normalize(lower_out + low_back(dense_product(attended.reshape(lower_out.shape), squares[5])), vector[1], vector[4])
    return normalize(crossed + feed_forward(crossed, up_matrix, down_matrix, vector), vector[2], vector[5])

def build_masks(enc_lengths, dec_lengths, block_rows):
    positions = jnp.arange(block_rows, dtype=jnp.int32)
    key_pos = positions[None, None, :]
    query_pos = positions[None, :, None]
    enc_allowed = jnp.broadcast_to(key_pos < enc_lengths[:, None, None], (enc_lengths.shape[0], block_rows, block_rows))
    dec_allowed = (key_pos <= query_pos) & (key_pos < dec_lengths[:, None, None])
    return (enc_allowed, dec_allowed)

def unit_tables(owner_row):
    ratio_units = FF // D
    tensor_sizes = np.array([1] * 6 + [ratio_units, ratio_units], dtype=np.int32)
    tensor_of = np.repeat(np.arange(8), tensor_sizes)
    first_unit = np.concatenate([np.zeros(1, np.int32), np.cumsum(tensor_sizes)[:-1]]).astype(np.int32)
    owned_by = owner_row[:8]
    earlier = (owned_by[:, None] == owned_by[None, :]) & jnp.asarray(np.arange(8)[None, :] < np.arange(8)[:, None])
    prior_units = lax.optimization_barrier(jnp.sum(jnp.where(earlier, jnp.asarray(tensor_sizes)[None, :], 0), axis=1)).astype(jnp.int32)
    unit_owner = owned_by[tensor_of]
    unit_slot = prior_units[tensor_of] + jnp.asarray(np.arange(tensor_of.shape[0]) - first_unit[tensor_of], dtype=jnp.int32)
    return (unit_owner, unit_slot)

def ownership(unit_owner, unit_slot, dp_index, slot_count):
    slot_ids = jnp.arange(slot_count, dtype=jnp.int32)[:, None]
    return ((unit_owner[None, :] == dp_index) & (unit_slot[None, :] == slot_ids)).astype(jnp.float32)

def split_units(unit_stack):
    ratio_units = FF // D
    squares = unit_stack[:6]
    up_matrix = unit_stack[6:6 + ratio_units].transpose(1, 0, 2).reshape(D, FF)
    down_matrix = unit_stack[6 + ratio_units:].reshape(FF, D)
    return (squares, up_matrix, down_matrix)

def join_units(squares, up_matrix, down_matrix):
    ratio_units = FF // D
    return jnp.concatenate([squares, up_matrix.reshape(D, ratio_units, D).transpose(1, 0, 2), down_matrix.reshape(ratio_units, D, D)], axis=0)

def adam_update(weight, moment_old, square_old, gradient, learn_rate, decay_rate):
    moment_one = 0.5 * moment_old + 0.5 * gradient
    moment_two = 0.5 * square_old + 0.5 * gradient * gradient
    correction = 1.0 - 0.5 ** STEP
    adam_step = moment_one / correction / (jnp.sqrt(moment_two / correction) + 1e-08)
    return (weight - learn_rate * (adam_step + decay_rate * weight), moment_one, moment_two)

def reference(tokens, cotangent, lengths, owners, master_sq, mom1_sq, mom2_sq, master_vec, mom1_vec, mom2_vec):
    tables = []
    params = []
    for section_index in range(2):
        unit_owner, unit_slot = unit_tables(owners[section_index])
        tables.append((unit_owner, unit_slot))
        picked = master_sq[section_index][unit_owner, unit_slot]
        picked = lax.optimization_barrier(picked.astype(jnp.bfloat16)).astype(jnp.float32)
        params.append(split_units(picked) + (master_vec[section_index, owners[section_index, 8]],))
    params = tuple(params)
    block_rows = P_SIZE
    enc_len = lengths[0].reshape(N_DP, BLK_DEV)
    dec_len = lengths[1].reshape(N_DP, BLK_DEV)
    inputs = tokens.astype(jnp.float32).reshape(2, N_DP, BLK_DEV * block_rows, D)

    def group_pass(weights, enc_in, dec_in, enc_lengths, dec_lengths):
        (enc_squares, enc_up, enc_down, enc_vector), (dec_squares, dec_up, dec_down, dec_vector) = weights
        enc_allowed, dec_allowed = build_masks(enc_lengths, dec_lengths, block_rows)
        memory, keys_made, values_made = encoder(enc_in, enc_squares, enc_up, enc_down, enc_vector, enc_allowed, BLK_DEV)
        lower_out = decoder_lower(dec_in, dec_squares, dec_vector, dec_allowed, BLK_DEV)
        return (memory, decoder_upper(lower_out, keys_made, values_made, dec_squares, dec_up, dec_down, dec_vector, enc_allowed, BLK_DEV))
    group_saved = jax.checkpoint(group_pass)

    def forward(weights, enc_all, dec_all):

        def scan_step(scan_carry, slices):
            return (scan_carry, group_saved(weights, *slices))
        return lax.scan(scan_step, jnp.zeros((), jnp.float32), (enc_all, dec_all, enc_len, dec_len))[1]
    (memory, output), pullback = jax.vjp(forward, params, inputs[0], inputs[1])
    row_mask = jnp.arange(block_rows, dtype=jnp.int32)[None, None, None, :] < lengths.reshape(2, N_DP, BLK_DEV)[..., None]
    row_mask = row_mask.astype(jnp.float32).reshape(2, N_DP, BLK_DEV * block_rows, 1)
    masked_ct = cotangent.astype(jnp.float32).reshape(2, N_DP, BLK_DEV * block_rows, D) * row_mask
    gradients, enc_grad, dec_grad = pullback((masked_ct[0], masked_ct[1]))
    hidden = jnp.stack([memory, output]).reshape(2, TOKENS, D).astype(jnp.bfloat16)
    d_tokens = jnp.stack([enc_grad, dec_grad]).reshape(2, TOKENS, D)
    collected = [[] for position in range(6)]
    for section_index in range(2):
        square_grad, up_grad, down_grad, vector_grad = gradients[section_index]
        grad_units = join_units(square_grad, up_grad, down_grad)
        unit_owner, unit_slot = tables[section_index]
        vector_owner = owners[section_index, 8]

        def one_device(dp_index, slot_store, slot_first, slot_second, vec_store, vec_first, vec_second):
            choose = ownership(unit_owner, unit_slot, dp_index, CAP)
            is_taken = lax.optimization_barrier(jnp.sum(choose, axis=1))[:, None, None] > 0.5
            grad_slots = jnp.einsum('cu,uxy->cxy', choose, grad_units, precision=highest)
            updated = adam_update(slot_store, slot_first, slot_second, grad_slots, matrix_rate, matrix_decay)
            slot_results = [jnp.where(is_taken, fresh_value, stale_value) for fresh_value, stale_value in zip(updated, (slot_store, slot_first, slot_second))]
            owns_vector = vector_owner == dp_index
            vector_new = adam_update(vec_store, vec_first, vec_second, vector_grad, vector_rate, 0.0)
            vector_results = [jnp.where(owns_vector, fresh_value, stale_value) for fresh_value, stale_value in zip(vector_new, (vec_store, vec_first, vec_second))]
            return tuple(slot_results + vector_results)
        results = jax.vmap(one_device)(jnp.arange(N_DP, dtype=jnp.int32), master_sq[section_index], mom1_sq[section_index], mom2_sq[section_index], master_vec[section_index], mom1_vec[section_index], mom2_vec[section_index])
        for position in range(6):
            collected[position].append(results[position])
    stacked = [jnp.stack(entries) for entries in collected]
    return (hidden, d_tokens, stacked[0], stacked[1], stacked[2], stacked[3], stacked[4], stacked[5])
```

```python
import functools
import jax
import jax.numpy as jnp
import numpy as np
from jax import lax
from jax.experimental import pallas as pl
from jax.experimental.pallas import tpu as pltpu
from jax.sharding import PartitionSpec as P

D = 512
HEADS = 8
HS = D // HEADS
FF = 2048
RU = FF // D
STEP = 5
LANES = 128
F32 = jnp.float32
BF = jnp.bfloat16
NEG = -1e30


def nn(a, b):
    return jnp.dot(a, b, preferred_element_type=F32)


def nt(a, b):
    return lax.dot_general(a, b, (((1,), (1,)), ((), ())), preferred_element_type=F32)


def tn(a, b):
    return lax.dot_general(a, b, (((0,), (0,)), ((), ())), preferred_element_type=F32)


def lane_loop(count, body):
    def step(i, carry):
        body(pl.ds(pl.multiple_of(i * LANES, LANES), LANES))
        return carry

    lax.fori_loop(0, count // LANES, step, 0)


def norm_parts(value):
    mean = jnp.mean(value, axis=0, keepdims=True)
    centred = value - mean
    inv = lax.rsqrt(jnp.mean(centred * centred, axis=0, keepdims=True) + 1e-05)
    return centred * inv, inv


def norm_grad(grad, normed, inv, gain):
    scaled = grad * gain
    mean_one = jnp.mean(scaled, axis=0, keepdims=True)
    mean_two = jnp.mean(scaled * normed, axis=0, keepdims=True)
    return (scaled - mean_one - normed * mean_two) * inv


def fill_bias(bias, length, causal):
    rows = bias.shape[0]

    def body(lanes):
        key = lax.broadcasted_iota(jnp.int32, (rows, LANES), 0)
        query = lax.broadcasted_iota(jnp.int32, (rows, LANES), 1) + lanes.start
        allowed = key < length
        if causal is not None:
            allowed = allowed & ((key <= query) | jnp.logical_not(causal))
        bias[:, lanes] = jnp.where(allowed, 0.0, NEG)

    lane_loop(bias.shape[1], body)


def head_rows(h):
    return pl.ds(pl.multiple_of(h * HS, HS), HS)


def attend(qt, kt, vt, bias, ot, lse, pair):
    def score(h, out):
        rows = head_rows(h)
        out[...] = tn(kt[rows, :], qt[rows, :] * BF(0.125))

    def finish(h, scores):
        rows = head_rows(h)
        biased = scores[...] + bias[...]
        top = jnp.max(biased, axis=0, keepdims=True)
        weights = jnp.exp(biased - top).astype(BF)
        values = jnp.concatenate([vt[rows, :], jnp.ones((16, vt.shape[1]), BF)], axis=0)
        out = nn(values, weights)
        total = out[HS : HS + 1]
        ot[rows, :] = (out[:HS] * (1.0 / total)).astype(BF)
        lse[pl.ds(h, 1), :] = top + jnp.log(total)

    one, two = pair.at[0], pair.at[1]
    score(0, one)

    def body(i, carry):
        score(2 * i + 1, two)
        finish(2 * i, one)
        score(jnp.minimum(2 * i + 2, HEADS - 1), one)
        finish(2 * i + 1, two)
        return carry

    lax.fori_loop(0, HEADS // 2, body, 0, unroll=True)


def attend_back(qt, kt, vt, bias, ot, lse, dot, dqt, dkt, dvt):
    def head(h, carry):
        rows = head_rows(h)
        keys, grads = kt[rows, :], dot[rows, :]
        queries = qt[rows, :] * BF(0.125)
        delta = jnp.sum(grads.astype(F32) * ot[rows, :].astype(F32), axis=0, keepdims=True)
        probs = jnp.exp(tn(keys, queries) + bias[...] - lse[pl.ds(h, 1), :])
        dscores = (probs * (tn(vt[rows, :], grads) - delta)).astype(BF)
        dvt[rows, :] = nt(grads, probs.astype(BF)).astype(BF)
        dkt[rows, :] = nt(queries, dscores).astype(BF)
        dqt[rows, :] = (nn(keys, dscores) * 0.125).astype(BF)
        return carry

    lax.fori_loop(0, HEADS, head, 0, unroll=4)


def self_forward(x, sq, vec, causal, length, ut, n0, r0, qt, kt, vt, ot, lse, n1, r1, y, bias, et, pair):
    first = jnp.logical_not(causal)
    tokens = x.shape[0]
    et[...] = x[...].astype(F32).T

    def entry(lanes):
        value = et[:, lanes]
        normed, inv = norm_parts(value)
        n0[:, lanes] = normed.astype(BF)
        r0[:, lanes] = inv
        value = jnp.where(first, normed * vec[:, 0:1] + vec[:, 1:2], value)
        et[:, lanes] = value
        ut[:, lanes] = value.astype(BF)

    lane_loop(tokens, entry)
    fill_bias(bias, length, causal)
    for index, out in enumerate((qt, kt, vt)):
        out[...] = tn(sq[index][...], ut[...]).astype(BF)
    attend(qt, kt, vt, bias, ot, lse, pair)
    et[...] += tn(sq[3][...], ot[...])

    def leave(lanes):
        normed, inv = norm_parts(et[:, lanes])
        n1[:, lanes] = normed.astype(BF)
        r1[:, lanes] = inv
        y[:, lanes] = normed * vec[:, 2:3] + vec[:, 3:4]

    lane_loop(tokens, leave)


def self_backward(dy, sq, vec, causal, length, ut, n0, r0, qt, kt, vt, ot, lse, n1, r1, dx, bias, dsa, dot, dqt, dkt, dvt, dsq, dvec, vacc):
    first = jnp.logical_not(causal)
    tokens = dy.shape[1]
    vacc[...] = jnp.zeros(vacc.shape, F32)

    def leave(lanes):
        grad, normed = dy[:, lanes], n1[:, lanes].astype(F32)
        vacc[2] += grad * normed
        vacc[3] += grad
        grad = norm_grad(grad, normed, r1[:, lanes], vec[:, 2:3])
        dy[:, lanes] = grad
        dsa[:, lanes] = grad.astype(BF)

    lane_loop(tokens, leave)
    fill_bias(bias, length, causal)
    dot[...] = nn(sq[3][...], dsa[...]).astype(BF)
    dsq[3] += nt(ot[...], dsa[...])
    attend_back(qt, kt, vt, bias, ot, lse, dot, dqt, dkt, dvt)
    for index, grad in enumerate((dqt, dkt, dvt)):
        dsq[index] += nt(ut[...], grad[...])
        dy[...] += nn(sq[index][...], grad[...])

    def entry(lanes):
        grad, normed = dy[:, lanes], n0[:, lanes].astype(F32)
        vacc[0] += grad * normed
        vacc[1] += grad
        dy[:, lanes] = jnp.where(first, norm_grad(grad, normed, r0[:, lanes], vec[:, 0:1]), grad)

    lane_loop(tokens, entry)
    dx[...] = dy[...].T
    for index in range(4):
        dvec[:, index : index + 1] += jnp.sum(vacc[index], axis=1, keepdims=True)


def gelu_parts(z):
    root = 0.7978845608028654
    square = z * z
    t = jnp.tanh(z * (root + (root * 0.044715) * square))
    half = 0.5 + 0.5 * t
    act = z * half
    slope = half + act * (1.0 - t) * (root + (3.0 * root * 0.044715) * square)
    return act, slope


def feed_forward(h, units, vec, hb, act, slope, n2, r2, out):
    hb[...] = h[...].astype(BF)
    for c in range(RU):
        rows = slice(c * D, (c + 1) * D)
        a, s = gelu_parts(tn(units[c][...], hb[...]) + vec[:, c : c + 1])
        act[rows, :] = a.astype(BF)
        slope[rows, :] = s.astype(BF)
    for c in range(RU):
        rows = slice(c * D, (c + 1) * D)
        h[...] += tn(units[RU + c][...], act[rows, :])

    def leave(lanes):
        normed, inv = norm_parts(h[:, lanes] + vec[:, RU : RU + 1])
        n2[:, lanes] = normed.astype(BF)
        r2[:, lanes] = inv
        out[:, lanes] = normed * vec[:, RU + 1 : RU + 2] + vec[:, RU + 2 : RU + 3]

    lane_loop(h.shape[1], leave)


def feed_backward(dm, units, vec, hb, act, slope, n2, r2, dfb, dz, dunits, dvec, vacc):
    vacc[...] = jnp.zeros(vacc.shape, F32)

    def leave(lanes):
        grad, normed = dm[:, lanes], n2[:, lanes].astype(F32)
        vacc[RU + 1] += grad * normed
        vacc[RU + 2] += grad
        grad = norm_grad(grad, normed, r2[:, lanes], vec[:, RU + 1 : RU + 2])
        dm[:, lanes] = grad
        short = grad.astype(BF)
        vacc[RU] += short.astype(F32)
        dfb[:, lanes] = short

    lane_loop(dm.shape[1], leave)
    for c in range(RU):
        rows = slice(c * D, (c + 1) * D)
        dz[rows, :] = (nn(units[RU + c][...], dfb[...]) * slope[rows, :].astype(F32)).astype(BF)
        dunits[RU + c][...] += nt(act[rows, :], dfb[...])
    for c in range(RU):
        rows = slice(c * D, (c + 1) * D)
        dm[...] += nn(units[c][...], dz[rows, :])
        dunits[c][...] += nt(hb[...], dz[rows, :])
        for lanes in range(0, dm.shape[1], LANES):
            vacc[c] += dz[rows, lanes : lanes + LANES].astype(F32)
    for index in range(RU + 3):
        dvec[:, index : index + 1] += jnp.sum(vacc[index], axis=1, keepdims=True)


def cross_forward(a, sq, vec, length, ab, cqt, kt, vt, ot, lse, n1, r1, bias, pair):
    ab[...] = a[...].astype(BF)
    cqt[...] = tn(sq[0][...], ab[...]).astype(BF)
    fill_bias(bias, length, None)
    attend(cqt, kt, vt, bias, ot, lse, pair)
    a[...] += tn(sq[1][...], ot[...])

    def leave(lanes):
        normed, inv = norm_parts(a[:, lanes])
        n1[:, lanes] = normed.astype(BF)
        r1[:, lanes] = inv
        a[:, lanes] = normed * vec[:, 0:1] + vec[:, 1:2]

    lane_loop(a.shape[1], leave)


def cross_backward(
    dbq, sq, vec, ab, cqt, kt, vt, ot, lse, n1, r1, bias, dca, dot, dqt, dkt, dvt, dsq, dvec, vacc
):
    vacc[0] = jnp.zeros(vacc.shape[1:], F32)
    vacc[1] = jnp.zeros(vacc.shape[1:], F32)

    def leave(lanes):
        grad, normed = dbq[:, lanes], n1[:, lanes].astype(F32)
        vacc[0] += grad * normed
        vacc[1] += grad
        grad = norm_grad(grad, normed, r1[:, lanes], vec[:, 0:1])
        dbq[:, lanes] = grad
        dca[:, lanes] = grad.astype(BF)

    lane_loop(dbq.shape[1], leave)
    dot[...] = nn(sq[1][...], dca[...]).astype(BF)
    dsq[1][...] += nt(ot[...], dca[...])
    attend_back(cqt, kt, vt, bias, ot, lse, dot, dqt, dkt, dvt)
    dsq[0][...] += nt(ab[...], dqt[...])
    dbq[...] += nn(sq[0][...], dqt[...])
    for index in range(2):
        dvec[:, index : index + 1] += jnp.sum(vacc[index], axis=1, keepdims=True)


SUB = 256
HALF = SUB // 2
QUART = SUB // 4
UNITS = 6 + 2 * RU
SUBS = UNITS * (D // SUB) + 1
MESH = pl.DeviceIdType.MESH
TENSOR_OF = (0, 1, 2, 3, 4, 5) + (6,) * RU + (7,) * RU
TENSOR_SIZE = (1,) * 6 + (RU, RU)
FIRST_UNIT = (0, 1, 2, 3, 4, 5, 6, 6 + RU)


def any_space():
    return pl.BlockSpec(memory_space=pl.ANY)


def vmem_space():
    return pl.BlockSpec(memory_space=pltpu.VMEM)


def smem_space():
    return pl.BlockSpec(memory_space=pltpu.SMEM)


def shape32(*dims):
    return jax.ShapeDtypeStruct(dims, F32)


def shape16(*dims):
    return jax.ShapeDtypeStruct(dims, BF)


def total_over_dp(n_dp, prepare, src, out, core_in, half, x_in, quart, right_in, left_in, right_out, left_out, sems):
    length = n_dp // 4
    section = lax.axis_index("section")
    dp = lax.axis_index("dp")
    core, x, z = dp % 2, (dp // 2) % 2, dp // 4
    sibling, beside = dp + 1 - 2 * core, dp + 2 - 4 * x
    has_left, has_right = z > 0, z < length - 1

    barrier = pltpu.get_barrier_semaphore()

    def greet(index):
        pl.semaphore_signal(barrier, inc=1, device_id=(section, index), device_id_type=MESH)

    greet(sibling)
    greet(beside)
    pl.when(has_left)(lambda: greet(dp - 4))
    pl.when(has_right)(lambda: greet(dp + 4))
    pl.semaphore_wait(barrier, 2 + has_left.astype(jnp.int32) + has_right.astype(jnp.int32))

    def block(t):
        return (t + SUBS - 1) % SUBS

    def base(t):
        return block(t) * SUB

    def rows(start, size):
        return pl.ds(pl.multiple_of(start, QUART), size)

    def send(step, t, source, target, index):
        return pltpu.make_async_remote_copy(
            src_ref=source,
            dst_ref=target,
            send_sem=sems.at[0, step, t],
            recv_sem=sems.at[1, step, t],
            device_id=(section, index),
            device_id_type=MESH,
        )

    def copy_core(t):
        return send(0, t, src.at[rows(base(t) + HALF * (1 - core), HALF)], core_in.at[t], sibling)

    def copy_x(t):
        return send(1, t, half.at[t, rows(QUART * (1 - x), QUART)], x_in.at[t], beside)

    def copy_right(t, source):
        return send(2, t, source.at[t], right_in.at[t], dp + 4)

    def copy_left(t, source):
        return send(3, t, source.at[t], left_in.at[t], dp - 4)

    def copy_back_x(t):
        place = rows(base(t) + HALF * core + QUART * x, QUART)
        return send(4, t, out.at[place], out.at[place], beside)

    def copy_back_core(t):
        place = rows(base(t) + HALF * core, HALF)
        return send(5, t, out.at[place], out.at[place], sibling)

    def add(one, two):
        return (one.astype(F32) + two.astype(F32)).astype(BF)

    def step_core(t):
        prepare(block(t))
        copy_core(t).start()

    def step_x(t):
        copy_core(t).wait_recv()
        half[t] = add(src[rows(base(t) + HALF * core, HALF), :], core_in[t])
        copy_x(t).start()

    def step_quart(t):
        copy_x(t).wait_recv()
        quart[t] = add(half[t, rows(QUART * x, QUART), :], x_in[t])

        @pl.when(jnp.logical_not(has_left) & has_right)
        def _():
            copy_right(t, quart).start()

        @pl.when(jnp.logical_not(has_right) & has_left)
        def _():
            copy_left(t, quart).start()

    def step_right(t):
        @pl.when(has_left)
        def _():
            copy_right(t, right_out).wait_recv()

            @pl.when(has_right)
            def _():
                right_out[t] = add(quart[t], right_in[t])
                copy_right(t, right_out).start()

    def step_left(t):
        @pl.when(has_right)
        def _():
            copy_left(t, left_out).wait_recv()

            @pl.when(has_left)
            def _():
                left_out[t] = add(quart[t], left_in[t])
                copy_left(t, left_out).start()

    def step_total(t):
        place = rows(base(t) + HALF * core + QUART * x, QUART)
        mine = quart[t].astype(F32)
        mine += jnp.where(has_left, right_in[t].astype(F32), 0.0)
        mine += jnp.where(has_right, left_in[t].astype(F32), 0.0)
        out[place, :] = mine.astype(BF)
        copy_back_x(t).start()

    def step_back(t):
        copy_back_x(t).wait_recv()
        copy_back_core(t).start()

    last = length - 1
    lags = (
        (step_core, 0),
        (step_x, 1),
        (step_quart, 2),
        (step_right, 2 + z),
        (step_left, 2 + last - z),
        (step_total, 2 + jnp.maximum(z, last - z)),
        (step_back, 3 + jnp.maximum(z, last - z)),
    )

    def tick(t, carry):
        for step, lag in lags:
            at = t - lag

            @pl.when((at >= 0) & (at < SUBS))
            def _(step=step, at=at):
                step(at)

        return carry

    lax.fori_loop(0, SUBS + 3 + last, tick, 0)

    def settle(t, carry):
        copy_back_core(t).wait_recv()
        copy_core(t).wait_send()
        copy_x(t).wait_send()
        pl.when(has_right)(lambda: copy_right(t, right_out).wait_send())
        pl.when(has_left)(lambda: copy_left(t, left_out).wait_send())
        copy_back_x(t).wait_send()
        copy_back_core(t).wait_send()
        return carry

    lax.fori_loop(0, SUBS, settle, 0)


def total_scratch():
    return [
        pltpu.VMEM((SUBS, HALF, D), BF),
        pltpu.VMEM((SUBS, HALF, D), BF),
        pltpu.VMEM((SUBS, QUART, D), BF),
        pltpu.VMEM((SUBS, QUART, D), BF),
        pltpu.VMEM((SUBS, QUART, D), BF),
        pltpu.VMEM((SUBS, QUART, D), BF),
        pltpu.VMEM((SUBS, QUART, D), BF),
        pltpu.VMEM((SUBS, QUART, D), BF),
        pltpu.SemaphoreType.DMA((2, 6, SUBS)),
    ]


def weights_kernel(n_dp, owners, slots, pack, out, src, *scratch):
    dp = lax.axis_index("dp")

    def slot_of(tensor):
        prior = jnp.int32(0)
        for earlier in range(tensor):
            prior += jnp.where(owners[0, earlier] == owners[0, tensor], TENSOR_SIZE[earlier], 0)
        return prior

    def prepare(sub):
        @pl.when(sub == SUBS - 1)
        def _():
            src[pl.ds((SUBS - 1) * SUB, SUB), :] = pack[...]

        for unit in range(UNITS):

            @pl.when(sub // 2 == unit)
            def _(unit=unit):
                tensor = TENSOR_OF[unit]
                slot = jnp.minimum(slot_of(tensor) + (unit - FIRST_UNIT[tensor]), slots.shape[0] - 1)
                start = pl.multiple_of((sub % 2) * SUB, SUB)
                kept = jnp.where(owners[0, tensor] == dp, slots[slot, pl.ds(start, SUB), :], 0.0)
                src[pl.ds(pl.multiple_of(sub * SUB, SUB), SUB), :] = kept.astype(BF)

    total_over_dp(n_dp, prepare, src, out, *scratch)


def gather_weights(n_dp, owners, slots, pack):
    return pl.pallas_call(
        functools.partial(weights_kernel, n_dp),
        name="gather_weights",
        out_shape=shape16(SUBS * SUB, D),
        in_specs=[smem_space(), vmem_space(), vmem_space()],
        out_specs=vmem_space(),
        scratch_shapes=[pltpu.VMEM((SUBS * SUB, D), BF)] + total_scratch(),
        compiler_params=pltpu.CompilerParams(
            collective_id=0, has_side_effects=True, vmem_limit_bytes=56 * 2**20
        ),
    )(owners, slots, pack)


def gradients_kernel(n_dp, src, out, *scratch):
    total_over_dp(n_dp, lambda sub: None, src, out, *scratch)


def sum_gradients(n_dp, grads):
    return pl.pallas_call(
        functools.partial(gradients_kernel, n_dp),
        name="sum_gradients",
        out_shape=shape16(SUBS * SUB, D),
        in_specs=[vmem_space()],
        out_specs=vmem_space(),
        scratch_shapes=total_scratch(),
        compiler_params=pltpu.CompilerParams(
            collective_id=1, has_side_effects=True, vmem_limit_bytes=56 * 2**20
        ),
    )(grads)


def self_forward_kernel(info, x, sq, vec, ut, n0, r0, qt, kt, vt, ot, lse, n1, r1, y, *scratch):
    block = pl.program_id(0)
    squares = [sq.at[pl.ds(i * D, D)] for i in range(4)]
    saved = [ref.at[0] for ref in (ut, n0, r0, qt, kt, vt, ot, lse, n1, r1, y)]
    self_forward(x, squares, vec, info[0] == 1, info[1 + block], *saved, *scratch)


def block_spec(*dims):
    return pl.BlockSpec((1,) + dims, lambda b, info: (b,) + (0,) * len(dims))


def fixed_spec(*dims):
    return pl.BlockSpec(dims, lambda b, info: (0,) * len(dims))


def saved_shapes(count, tokens):
    wide = shape16(count, D, tokens)
    row = shape32(count, 1, tokens)
    return [wide, wide, row, wide, wide, wide, wide, shape32(count, HEADS, tokens), wide, row]


def call_self_forward(info, x, weights, vec, count, tokens):
    shapes = saved_shapes(count, tokens) + [shape32(count, D, tokens)]
    return pl.pallas_call(
        self_forward_kernel,
        name="self_forward",
        out_shape=shapes,
        grid_spec=pltpu.PrefetchScalarGridSpec(
            num_scalar_prefetch=1,
            grid=(count,),
            in_specs=[
                pl.BlockSpec((tokens, D), lambda b, info: (b, 0)),
                fixed_spec(4 * D, D),
                fixed_spec(D, LANES),
            ],
            out_specs=[block_spec(*s.shape[1:]) for s in shapes],
            scratch_shapes=[
                pltpu.VMEM((tokens, tokens), F32),
                pltpu.VMEM((D, tokens), F32),
                pltpu.VMEM((2, tokens, tokens), F32),
            ],
        ),
        compiler_params=pltpu.CompilerParams(vmem_limit_bytes=56 * 2**20),
    )(info, x, weights, vec)


def self_backward_kernel(info, dy, sq, vec, *refs):
    block = pl.program_id(0)
    saved = [ref.at[0] for ref in refs[:10]]
    dx, dsq_out, dvec, dys, bias, dsa, dot, dqt, dkt, dvt, dsq, vacc = refs[10:]
    squares = [sq.at[pl.ds(i * D, D)] for i in range(4)]

    @pl.when(block == 0)
    def _():
        dsq[...] = jnp.zeros(dsq.shape, F32)
        dvec[...] = jnp.zeros(dvec.shape, F32)

    dys[...] = dy[0]
    self_backward(
        dys, squares, vec, info[0] == 1, info[1 + block], *saved, dx, bias, dsa, dot, dqt, dkt, dvt, dsq, dvec, vacc
    )

    @pl.when(block == pl.num_programs(0) - 1)
    def _():
        for i in range(4):
            dsq_out[i * D : (i + 1) * D, :] = dsq[i].astype(BF)


def call_self_backward(info, dy, weights, vec, saved, count, tokens):
    return pl.pallas_call(
        self_backward_kernel,
        name="self_backward",
        out_shape=[shape32(count * tokens, D), shape16(4 * D, D), shape32(D, LANES)],
        grid_spec=pltpu.PrefetchScalarGridSpec(
            num_scalar_prefetch=1,
            grid=(count,),
            in_specs=[block_spec(D, tokens), fixed_spec(4 * D, D), fixed_spec(D, LANES)]
            + [block_spec(*s.shape[1:]) for s in saved],
            out_specs=[
                pl.BlockSpec((tokens, D), lambda b, info: (b, 0)),
                fixed_spec(4 * D, D),
                fixed_spec(D, LANES),
            ],
            scratch_shapes=[pltpu.VMEM((D, tokens), F32), pltpu.VMEM((tokens, tokens), F32)]
            + [pltpu.VMEM((D, tokens), BF)] * 5
            + [pltpu.VMEM((4, D, D), F32), pltpu.VMEM((4, D, LANES), F32)],
        ),
        compiler_params=pltpu.CompilerParams(vmem_limit_bytes=56 * 2**20),
    )(info, dy, weights, vec, *saved)


def middle_kernel(
    info, vec, y, cot, weights, hidden, dy, grads, dvec,
    wts, acc, sent, got, h, mem, hb, act, slope, n2, r2, dfb, dz, vacc, fvec_acc,
    ab, cqt, kt, vt, ot, lse, n1, r1, bias, dca, dot, dqt, pair, tok, stage, sems, load_sem,
):
    section = lax.axis_index("section")
    dp = lax.axis_index("dp")
    count, tokens = y.shape[0], y.shape[2]
    other = 1 - section
    barrier = pltpu.get_barrier_semaphore()
    pl.semaphore_signal(barrier, inc=1, device_id=(other, dp), device_id_type=MESH)
    pl.semaphore_wait(barrier, 1)

    def move(source, target):
        copy = pltpu.make_async_copy(source, target, load_sem)
        copy.start()
        copy.wait()

    def swap(b):
        return pltpu.make_async_remote_copy(
            src_ref=sent.at[b],
            dst_ref=got.at[b],
            send_sem=sems.at[0, b],
            recv_sem=sems.at[1, b],
            device_id=(other, dp),
            device_id_type=MESH,
        )

    def each(body):
        def step(b, carry):
            body(b)
            return carry

        lax.fori_loop(0, count, step, 0)

    move(weights.at[pl.ds(4 * D, 10 * D)], wts)
    unit = [wts.at[pl.ds(i * D, D)] for i in range(10)]
    s4, s5, ffn = unit[0], unit[1], unit[2:]
    gain = vec.at[:, pl.ds(0, LANES)]
    cross_vec = vec.at[:, pl.ds(LANES, LANES)]
    acc[...] = jnp.zeros(acc.shape, F32)
    fvec_acc[...] = jnp.zeros(fvec_acc.shape, F32)
    cross_acc = [acc.at[i] for i in range(2)]
    ffn_acc = [acc.at[2 + i] for i in range(8)]

    def run_feed_forward():
        feed_forward(h, ffn, gain, hb, act, slope, n2, r2, mem)

    def emit_hidden(b):
        tok[...] = mem[...].T.astype(BF)
        move(tok, hidden.at[pl.ds(pl.multiple_of(b * tokens, tokens), tokens)])

    def load_cotangent(b):
        move(cot.at[pl.ds(pl.multiple_of(b * tokens, tokens), tokens)], tok)
        token = lax.broadcasted_iota(jnp.int32, (D, tokens), 1)
        h[...] = jnp.where(token < info[1 + b], tok[...].astype(F32).T, 0.0)

    def run_feed_backward():
        feed_backward(h, ffn, gain, hb, act, slope, n2, r2, dfb, dz, ffn_acc, fvec_acc.at[0], vacc)

    @pl.when(section == 0)
    def _():
        def ahead(b):
            move(y.at[b], h)
            run_feed_forward()
            emit_hidden(b)
            short = mem[...].astype(BF)
            sent[b, 0] = tn(s4[...], short).astype(BF)
            sent[b, 1] = tn(s5[...], short).astype(BF)
            swap(b).start()

        each(ahead)

        def back(b):
            move(y.at[b], h)
            run_feed_forward()
            ab[...] = mem[...].astype(BF)
            load_cotangent(b)
            swap(b).wait_recv()
            for i, matrix in enumerate((s4, s5)):
                h[...] += nn(matrix[...], got[b, i])
                acc[i] += nt(ab[...], got[b, i])
            run_feed_backward()
            move(h, dy.at[b])

        each(back)

    @pl.when(section == 1)
    def _():
        def both(b):
            move(y.at[b], h)
            swap(b).wait_recv()
            kt[...] = got[b, 0]
            vt[...] = got[b, 1]
            cross_forward(h, (s4, s5), cross_vec, info[1 + count + b], ab, cqt, kt, vt, ot, lse, n1, r1, bias, pair)
            run_feed_forward()
            emit_hidden(b)
            load_cotangent(b)
            run_feed_backward()
            cross_backward(
                h, (s4, s5), cross_vec, ab, cqt, kt, vt, ot, lse, n1, r1, bias, dca, dot, dqt,
                sent.at[b, 0], sent.at[b, 1], cross_acc, fvec_acc.at[1], vacc,
            )
            swap(b).start()
            move(h, dy.at[b])

        each(both)

    def finish(b):
        swap(b).wait_send()

    each(finish)
    for i in range(10):
        stage[...] = acc[i].astype(BF)
        move(stage, grads.at[pl.ds(i * D, D)])
    dvec[...] = fvec_acc[...]


def call_middle(info, vec, y, cot, weights, count, tokens):
    wide16 = pltpu.VMEM((D, tokens), BF)
    wide32 = pltpu.VMEM((D, tokens), F32)
    row = pltpu.VMEM((1, tokens), F32)
    return pl.pallas_call(
        middle_kernel,
        name="middle",
        out_shape=[
            shape16(count * tokens, D),
            shape32(count, D, tokens),
            shape16(10 * D, D),
            shape32(2, D, LANES),
        ],
        in_specs=[smem_space(), vmem_space(), any_space(), any_space(), any_space()],
        out_specs=[any_space(), any_space(), any_space(), vmem_space()],
        scratch_shapes=[
            pltpu.VMEM((10 * D, D), BF),
            pltpu.VMEM((10, D, D), F32),
            pltpu.VMEM((count, 2, D, tokens), BF),
            pltpu.VMEM((count, 2, D, tokens), BF),
            wide32, wide32, wide16,
            pltpu.VMEM((FF, tokens), BF), pltpu.VMEM((FF, tokens), BF),
            wide16, row, wide16,
            pltpu.VMEM((FF, tokens), BF),
            pltpu.VMEM((RU + 3, D, LANES), F32),
            pltpu.VMEM((2, D, LANES), F32),
            wide16, wide16, wide16, wide16, wide16,
            pltpu.VMEM((HEADS, tokens), F32),
            wide16, row,
            pltpu.VMEM((tokens, tokens), F32),
            wide16, wide16, wide16,
            pltpu.VMEM((2, tokens, tokens), F32),
            pltpu.VMEM((tokens, D), BF),
            pltpu.VMEM((D, D), BF),
            pltpu.SemaphoreType.DMA((2, count)),
            pltpu.SemaphoreType.DMA,
        ],
        compiler_params=pltpu.CompilerParams(
            collective_id=2, has_side_effects=True, vmem_limit_bytes=60 * 2**20
        ),
    )(info, vec, y, cot, weights)


matrix_rate = 0.04
vector_rate = 0.25
matrix_decay = 0.01


def adam_update(weight, moment_old, square_old, gradient, learn_rate, decay_rate):
    moment_one = 0.5 * moment_old + 0.5 * gradient
    moment_two = 0.5 * square_old + 0.5 * gradient * gradient
    correction = 1.0 - 0.5**STEP
    adam_step = moment_one / correction / (jnp.sqrt(moment_two / correction) + 1e-08)
    return (weight - learn_rate * (adam_step + decay_rate * weight), moment_one, moment_two)


def adam_kernel(place, grad, weight, first, second, weight_out, first_out, second_out):
    taken = place[pl.program_id(0)] >= 0
    fresh = adam_update(weight[0], first[0], second[0], grad[...].astype(F32), matrix_rate, matrix_decay)
    for new, old, out in zip(fresh, (weight, first, second), (weight_out, first_out, second_out)):
        out[0] = jnp.where(taken, new, old[0])


def call_adam(place, grads, weight, first, second):
    slots = weight.shape[0]
    spec = block_spec(D, D)
    out = shape32(slots, D, D)
    return pl.pallas_call(
        adam_kernel,
        name="adam",
        out_shape=[out] * 3,
        grid_spec=pltpu.PrefetchScalarGridSpec(
            num_scalar_prefetch=1,
            grid=(slots,),
            in_specs=[pl.BlockSpec((D, D), lambda s, place: (jnp.maximum(place[s], 0), 0))] + [spec] * 3,
            out_specs=[spec] * 3,
        ),
    )(place, grads, weight, first, second)


def unit_tables(owner_row):
    tensor_of = np.array(TENSOR_OF)
    first_unit = np.array(FIRST_UNIT)
    owned_by = owner_row[:8]
    earlier = (owned_by[:, None] == owned_by[None, :]) & jnp.asarray(
        np.arange(8)[None, :] < np.arange(8)[:, None]
    )
    prior = jnp.sum(jnp.where(earlier, jnp.array(TENSOR_SIZE, jnp.int32)[None, :], 0), axis=1)
    unit_owner = owned_by[tensor_of]
    unit_slot = prior[tensor_of] + jnp.asarray(np.arange(UNITS) - first_unit[tensor_of], jnp.int32)
    return unit_owner, unit_slot.astype(jnp.int32)


def slot_units(owner_row, dp, slots):
    unit_owner, unit_slot = unit_tables(owner_row)
    hit = (unit_owner[None, :] == dp) & (unit_slot[None, :] == jnp.arange(slots, dtype=jnp.int32)[:, None])
    return jnp.sum(jnp.where(hit, jnp.arange(UNITS, dtype=jnp.int32)[None, :] + 1, 0), axis=1) - 1


def three_pieces(value):
    high = value.astype(BF)
    rest = value - high.astype(F32)
    mid = rest.astype(BF)
    low = (rest - mid.astype(F32)).astype(BF)
    return jnp.concatenate([high, mid, low], axis=0)


def pad_rows(value, rows):
    return jnp.pad(value, ((0, rows - value.shape[0]), (0, 0)))


def columns(rows):
    stacked = jnp.stack(rows, axis=1)
    return jnp.pad(stacked, ((0, 0), (0, LANES - stacked.shape[1])))


def local(n_dp, tokens, cotangent, lengths, owners, master_sq, mom1_sq, mom2_sq, master_vec, mom1_vec, mom2_vec):
    section = lax.axis_index("section")
    dp = lax.axis_index("dp")
    first = section == 0
    count = lengths.shape[1]
    width = tokens.shape[1] // count
    vec_store = master_vec[0, 0]
    vrows = vec_store.shape[0]
    owns_vector = owners[0, 8] == dp
    pack = pad_rows(three_pieces(jnp.where(owns_vector, vec_store, 0.0)), SUB)
    weights = gather_weights(n_dp, owners, master_sq[0, 0], pack)
    pieces = weights[UNITS * D : UNITS * D + 3 * vrows].astype(F32)
    vector = pieces[:vrows] + pieces[vrows : 2 * vrows] + pieces[2 * vrows :]
    own = jnp.where(first, lengths[0], lengths[1])
    info = jnp.concatenate([section[None].astype(jnp.int32), own, lengths[0]])
    after = [jnp.where(first, vector[1], vector[0]), jnp.where(first, vector[4], vector[3])]
    self_vec = columns([vector[0], vector[3]] + after)
    ffn_vec = columns([vector[7], vector[8], vector[9], vector[10], vector[6], vector[2], vector[5]])
    cross_vec = columns([vector[1], vector[4]])
    saved = call_self_forward(info, tokens[0], weights, self_vec, count, width)
    hidden, dy, late, late_vec = call_middle(
        info, jnp.concatenate([ffn_vec, cross_vec], axis=1), saved[10], cotangent[0], weights, count, width
    )
    dx, early, early_vec = call_self_backward(info, dy, weights, self_vec, saved[:10], count, width)
    ffn_grad, cross_grad = late_vec[0], late_vec[1]
    vector_grad = jnp.stack(
        [
            jnp.where(first, early_vec[:, 0], early_vec[:, 2]),
            jnp.where(first, early_vec[:, 2], cross_grad[:, 0]),
            ffn_grad[:, RU + 1],
            jnp.where(first, early_vec[:, 1], early_vec[:, 3]),
            jnp.where(first, early_vec[:, 3], cross_grad[:, 1]),
            ffn_grad[:, RU + 2],
            ffn_grad[:, RU],
        ]
        + [ffn_grad[:, i] for i in range(RU)]
    )
    grads = jnp.concatenate([early, late, pad_rows(three_pieces(vector_grad), SUB)], axis=0)
    total = sum_gradients(n_dp, grads)
    pieces = total[UNITS * D : UNITS * D + 3 * vrows].astype(F32)
    total_vector = pieces[:vrows] + pieces[vrows : 2 * vrows] + pieces[2 * vrows :]
    place = slot_units(owners[0], dp, master_sq.shape[2])
    squares_new = call_adam(place, total, master_sq[0, 0], mom1_sq[0, 0], mom2_sq[0, 0])
    vector_new = adam_update(vec_store, mom1_vec[0, 0], mom2_vec[0, 0], total_vector, vector_rate, 0.0)
    vector_new = [
        jnp.where(owns_vector, new, old)
        for new, old in zip(vector_new, (vec_store, mom1_vec[0, 0], mom2_vec[0, 0]))
    ]
    return (
        hidden[None],
        dx[None],
        *[value[None, None] for value in squares_new],
        *[value[None, None] for value in vector_new],
    )


def solution(mesh):
    n_dp = mesh.shape["dp"]
    slots = P("section", "dp", None, None, None)
    packs = P("section", "dp", None, None)
    rows = P("section", "dp", None)
    return jax.shard_map(
        functools.partial(local, n_dp),
        mesh=mesh,
        in_specs=(rows, rows, P(None, "dp"), P("section", None), slots, slots, slots, packs, packs, packs),
        out_specs=(rows, rows, slots, slots, slots, packs, packs, packs),
        check_vma=False,
    )
```

```python
import functools
import jax
import jax.numpy as jnp
import numpy as np
from jax import lax
from jax.experimental import pallas as pl
from jax.experimental.pallas import tpu as pltpu
from jax.sharding import PartitionSpec as P

D = 512
HEADS = 8
HS = D // HEADS
FF = 2048
RU = FF // D
STEP = 5
LANES = 128
F32 = jnp.float32
BF = jnp.bfloat16
NEG = -1e30


def nn(a, b):
    return jnp.dot(a, b, preferred_element_type=F32)


def nt(a, b):
    return lax.dot_general(a, b, (((1,), (1,)), ((), ())), preferred_element_type=F32)


def tn(a, b):
    return lax.dot_general(a, b, (((0,), (0,)), ((), ())), preferred_element_type=F32)


def lane_loop(count, body):
    def step(i, carry):
        body(pl.ds(pl.multiple_of(i * LANES, LANES), LANES))
        return carry

    lax.fori_loop(0, count // LANES, step, 0)


def norm_parts(value):
    mean = jnp.mean(value, axis=0, keepdims=True)
    centred = value - mean
    inv = lax.rsqrt(jnp.mean(centred * centred, axis=0, keepdims=True) + 1e-05)
    return centred * inv, inv


def norm_grad(grad, normed, inv, gain):
    scaled = grad * gain
    mean_one = jnp.mean(scaled, axis=0, keepdims=True)
    mean_two = jnp.mean(scaled * normed, axis=0, keepdims=True)
    return (scaled - mean_one - normed * mean_two) * inv


def fill_bias(bias, length, causal):
    rows = bias.shape[0]

    def body(lanes):
        key = lax.broadcasted_iota(jnp.int32, (rows, LANES), 0)
        query = lax.broadcasted_iota(jnp.int32, (rows, LANES), 1) + lanes.start
        allowed = key < length
        if causal is not None:
            allowed = allowed & ((key <= query) | jnp.logical_not(causal))
        bias[:, lanes] = jnp.where(allowed, 0.0, NEG)

    lane_loop(bias.shape[1], body)


def head_rows(h):
    return pl.ds(pl.multiple_of(h * HS, HS), HS)


def attend(qt, kt, vt, bias, ot, lse, pair, pause=None):
    def score(h, out):
        rows = head_rows(h)
        out[...] = tn(kt[rows, :], qt[rows, :] * BF(0.125))

    def finish(h, scores):
        rows = head_rows(h)
        biased = scores[...] + bias[...]
        top = jnp.max(biased, axis=0, keepdims=True)
        weights = jnp.exp(biased - top).astype(BF)
        values = jnp.concatenate([vt[rows, :], jnp.ones((16, vt.shape[1]), BF)], axis=0)
        out = nn(values, weights)
        total = out[HS : HS + 1]
        ot[rows, :] = (out[:HS] * (1.0 / total)).astype(BF)
        lse[pl.ds(h, 1), :] = top + jnp.log(total)

    one, two = pair.at[0], pair.at[1]
    score(0, one)

    def body(i, carry):
        score(2 * i + 1, two)
        finish(2 * i, one)
        score(jnp.minimum(2 * i + 2, HEADS - 1), one)
        finish(2 * i + 1, two)
        return carry

    if pause is None:
        lax.fori_loop(0, HEADS // 2, body, 0, unroll=True)
    else:
        lax.fori_loop(0, HEADS // 4, body, 0, unroll=True)
        pause()
        lax.fori_loop(HEADS // 4, HEADS // 2, body, 0, unroll=True)


def attend_back(qt, kt, vt, bias, ot, lse, dot, dqt, dkt, dvt, pause=None):
    def head(h, carry):
        rows = head_rows(h)
        keys, grads = kt[rows, :], dot[rows, :]
        queries = qt[rows, :] * BF(0.125)
        delta = jnp.sum(grads.astype(F32) * ot[rows, :].astype(F32), axis=0, keepdims=True)
        probs = jnp.exp(tn(keys, queries) + bias[...] - lse[pl.ds(h, 1), :])
        dscores = (probs * (tn(vt[rows, :], grads) - delta)).astype(BF)
        dvt[rows, :] = nt(grads, probs.astype(BF)).astype(BF)
        dkt[rows, :] = nt(queries, dscores).astype(BF)
        dqt[rows, :] = (nn(keys, dscores) * 0.125).astype(BF)
        return carry

    if pause is None:
        lax.fori_loop(0, HEADS, head, 0, unroll=4)
    else:
        def half(i, carry):
            lax.fori_loop(4 * i, 4 * i + 4, head, 0, unroll=True)
            pause()
            return carry

        lax.fori_loop(0, HEADS // 4, half, 0)


GAIN, SHIFT, B2, B1 = 0, 3, 6, 7


def column(vec, index):
    return vec[:, index : index + 1]


def self_column(vec, first, row):
    return jnp.where(first, column(vec, row + 1), column(vec, row))


def add_column(dvec, index, acc):
    dvec[:, index : index + 1] += jnp.sum(acc, axis=1, keepdims=True)


def self_forward(x, sq, vec, first, length, ut, n0, r0, qt, kt, vt, ot, lse, n1, r1, y, bias, et, pair, pause):
    tokens = x.shape[0]
    et[...] = x[...].astype(F32).T

    def entry(lanes):
        value = et[:, lanes]
        normed, inv = norm_parts(value)
        n0[:, lanes] = normed.astype(BF)
        r0[:, lanes] = inv
        value = jnp.where(first, normed * column(vec, GAIN) + column(vec, SHIFT), value)
        et[:, lanes] = value
        ut[:, lanes] = value.astype(BF)

    lane_loop(tokens, entry)
    fill_bias(bias, length, jnp.logical_not(first))
    for index, out in enumerate((qt, kt, vt)):
        out[...] = tn(sq[index][...], ut[...]).astype(BF)
    pause()
    attend(qt, kt, vt, bias, ot, lse, pair, pause)
    pause()
    et[...] += tn(sq[3][...], ot[...])
    gain, shift = self_column(vec, first, GAIN), self_column(vec, first, SHIFT)

    def leave(lanes):
        normed, inv = norm_parts(et[:, lanes])
        n1[:, lanes] = normed.astype(BF)
        r1[:, lanes] = inv
        y[:, lanes] = normed * gain + shift

    lane_loop(tokens, leave)


def self_backward(
    dy, sq, vec, first, length, ut, n0, r0, qt, kt, vt, ot, lse, n1, r1, dx,
    bias, dsa, dot, dqt, dkt, dvt, dsq, dvec, vacc, pause,
):
    tokens = dy.shape[1]
    vacc[...] = jnp.zeros(vacc.shape, F32)
    gain = self_column(vec, first, GAIN)

    def leave(lanes):
        grad, normed = dy[:, lanes], n1[:, lanes].astype(F32)
        vacc[2] += grad * normed
        vacc[3] += grad
        grad = norm_grad(grad, normed, r1[:, lanes], gain)
        dy[:, lanes] = grad
        dsa[:, lanes] = grad.astype(BF)

    lane_loop(tokens, leave)
    fill_bias(bias, length, jnp.logical_not(first))
    dot[...] = nn(sq[3][...], dsa[...]).astype(BF)
    dsq[3] += nt(ot[...], dsa[...])
    pause()
    attend_back(qt, kt, vt, bias, ot, lse, dot, dqt, dkt, dvt, pause)
    for index, grad in enumerate((dqt, dkt, dvt)):
        dsq[index] += nt(ut[...], grad[...])
        dy[...] += nn(sq[index][...], grad[...])
    pause()
    entry_gain = column(vec, GAIN)

    def entry(lanes):
        grad, normed = dy[:, lanes], n0[:, lanes].astype(F32)
        vacc[0] += grad * normed
        vacc[1] += grad
        dy[:, lanes] = jnp.where(first, norm_grad(grad, normed, r0[:, lanes], entry_gain), grad)

    lane_loop(tokens, entry)
    dx[...] = dy[...].T

    @pl.when(first)
    def _():
        add_column(dvec, GAIN, vacc[0])
        add_column(dvec, SHIFT, vacc[1])
        add_column(dvec, GAIN + 1, vacc[2])
        add_column(dvec, SHIFT + 1, vacc[3])

    @pl.when(jnp.logical_not(first))
    def _():
        add_column(dvec, GAIN, vacc[2])
        add_column(dvec, SHIFT, vacc[3])


def gelu_parts(z):
    root = 0.7978845608028654
    square = z * z
    t = jnp.tanh(z * (root + (root * 0.044715) * square))
    half = 0.5 + 0.5 * t
    act = z * half
    slope = half + act * (1.0 - t) * (root + (3.0 * root * 0.044715) * square)
    return act, slope


def feed_forward(h, units, vec, hb, act, slope, n2, r2, out):
    hb[...] = h[...].astype(BF)
    for c in range(RU):
        rows = slice(c * D, (c + 1) * D)
        a, s = gelu_parts(tn(units[c][...], hb[...]) + column(vec, B1 + c))
        act[rows, :] = a.astype(BF)
        slope[rows, :] = s.astype(BF)
    for c in range(RU):
        rows = slice(c * D, (c + 1) * D)
        h[...] += tn(units[RU + c][...], act[rows, :])

    def leave(lanes):
        normed, inv = norm_parts(h[:, lanes] + column(vec, B2))
        n2[:, lanes] = normed.astype(BF)
        r2[:, lanes] = inv
        out[:, lanes] = normed * column(vec, GAIN + 2) + column(vec, SHIFT + 2)

    lane_loop(h.shape[1], leave)


def feed_backward(dm, units, vec, hb, act, slope, n2, r2, dfb, dz, dunits, dvec, vacc):
    vacc[...] = jnp.zeros(vacc.shape, F32)

    def leave(lanes):
        grad, normed = dm[:, lanes], n2[:, lanes].astype(F32)
        vacc[RU + 1] += grad * normed
        vacc[RU + 2] += grad
        grad = norm_grad(grad, normed, r2[:, lanes], column(vec, GAIN + 2))
        dm[:, lanes] = grad
        short = grad.astype(BF)
        vacc[RU] += short.astype(F32)
        dfb[:, lanes] = short

    lane_loop(dm.shape[1], leave)
    for c in range(RU):
        rows = slice(c * D, (c + 1) * D)
        dz[rows, :] = (nn(units[RU + c][...], dfb[...]) * slope[rows, :].astype(F32)).astype(BF)
        dunits[RU + c][...] += nt(act[rows, :], dfb[...])
    for c in range(RU):
        rows = slice(c * D, (c + 1) * D)
        dm[...] += nn(units[c][...], dz[rows, :])
        dunits[c][...] += nt(hb[...], dz[rows, :])
        for lanes in range(0, dm.shape[1], LANES):
            vacc[c] += dz[rows, lanes : lanes + LANES].astype(F32)
    for index in range(RU):
        add_column(dvec, B1 + index, vacc[index])
    add_column(dvec, B2, vacc[RU])
    add_column(dvec, GAIN + 2, vacc[RU + 1])
    add_column(dvec, SHIFT + 2, vacc[RU + 2])


def cross_forward(a, sq, vec, length, ab, cqt, kt, vt, ot, lse, n1, r1, bias, pair):
    ab[...] = a[...].astype(BF)
    cqt[...] = tn(sq[0][...], ab[...]).astype(BF)
    fill_bias(bias, length, None)
    attend(cqt, kt, vt, bias, ot, lse, pair)
    a[...] += tn(sq[1][...], ot[...])

    def leave(lanes):
        normed, inv = norm_parts(a[:, lanes])
        n1[:, lanes] = normed.astype(BF)
        r1[:, lanes] = inv
        a[:, lanes] = normed * column(vec, GAIN + 1) + column(vec, SHIFT + 1)

    lane_loop(a.shape[1], leave)


def cross_backward(
    dbq, sq, vec, ab, cqt, kt, vt, ot, lse, n1, r1, bias, dca, dot, dqt, dkt, dvt, dsq, dvec, vacc
):
    vacc[0] = jnp.zeros(vacc.shape[1:], F32)
    vacc[1] = jnp.zeros(vacc.shape[1:], F32)

    def leave(lanes):
        grad, normed = dbq[:, lanes], n1[:, lanes].astype(F32)
        vacc[0] += grad * normed
        vacc[1] += grad
        grad = norm_grad(grad, normed, r1[:, lanes], column(vec, GAIN + 1))
        dbq[:, lanes] = grad
        dca[:, lanes] = grad.astype(BF)

    lane_loop(dbq.shape[1], leave)
    dot[...] = nn(sq[1][...], dca[...]).astype(BF)
    dsq[1][...] += nt(ot[...], dca[...])
    attend_back(cqt, kt, vt, bias, ot, lse, dot, dqt, dkt, dvt)
    dsq[0][...] += nt(ab[...], dqt[...])
    dbq[...] += nn(sq[0][...], dqt[...])
    add_column(dvec, GAIN + 1, vacc[0])
    add_column(dvec, SHIFT + 1, vacc[1])


SUB = 256
HOP = 3
HALF = SUB // 2
QUART = SUB // 4
UNITS = 6 + 2 * RU
VEC_ROWS = 256
SUBS = (UNITS * D + VEC_ROWS) // SUB
MESH = pl.DeviceIdType.MESH


class Total:
    def __init__(self, n_dp, order, shorts, other, mine, out, core_in, half, x_in, right_in, left_in, passed, sems):
        self.length = n_dp // 4
        self.last = self.length - 1
        self.section = lax.axis_index("section")
        self.dp = lax.axis_index("dp")
        self.core, self.x, self.z = self.dp % 2, (self.dp // 2) % 2, self.dp // 4
        self.sibling, self.beside = self.dp + 1 - 2 * self.core, self.dp + 2 - 4 * self.x
        self.has_left, self.has_right = self.z > 0, self.z < self.last
        self.order, self.shorts, self.other, self.mine = order, shorts, other, mine
        self.out, self.core_in, self.half, self.x_in = out, core_in, half, x_in
        self.right_in, self.left_in, self.passed, self.sems = right_in, left_in, passed, sems
        far = self.last
        self.ticks = SUBS + HOP * (2 + far + far) + 1

    def greet(self):
        barrier = pltpu.get_barrier_semaphore()

        def signal(index):
            pl.semaphore_signal(barrier, inc=1, device_id=(self.section, index), device_id_type=MESH)

        signal(self.sibling)
        signal(self.beside)
        pl.when(self.has_left)(lambda: signal(self.dp - 4))
        pl.when(self.has_right)(lambda: signal(self.dp + 4))
        pl.semaphore_wait(barrier, 2 + self.has_left.astype(jnp.int32) + self.has_right.astype(jnp.int32))

    def short_route(self, t):
        return ((t & 1) == 0) | ((t >= self.shorts[0]) & (t < self.shorts[1]))

    def home(self, t):
        return (t >> 1) & self.last

    def place(self, t, start, size):
        return pl.ds(pl.multiple_of(self.order(t) * SUB + start, QUART), size)

    def send(self, step, t, source, target, index):
        return pltpu.make_async_remote_copy(
            src_ref=source,
            dst_ref=target,
            send_sem=self.sems.at[0, step, t],
            recv_sem=self.sems.at[1, step, t],
            device_id=(self.section, index),
            device_id_type=MESH,
        )

    def part(self, size, index):
        return pl.ds(pl.multiple_of(index * size, size), size)

    def copy_core(self, t):
        source = self.other(t, self.order(t), HALF * (1 - self.core))
        return self.send(0, t, source, self.core_in.at[t], self.sibling)

    def copy_x(self, t):
        rows = self.part(QUART, 1 - self.x)
        return self.send(1, t, self.half.at[t, rows], self.x_in.at[t, pl.ds(0, QUART)], self.beside)

    def copy_x_whole(self, t):
        return self.send(1, t, self.passed.at[t], self.x_in.at[t], self.beside)

    def copy_right(self, t, source):
        return self.send(2, t, source, self.right_in.at[t, pl.ds(0, QUART)], self.dp + 4)

    def copy_left(self, t, source):
        return self.send(3, t, source, self.left_in.at[t, pl.ds(0, QUART)], self.dp - 4)

    def copy_right_whole(self, t, source):
        return self.send(2, t, source, self.right_in.at[t], self.dp + 4)

    def copy_left_whole(self, t, source):
        return self.send(3, t, source, self.left_in.at[t], self.dp - 4)

    def copy_back_x(self, t):
        place = self.place(t, HALF * self.core + QUART * self.x, QUART)
        return self.send(4, t, self.out.at[place], self.out.at[place], self.beside)

    def copy_back_core(self, t):
        place = self.place(t, HALF * self.core, HALF)
        return self.send(5, t, self.out.at[place], self.out.at[place], self.sibling)

    def copy_back_right(self, t):
        place = self.place(t, HALF * self.core, HALF)
        return self.send(4, t, self.out.at[place], self.out.at[place], self.dp + 4)

    def copy_back_left(self, t):
        place = self.place(t, HALF * self.core, HALF)
        return self.send(6, t, self.out.at[place], self.out.at[place], self.dp - 4)

    def add(self, one, two):
        return one + two

    def own_quarter(self, t):
        return self.half.at[t, self.part(QUART, self.x)]

    def short_core(self, t):
        self.copy_core(t).wait_recv()
        self.half[t] = self.add(self.mine(t, self.order(t), HALF * self.core), self.core_in[t])
        self.copy_x(t).start()

    def short_x(self, t):
        self.copy_x(t).wait_recv()
        quart = self.own_quarter(t)
        quart[...] = self.add(quart[...], self.x_in[t, 0:QUART])

        @pl.when(jnp.logical_not(self.has_left) & self.has_right)
        def _():
            self.copy_right(t, quart).start()

        @pl.when(jnp.logical_not(self.has_right) & self.has_left)
        def _():
            self.copy_left(t, quart).start()

    def short_right(self, t):
        @pl.when(self.has_left)
        def _():
            target = self.passed.at[t, pl.ds(0, QUART)]
            self.copy_right(t, target).wait_recv()

            @pl.when(self.has_right)
            def _():
                target[...] = self.add(self.own_quarter(t)[...], self.right_in[t, 0:QUART])
                self.copy_right(t, target).start()

    def short_left(self, t):
        @pl.when(self.has_right)
        def _():
            target = self.passed.at[t, pl.ds(QUART, QUART)]
            self.copy_left(t, target).wait_recv()

            @pl.when(self.has_left)
            def _():
                target[...] = self.add(self.own_quarter(t)[...], self.left_in[t, 0:QUART])
                self.copy_left(t, target).start()

    def short_total(self, t):
        total = self.own_quarter(t)[...].astype(F32)
        total += jnp.where(self.has_left, self.right_in[t, 0:QUART].astype(F32), 0.0)
        total += jnp.where(self.has_right, self.left_in[t, 0:QUART].astype(F32), 0.0)
        self.out[self.place(t, HALF * self.core + QUART * self.x, QUART), :] = total.astype(BF)
        self.copy_back_x(t).start()

    def short_back(self, t):
        self.copy_back_x(t).wait_recv()
        self.copy_back_core(t).start()

    def long_core(self, t):
        self.copy_core(t).wait_recv()
        self.half[t] = self.add(self.mine(t, self.order(t), HALF * self.core), self.core_in[t])
        home = self.home(t)

        @pl.when(jnp.logical_not(self.has_left) & (home > 0))
        def _():
            self.copy_right_whole(t, self.half.at[t]).start()

        @pl.when(jnp.logical_not(self.has_right) & (home < self.last))
        def _():
            self.copy_left_whole(t, self.half.at[t]).start()

    def long_right(self, t):
        @pl.when(self.has_left & (self.z < self.home(t)))
        def _():
            self.copy_right_whole(t, self.passed.at[t]).wait_recv()
            self.passed[t] = self.add(self.half[t], self.right_in[t])
            self.copy_right_whole(t, self.passed.at[t]).start()

    def long_left(self, t):
        @pl.when(self.has_right & (self.z > self.home(t)))
        def _():
            self.copy_left_whole(t, self.passed.at[t]).wait_recv()
            self.passed[t] = self.add(self.half[t], self.left_in[t])
            self.copy_left_whole(t, self.passed.at[t]).start()

    def long_home(self, t):
        @pl.when(self.z == self.home(t))
        def _():
            pl.when(self.has_left)(lambda: self.copy_right_whole(t, self.half.at[t]).wait_recv())
            pl.when(self.has_right)(lambda: self.copy_left_whole(t, self.half.at[t]).wait_recv())
            total = self.half[t].astype(F32)
            total += jnp.where(self.has_left, self.right_in[t].astype(F32), 0.0)
            total += jnp.where(self.has_right, self.left_in[t].astype(F32), 0.0)
            self.passed[t] = total.astype(BF)
            self.copy_x_whole(t).start()

    def long_x(self, t):
        @pl.when(self.z == self.home(t))
        def _():
            self.copy_x_whole(t).wait_recv()
            self.out[self.place(t, HALF * self.core, HALF), :] = self.add(self.passed[t], self.x_in[t])
            pl.when(self.has_left)(lambda: self.copy_back_left(t).start())
            pl.when(self.has_right)(lambda: self.copy_back_right(t).start())
            self.copy_back_core(t).start()

    def long_back(self, t):
        home = self.home(t)

        @pl.when(self.z > home)
        def _():
            self.copy_back_right(t).wait_recv()
            pl.when(self.has_right)(lambda: self.copy_back_right(t).start())

        @pl.when(self.z < home)
        def _():
            self.copy_back_left(t).wait_recv()
            pl.when(self.has_left)(lambda: self.copy_back_left(t).start())

        pl.when(self.z != home)(lambda: self.copy_back_core(t).start())

    def tick(self, now, prepare):
        z, last = self.z, self.last
        far = jnp.maximum(z, last - z)
        prepared = now

        @pl.when(prepared < SUBS)
        def _():
            prepare(prepared)
            self.copy_core(prepared).start()

        def due(step, lag, short):
            t = now - HOP * lag
            fits = (t >= 0) & (t < SUBS)
            kind = self.short_route(t) if short else jnp.logical_not(self.short_route(t))
            pl.when(fits & kind)(lambda: step(t))

        due(self.short_core, 1, True)
        due(self.short_x, 2, True)
        due(self.short_right, 2 + z, True)
        due(self.short_left, 2 + last - z, True)
        due(self.short_total, 2 + far, True)
        due(self.short_back, 3 + far, True)
        due(self.long_core, 1, False)
        due(self.long_right, 1 + z, False)
        due(self.long_left, 1 + last - z, False)
        due(self.long_home, 1 + far, False)
        due(self.long_x, 2 + far, False)
        for home in range(self.length):
            lag = 2 + max(home, last - home) + jnp.abs(z - home)
            t = now - HOP * lag
            fits = (t >= 0) & (t < SUBS) & jnp.logical_not(self.short_route(t)) & (self.home(t) == home)
            pl.when(fits & (z != home))(lambda t=t: self.long_back(t))

    def arrive(self, t):
        self.copy_back_core(t).wait_recv()

    def settle(self, t):
        self.copy_core(t).wait_send()
        self.copy_back_core(t).wait_send()
        home = self.home(t)

        @pl.when(self.short_route(t))
        def _():
            self.copy_x(t).wait_send()
            pl.when(self.has_right)(lambda: self.copy_right(t, self.own_quarter(t)).wait_send())
            pl.when(self.has_left)(lambda: self.copy_left(t, self.own_quarter(t)).wait_send())
            self.copy_back_x(t).wait_send()

        @pl.when(jnp.logical_not(self.short_route(t)))
        def _():
            pl.when(self.z < home)(lambda: self.copy_right_whole(t, self.half.at[t]).wait_send())
            pl.when(self.z > home)(lambda: self.copy_left_whole(t, self.half.at[t]).wait_send())
            pl.when(self.z == home)(lambda: self.copy_x_whole(t).wait_send())
            pl.when(self.has_right & (self.z >= home))(lambda: self.copy_back_right(t).wait_send())
            pl.when(self.has_left & (self.z <= home))(lambda: self.copy_back_left(t).wait_send())


def loop(start, stop, body):
    def step(i, carry):
        body(i)
        return carry

    lax.fori_loop(start, stop, step, 0)


def total_scratch():
    return [pltpu.VMEM((SUBS, HALF, D), BF)] * 6 + [pltpu.SemaphoreType.DMA((2, 7, SUBS))]


def any_space():
    return pl.BlockSpec(memory_space=pl.ANY)


def vmem_space():
    return pl.BlockSpec(memory_space=pltpu.VMEM)


def smem_space():
    return pl.BlockSpec(memory_space=pltpu.SMEM)


def block_spec(*dims):
    return pl.BlockSpec((1,) + dims, lambda b, info: (b,) + (0,) * len(dims))


def shape32(*dims):
    return jax.ShapeDtypeStruct(dims, F32)


def shape16(*dims):
    return jax.ShapeDtypeStruct(dims, BF)


TENSOR_OF = (0, 1, 2, 3, 4, 5) + (6,) * RU + (7,) * RU
TENSOR_SIZE = (1,) * 6 + (RU, RU)
FIRST_UNIT = (0, 1, 2, 3, 4, 5, 6, 6 + RU)
VEC_BLOCKS = VEC_ROWS // SUB
EARLY = 4 * D // SUB + VEC_BLOCKS
PIECE = 16


def copies(sources, targets, sems):
    return [pltpu.make_async_copy(s, t, sems.at[i]) for i, (s, t) in enumerate(zip(sources, targets))]


def slot_of(owners, tensor):
    prior = jnp.int32(0)
    for earlier in range(tensor):
        prior += jnp.where(owners[0, earlier] == owners[0, tensor], TENSOR_SIZE[earlier], 0)
    return prior


def start_kernel(n_dp, info, owners, x, slots, pack, out, vec, *refs):
    saved_out, (y_out, stage, *comm), refs = refs[:10], refs[10:19], refs[19:]
    saved, (y, xb, bias, et, pair, places, counter, sems) = refs[:10], refs[10:]
    count, tokens = saved_out[0].shape[0], saved_out[0].shape[2]
    first = lax.axis_index("section") == 0
    dp = lax.axis_index("dp")
    for unit in range(UNITS):
        tensor = TENSOR_OF[unit]
        slot = jnp.minimum(slot_of(owners, tensor) + (unit - FIRST_UNIT[tensor]), slots.shape[0] - 1)
        places[0, unit] = slot
        places[1, unit] = (owners[0, tensor] == dp).astype(jnp.int32)

    def own(block, start):
        is_pack = block >= SUBS - VEC_BLOCKS
        unit = jnp.minimum(block * SUB // D, UNITS - 1)
        at = pl.multiple_of((block * SUB) % D + start, HALF)
        value = jnp.where(places[1, unit] == 1, slots[places[0, unit], pl.ds(at, HALF), :], 0.0).astype(BF)
        return jnp.where(is_pack, pack[pl.ds(pl.multiple_of(start, HALF), HALF), :], value)

    def order(t):
        return jnp.where(t < VEC_BLOCKS, t + SUBS - VEC_BLOCKS, t - VEC_BLOCKS)

    total = Total(
        n_dp,
        order,
        (0, EARLY),
        lambda t, block, start: stage.at[t],
        lambda t, block, start: own(block, start),
        out,
        *comm,
    )

    def prepare(t):
        stage[t] = own(order(t), HALF * (1 - total.core))

    def run(ticks):
        begin = counter[0]
        stop = jnp.minimum(begin + ticks, total.ticks)
        loop(begin, stop, lambda now: total.tick(now, prepare))
        counter[0] = stop

    total.greet()
    counter[0] = 0
    run(EARLY + HOP * (3 + total.last))
    loop(0, EARLY, total.arrive)
    rows = [out[pl.ds(UNITS * D + i * PIECE, PIECE), :].astype(F32) for i in range(3)]
    whole = jnp.concatenate([rows[0] + rows[1] + rows[2], jnp.zeros((LANES - PIECE, D), F32)], axis=0)
    vec[...] = whole.T
    squares = [out.at[pl.ds(i * D, D)] for i in range(4)]

    def outward(b):
        return copies(saved + (y,), [ref.at[b] for ref in saved_out + (y_out,)], sems)

    def block(b):
        load = pltpu.make_async_copy(x.at[pl.ds(pl.multiple_of(b * tokens, tokens), tokens)], xb, sems.at[11])
        load.start()

        @pl.when(b > 0)
        def _():
            for copy in outward(b - 1):
                copy.wait()

        load.wait()
        self_forward(
            xb, squares, vec, first, info[1 + b], *saved, y, bias, et, pair, lambda: run(2)
        )
        for copy in outward(b):
            copy.start()
        run(1)

    loop(0, count, block)
    run(total.ticks)
    for copy in outward(count - 1):
        copy.wait()
    loop(EARLY, SUBS, total.arrive)
    loop(0, SUBS, total.settle)


def saved_dims(tokens):
    wide, row = ((D, tokens), BF), ((1, tokens), F32)
    return [wide, wide, row, wide, wide, wide, wide, ((HEADS, tokens), F32), wide, row]


def call_start(n_dp, info, owners, x, slots, pack, count):
    tokens = x.shape[0] // count
    kept = saved_dims(tokens)
    scores = pltpu.VMEM((tokens, tokens), F32)
    return pl.pallas_call(
        functools.partial(start_kernel, n_dp),
        name="start",
        out_shape=[shape16(SUBS * SUB, D), shape32(D, LANES)]
        + [jax.ShapeDtypeStruct((count,) + dims, kind) for dims, kind in kept]
        + [shape32(count, D, tokens)],
        in_specs=[smem_space(), smem_space(), any_space(), vmem_space(), vmem_space()],
        out_specs=[vmem_space(), vmem_space()] + [any_space()] * 11,
        scratch_shapes=[pltpu.VMEM((SUBS, HALF, D), BF)]
        + total_scratch()
        + [pltpu.VMEM(dims, kind) for dims, kind in kept]
        + [
            pltpu.VMEM((D, tokens), F32),
            pltpu.VMEM((tokens, D), BF),
            scores,
            pltpu.VMEM((D, tokens), F32),
            pltpu.VMEM((2, tokens, tokens), F32),
            pltpu.SMEM((2, UNITS), jnp.int32),
            pltpu.SMEM((1,), jnp.int32),
            pltpu.SemaphoreType.DMA((12,)),
        ],
        compiler_params=pltpu.CompilerParams(
            collective_id=0, has_side_effects=True, vmem_limit_bytes=60 * 2**20
        ),
    )(info, owners, x, slots, pack)


def finish_kernel(n_dp, info, dy, sq, vec, late, late_vec, *refs):
    saved_in, (dx_out, out), (stage, *comm), refs = refs[:10], refs[10:12], refs[12:20], refs[20:]
    saved, (dys, dx, bias, dsa, dot, dqt, dkt, dvt, dsq, dvec, vacc, pack, counter, sems) = refs[:10], refs[10:]
    count, tokens = dy.shape[0], dy.shape[2]
    first = lax.axis_index("section") == 0
    early = EARLY - VEC_BLOCKS
    others = SUBS - EARLY

    def order(t):
        return jnp.where(t < others, t + early, jnp.where(t < SUBS - VEC_BLOCKS, t - others, t))

    def late_rows(block, start):
        return pl.ds(pl.multiple_of((block - early) * SUB + start, HALF), HALF)

    def own_early(block, start):
        unit = jnp.minimum(block * SUB // D, 3)
        at = pl.multiple_of((block * SUB) % D + start, HALF)
        value = dsq[unit, pl.ds(at, HALF), :].astype(BF)
        return jnp.where(block >= SUBS - VEC_BLOCKS, pack[pl.ds(pl.multiple_of(start, HALF), HALF), :], value)

    def mine(t, block, start):
        at = jnp.clip((block - early) * SUB, 0, (others - 1) * SUB) + start
        return jnp.where(t < others, late[pl.ds(pl.multiple_of(at, HALF), HALF), :], own_early(block, start))

    total = Total(
        n_dp, order, (others, SUBS), lambda t, block, start: stage.at[t], mine, out, *comm
    )

    def prepare(t):
        stage[t] = mine(t, order(t), HALF * (1 - total.core))

    def run(ticks, end):
        begin = counter[0]
        stop = jnp.minimum(begin + ticks, end)
        loop(begin, stop, lambda now: total.tick(now, prepare))
        counter[0] = stop

    total.greet()
    counter[0] = 0
    dsq[...] = jnp.zeros(dsq.shape, F32)
    dvec[...] = late_vec[...]
    squares = [sq.at[pl.ds(i * D, D)] for i in range(4)]

    def block(b):
        loads = copies([ref.at[b] for ref in saved_in] + [dy.at[b]], saved + (dys,), sems)
        for copy in loads:
            copy.start()
        run(1, others)
        store = pltpu.make_async_copy(
            dx, dx_out.at[pl.ds(pl.multiple_of(b * tokens, tokens), tokens)], sems.at[11]
        )
        pl.when(b > 0)(lambda: store.wait())
        for copy in loads:
            copy.wait()
        self_backward(
            dys, squares, vec, first, info[1 + b], *saved, dx,
            bias, dsa, dot, dqt, dkt, dvt, dsq, dvec, vacc, lambda: run(1, others),
        )
        store.start()

    loop(0, count, block)
    value = dvec[...].T[:PIECE]
    high = value.astype(BF)
    rest = value - high.astype(F32)
    mid = rest.astype(BF)
    pack[...] = jnp.zeros(pack.shape, BF)
    pack[0:PIECE, :] = high
    pack[PIECE : 2 * PIECE, :] = mid
    pack[2 * PIECE : 3 * PIECE, :] = (rest - mid.astype(F32)).astype(BF)
    run(total.ticks, total.ticks)
    pltpu.make_async_copy(dx, dx_out.at[pl.ds(0, tokens)], sems.at[11]).wait()
    loop(0, SUBS, total.arrive)
    loop(0, SUBS, total.settle)


def call_finish(n_dp, info, dy, weights, vec, late, late_vec, saved):
    count, tokens = dy.shape[0], dy.shape[2]
    kept = saved_dims(tokens)
    wide16 = pltpu.VMEM((D, tokens), BF)
    wide32 = pltpu.VMEM((D, tokens), F32)
    return pl.pallas_call(
        functools.partial(finish_kernel, n_dp),
        name="finish",
        out_shape=[shape32(count * tokens, D), shape16(SUBS * SUB, D)],
        grid=(1,),
        in_specs=[
            smem_space(),
            any_space(),
            pl.BlockSpec((4 * D, D), lambda i: (0, 0)),
            vmem_space(),
            vmem_space(),
            vmem_space(),
        ]
        + [any_space()] * 10,
        out_specs=[any_space(), vmem_space()],
        scratch_shapes=[pltpu.VMEM((SUBS, HALF, D), BF)]
        + total_scratch()
        + [pltpu.VMEM(dims, kind) for dims, kind in kept]
        + [wide32, pltpu.VMEM((tokens, D), F32), pltpu.VMEM((tokens, tokens), F32)]
        + [wide16] * 5
        + [
            pltpu.VMEM((4, D, D), F32),
            pltpu.VMEM((D, LANES), F32),
            pltpu.VMEM((4, D, LANES), F32),
            pltpu.VMEM((VEC_ROWS, D), BF),
            pltpu.SMEM((1,), jnp.int32),
            pltpu.SemaphoreType.DMA((12,)),
        ],
        compiler_params=pltpu.CompilerParams(
            collective_id=2, has_side_effects=True, vmem_limit_bytes=60 * 2**20
        ),
    )(info, dy, weights, vec, late, late_vec, *saved)


def middle_kernel(
    info, vec, y, cot, weights, hidden, dy, grads, dvec,
    wts, acc, sent, got, h, mem, hb, act, slope, n2, r2, dfb, dz, vacc,
    ab, cqt, kt, vt, ot, lse, n1, r1, bias, dca, dot, dqt, pair, tok, stage, sems, load_sem,
):
    section = lax.axis_index("section")
    dp = lax.axis_index("dp")
    count, tokens = y.shape[0], y.shape[2]
    other = 1 - section
    barrier = pltpu.get_barrier_semaphore()
    pl.semaphore_signal(barrier, inc=1, device_id=(other, dp), device_id_type=MESH)
    pl.semaphore_wait(barrier, 1)

    def move(source, target):
        copy = pltpu.make_async_copy(source, target, load_sem)
        copy.start()
        copy.wait()

    def swap(b):
        return pltpu.make_async_remote_copy(
            src_ref=sent.at[b],
            dst_ref=got.at[b],
            send_sem=sems.at[0, b],
            recv_sem=sems.at[1, b],
            device_id=(other, dp),
            device_id_type=MESH,
        )

    def each(body):
        def step(b, carry):
            body(b)
            return carry

        lax.fori_loop(0, count, step, 0)

    move(weights.at[pl.ds(4 * D, 10 * D)], wts)
    unit = [wts.at[pl.ds(i * D, D)] for i in range(10)]
    s4, s5, ffn = unit[0], unit[1], unit[2:]
    acc[...] = jnp.zeros(acc.shape, F32)
    dvec[...] = jnp.zeros(dvec.shape, F32)
    cross_acc = [acc.at[i] for i in range(2)]
    ffn_acc = [acc.at[2 + i] for i in range(8)]

    def run_feed_forward():
        feed_forward(h, ffn, vec, hb, act, slope, n2, r2, mem)

    def emit_hidden(b):
        tok[...] = mem[...].T.astype(BF)
        move(tok, hidden.at[pl.ds(pl.multiple_of(b * tokens, tokens), tokens)])

    def load_cotangent(b):
        move(cot.at[pl.ds(pl.multiple_of(b * tokens, tokens), tokens)], tok)
        token = lax.broadcasted_iota(jnp.int32, (D, tokens), 1)
        h[...] = jnp.where(token < info[1 + b], tok[...].astype(F32).T, 0.0)

    def run_feed_backward():
        feed_backward(h, ffn, vec, hb, act, slope, n2, r2, dfb, dz, ffn_acc, dvec, vacc)

    @pl.when(section == 0)
    def _():
        def ahead(b):
            move(y.at[b], h)
            run_feed_forward()
            emit_hidden(b)
            short = mem[...].astype(BF)
            sent[b, 0] = tn(s4[...], short).astype(BF)
            sent[b, 1] = tn(s5[...], short).astype(BF)
            swap(b).start()

        each(ahead)

        def back(b):
            move(y.at[b], h)
            run_feed_forward()
            ab[...] = mem[...].astype(BF)
            load_cotangent(b)
            swap(b).wait_recv()
            for i, matrix in enumerate((s4, s5)):
                h[...] += nn(matrix[...], got[b, i])
                acc[i] += nt(ab[...], got[b, i])
            run_feed_backward()
            move(h, dy.at[b])

        each(back)

    @pl.when(section == 1)
    def _():
        def both(b):
            move(y.at[b], h)
            swap(b).wait_recv()
            kt[...] = got[b, 0]
            vt[...] = got[b, 1]
            cross_forward(h, (s4, s5), vec, info[1 + count + b], ab, cqt, kt, vt, ot, lse, n1, r1, bias, pair)
            run_feed_forward()
            emit_hidden(b)
            load_cotangent(b)
            run_feed_backward()
            cross_backward(
                h, (s4, s5), vec, ab, cqt, kt, vt, ot, lse, n1, r1, bias, dca, dot, dqt,
                sent.at[b, 0], sent.at[b, 1], cross_acc, dvec, vacc,
            )
            swap(b).start()
            move(h, dy.at[b])

        each(both)

    def finish(b):
        swap(b).wait_send()

    each(finish)
    for i in range(10):
        stage[...] = acc[i].astype(BF)
        move(stage, grads.at[pl.ds(i * D, D)])


def call_middle(info, vec, y, cot, weights, count, tokens):
    wide16 = pltpu.VMEM((D, tokens), BF)
    wide32 = pltpu.VMEM((D, tokens), F32)
    row = pltpu.VMEM((1, tokens), F32)
    return pl.pallas_call(
        middle_kernel,
        name="middle",
        out_shape=[
            shape16(count * tokens, D),
            shape32(count, D, tokens),
            shape16(10 * D, D),
            shape32(D, LANES),
        ],
        in_specs=[smem_space(), vmem_space(), any_space(), any_space(), any_space()],
        out_specs=[any_space(), any_space(), any_space(), vmem_space()],
        scratch_shapes=[
            pltpu.VMEM((10 * D, D), BF),
            pltpu.VMEM((10, D, D), F32),
            pltpu.VMEM((count, 2, D, tokens), BF),
            pltpu.VMEM((count, 2, D, tokens), BF),
            wide32, wide32, wide16,
            pltpu.VMEM((FF, tokens), BF), pltpu.VMEM((FF, tokens), BF),
            wide16, row, wide16,
            pltpu.VMEM((FF, tokens), BF),
            pltpu.VMEM((RU + 3, D, LANES), F32),
                wide16, wide16, wide16, wide16, wide16,
            pltpu.VMEM((HEADS, tokens), F32),
            wide16, row,
            pltpu.VMEM((tokens, tokens), F32),
            wide16, wide16, wide16,
            pltpu.VMEM((2, tokens, tokens), F32),
            pltpu.VMEM((tokens, D), BF),
            pltpu.VMEM((D, D), BF),
            pltpu.SemaphoreType.DMA((2, count)),
            pltpu.SemaphoreType.DMA,
        ],
        compiler_params=pltpu.CompilerParams(
            collective_id=1, has_side_effects=True, vmem_limit_bytes=60 * 2**20
        ),
    )(info, vec, y, cot, weights)


matrix_rate = 0.04
vector_rate = 0.25
matrix_decay = 0.01


def adam_update(weight, moment_old, square_old, gradient, learn_rate, decay_rate):
    moment_one = 0.5 * moment_old + 0.5 * gradient
    moment_two = 0.5 * square_old + 0.5 * gradient * gradient
    correction = 1.0 - 0.5**STEP
    adam_step = moment_one / correction / (jnp.sqrt(moment_two / correction) + 1e-08)
    return (weight - learn_rate * (adam_step + decay_rate * weight), moment_one, moment_two)


def adam_kernel(place, grad, weight, first, second, weight_out, first_out, second_out):
    taken = place[pl.program_id(0)] >= 0
    fresh = adam_update(weight[0], first[0], second[0], grad[...].astype(F32), matrix_rate, matrix_decay)
    for new, old, out in zip(fresh, (weight, first, second), (weight_out, first_out, second_out)):
        out[0] = jnp.where(taken, new, old[0])


def call_adam(place, grads, weight, first, second):
    slots = weight.shape[0]
    spec = block_spec(D, D)
    out = shape32(slots, D, D)
    return pl.pallas_call(
        adam_kernel,
        name="adam",
        out_shape=[out] * 3,
        grid_spec=pltpu.PrefetchScalarGridSpec(
            num_scalar_prefetch=1,
            grid=(slots,),
            in_specs=[pl.BlockSpec((D, D), lambda s, place: (jnp.maximum(place[s], 0), 0))] + [spec] * 3,
            out_specs=[spec] * 3,
        ),
    )(place, grads, weight, first, second)


def unit_tables(owner_row):
    tensor_of = np.array(TENSOR_OF)
    first_unit = np.array(FIRST_UNIT)
    owned_by = owner_row[:8]
    earlier = (owned_by[:, None] == owned_by[None, :]) & jnp.asarray(
        np.arange(8)[None, :] < np.arange(8)[:, None]
    )
    prior = jnp.sum(jnp.where(earlier, jnp.array(TENSOR_SIZE, jnp.int32)[None, :], 0), axis=1)
    unit_owner = owned_by[tensor_of]
    unit_slot = prior[tensor_of] + jnp.asarray(np.arange(UNITS) - first_unit[tensor_of], jnp.int32)
    return unit_owner, unit_slot.astype(jnp.int32)


def slot_units(owner_row, dp, slots):
    unit_owner, unit_slot = unit_tables(owner_row)
    hit = (unit_owner[None, :] == dp) & (unit_slot[None, :] == jnp.arange(slots, dtype=jnp.int32)[:, None])
    return jnp.sum(jnp.where(hit, jnp.arange(UNITS, dtype=jnp.int32)[None, :] + 1, 0), axis=1) - 1


def three_pieces(value):
    high = value.astype(BF)
    rest = value - high.astype(F32)
    mid = rest.astype(BF)
    low = (rest - mid.astype(F32)).astype(BF)
    pad = ((0, PIECE - value.shape[0]), (0, 0))
    parts = jnp.concatenate([jnp.pad(part, pad) for part in (high, mid, low)], axis=0)
    return jnp.pad(parts, ((0, VEC_ROWS - 3 * PIECE), (0, 0)))


def local(n_dp, tokens, cotangent, lengths, owners, master_sq, mom1_sq, mom2_sq, master_vec, mom1_vec, mom2_vec):
    section = lax.axis_index("section")
    dp = lax.axis_index("dp")
    count = lengths.shape[1]
    vec_store = master_vec[0, 0]
    vrows = vec_store.shape[0]
    owns_vector = owners[0, 8] == dp
    pack = three_pieces(jnp.where(owns_vector, vec_store, 0.0))
    own = jnp.where(section == 0, lengths[0], lengths[1])
    info = jnp.concatenate([section[None].astype(jnp.int32), own, lengths[0]])
    weights, vec, *saved = call_start(n_dp, info, owners, tokens[0], master_sq[0, 0], pack, count)
    width = tokens.shape[1] // count
    hidden, dy, late, late_vec = call_middle(info, vec, saved[10], cotangent[0], weights, count, width)
    dx, total = call_finish(n_dp, info, dy, weights, vec, late, late_vec, saved[:10])
    pieces = total[UNITS * D : UNITS * D + 3 * PIECE].astype(F32).reshape(3, PIECE, D)[:, :vrows]
    total_vector = pieces[0] + pieces[1] + pieces[2]
    place = slot_units(owners[0], dp, master_sq.shape[2])
    squares_new = call_adam(place, total, master_sq[0, 0], mom1_sq[0, 0], mom2_sq[0, 0])
    vector_new = adam_update(vec_store, mom1_vec[0, 0], mom2_vec[0, 0], total_vector, vector_rate, 0.0)
    vector_new = [
        jnp.where(owns_vector, new, old)
        for new, old in zip(vector_new, (vec_store, mom1_vec[0, 0], mom2_vec[0, 0]))
    ]
    return (
        hidden[None],
        dx[None],
        *[value[None, None] for value in squares_new],
        *[value[None, None] for value in vector_new],
    )


def solution(mesh):
    n_dp = mesh.shape["dp"]
    slots = P("section", "dp", None, None, None)
    packs = P("section", "dp", None, None)
    rows = P("section", "dp", None)
    return jax.shard_map(
        functools.partial(local, n_dp),
        mesh=mesh,
        in_specs=(rows, rows, P(None, "dp"), P("section", None), slots, slots, slots, packs, packs, packs),
        out_specs=(rows, rows, slots, slots, slots, packs, packs, packs),
        check_vma=False,
    )
```

```python
import functools
import jax
import jax.numpy as jnp
import numpy as np
from jax import lax
from jax.experimental import pallas as pl
from jax.experimental.pallas import tpu as pltpu
from jax.sharding import PartitionSpec as P

D = 512
HEADS = 8
HS = D // HEADS
FF = 2048
RU = FF // D
STEP = 5
LANES = 128
F32 = jnp.float32
BF = jnp.bfloat16
NEG = -1e30


def nn(a, b):
    return jnp.dot(a, b, preferred_element_type=F32)


def nt(a, b):
    return lax.dot_general(a, b, (((1,), (1,)), ((), ())), preferred_element_type=F32)


def tn(a, b):
    return lax.dot_general(a, b, (((0,), (0,)), ((), ())), preferred_element_type=F32)


def lane_loop(count, body):
    def step(i, carry):
        body(pl.ds(pl.multiple_of(i * LANES, LANES), LANES))
        return carry

    lax.fori_loop(0, count // LANES, step, 0, unroll=True)


def norm_parts(value):
    mean = jnp.mean(value, axis=0, keepdims=True)
    centred = value - mean
    inv = lax.rsqrt(jnp.mean(centred * centred, axis=0, keepdims=True) + 1e-05)
    return centred * inv, inv


def norm_grad(grad, normed, inv, gain):
    scaled = grad * gain
    mean_one = jnp.mean(scaled, axis=0, keepdims=True)
    mean_two = jnp.mean(scaled * normed, axis=0, keepdims=True)
    return (scaled - mean_one - normed * mean_two) * inv


def fill_bias(bias, length, causal, key_dim=0):
    rows = bias.shape[0]

    def body(lanes):
        across = lax.broadcasted_iota(jnp.int32, (rows, LANES), 0)
        along = lax.broadcasted_iota(jnp.int32, (rows, LANES), 1) + lanes.start
        key, query = (across, along) if key_dim == 0 else (along, across)
        allowed = key < length
        if causal is not None:
            allowed = allowed & ((key <= query) | jnp.logical_not(causal))
        bias[:, lanes] = jnp.where(allowed, 0.0, NEG)

    lane_loop(bias.shape[1], body)


def head_rows(h):
    return pl.ds(pl.multiple_of(h * HS, HS), HS)


def attend(qt, kt, vt, bias, length, ot, lse, pair):
    width = kt.shape[1]
    index = lax.broadcasted_iota(jnp.int32, (16, width), 0)
    if bias is None:
        masked = (index == 0) & (lax.broadcasted_iota(jnp.int32, index.shape, 1) >= length)
        masks = jnp.where(masked, NEG, 0.0).astype(BF)
        ones = jnp.where(index == 0, 1.0, 0.0).astype(BF)

    def score(h, out):
        rows = head_rows(h)
        keys, queries = kt[rows, :], qt[rows, :] * BF(0.125)
        if bias is None:
            keys = jnp.concatenate([keys, masks], axis=0)
            queries = jnp.concatenate([queries, ones], axis=0)
        out[...] = tn(keys, queries)

    def finish(h, scores):
        rows = head_rows(h)
        biased = scores[...] if bias is None else scores[...] + bias[...]
        top = jnp.max(biased, axis=0, keepdims=True)
        weights = jnp.exp(biased - top).astype(BF)
        values = jnp.concatenate([vt[rows, :], jnp.ones((16, width), BF)], axis=0)
        out = nn(values, weights)
        total = out[HS : HS + 1]
        ot[rows, :] = (out[:HS] * (1.0 / total)).astype(BF)
        lse[pl.ds(h, 1), :] = top + jnp.log(total)

    one, two = pair.at[0], pair.at[1]
    score(0, one)

    def body(i, carry):
        score(2 * i + 1, two)
        finish(2 * i, one)
        score(jnp.minimum(2 * i + 2, HEADS - 1), one)
        finish(2 * i + 1, two)
        return carry

    lax.fori_loop(0, HEADS // 2, body, 0, unroll=True)


def split_rows(row, count):
    high = row.astype(BF)
    rest = row - high.astype(F32)
    mid = rest.astype(BF)
    low = (rest - mid.astype(F32)).astype(BF)
    index = lax.broadcasted_iota(jnp.int32, (16, row.shape[1]), 0)
    parts = jnp.where(index == 0, high, jnp.where(index == 1, mid, low))
    return jnp.where(index < 3, parts, BF(count))


def attend_back(qt, kt, vt, bias, length, ot, lse, dot, dqt, dkt, dvt):
    index = lax.broadcasted_iota(jnp.int32, (16, kt.shape[1]), 0)
    ones = jnp.where(index < 3, 1.0, 0.0).astype(BF)
    masks = ones
    if bias is None:
        masked = (index == 3) & (lax.broadcasted_iota(jnp.int32, index.shape, 1) >= length)
        masks = jnp.where(masked, NEG, ones.astype(F32)).astype(BF)

    def head(h, carry):
        rows = head_rows(h)
        keys, grads = kt[rows, :], dot[rows, :]
        queries = qt[rows, :] * BF(0.125)
        delta = jnp.sum(grads.astype(F32) * ot[rows, :].astype(F32), axis=0, keepdims=True)
        left = jnp.concatenate([queries, split_rows(-lse[pl.ds(h, 1), :], 1)], axis=0)
        scores = tn(left, jnp.concatenate([keys, masks], axis=0))
        probs = jnp.exp(scores if bias is None else scores + bias[...])
        left = jnp.concatenate([grads, split_rows(-delta, 0)], axis=0)
        dscores = (probs * tn(left, jnp.concatenate([vt[rows, :], ones], axis=0))).astype(BF)
        dvt[rows, :] = nn(grads, probs.astype(BF)).astype(BF)
        dkt[rows, :] = nn(queries, dscores).astype(BF)
        dqt[rows, :] = (nt(keys, dscores) * 0.125).astype(BF)
        return carry

    lax.fori_loop(0, HEADS, head, 0, unroll=True)


GAIN, SHIFT, B2, B1 = 0, 3, 6, 7


def column(vec, index):
    return vec[:, index : index + 1]


def self_column(vec, first, row):
    return jnp.where(first, column(vec, row + 1), column(vec, row))


def add_column(dvec, index, acc):
    dvec[:, index : index + 1] += jnp.sum(acc, axis=1, keepdims=True)


def self_forward(x, sq, vec, first, length, ut, n0, r0, qt, kt, vt, ot, lse, n1, r1, y, bias, et, pair, pause):
    tokens = x.shape[0]
    et[...] = x[...].astype(F32).T

    def entry(lanes):
        value = et[:, lanes]
        normed, inv = norm_parts(value)
        n0[:, lanes] = normed.astype(BF)
        r0[:, lanes] = inv
        value = jnp.where(first, normed * column(vec, GAIN) + column(vec, SHIFT), value)
        et[:, lanes] = value
        ut[:, lanes] = value.astype(BF)

    lane_loop(tokens, entry)
    fill_bias(bias, length, jnp.logical_not(first))
    for index, out in enumerate((qt, kt, vt)):
        out[...] = tn(sq[index][...], ut[...]).astype(BF)
    pause()
    attend(qt, kt, vt, bias, length, ot, lse, pair)
    pause()
    et[...] += tn(sq[3][...], ot[...])
    gain, shift = self_column(vec, first, GAIN), self_column(vec, first, SHIFT)

    def leave(lanes):
        normed, inv = norm_parts(et[:, lanes])
        n1[:, lanes] = normed.astype(BF)
        r1[:, lanes] = inv
        y[:, lanes] = normed * gain + shift

    lane_loop(tokens, leave)


def self_backward(
    dy, sq, vec, first, length, ut, n0, r0, qt, kt, vt, ot, lse, n1, r1, dx,
    bias, dsa, dot, dqt, dkt, dvt, dsq, dvec, vacc, pause,
):
    tokens = dy.shape[1]
    vacc[...] = jnp.zeros(vacc.shape, F32)
    gain = self_column(vec, first, GAIN)

    def leave(lanes):
        grad, normed = dy[:, lanes], n1[:, lanes].astype(F32)
        vacc[2] += grad * normed
        vacc[3] += grad
        grad = norm_grad(grad, normed, r1[:, lanes], gain)
        dy[:, lanes] = grad
        dsa[:, lanes] = grad.astype(BF)

    lane_loop(tokens, leave)
    fill_bias(bias, length, jnp.logical_not(first), 1)
    dot[...] = nn(sq[3][...], dsa[...]).astype(BF)
    dsq[3] += nt(ot[...], dsa[...])
    pause()
    attend_back(qt, kt, vt, bias, length, ot, lse, dot, dqt, dkt, dvt)
    for index, grad in enumerate((dqt, dkt, dvt)):
        dsq[index] += nt(ut[...], grad[...])
        dy[...] += nn(sq[index][...], grad[...])
    pause()
    entry_gain = column(vec, GAIN)

    def entry(lanes):
        grad, normed = dy[:, lanes], n0[:, lanes].astype(F32)
        vacc[0] += grad * normed
        vacc[1] += grad
        dy[:, lanes] = jnp.where(first, norm_grad(grad, normed, r0[:, lanes], entry_gain), grad)

    lane_loop(tokens, entry)
    dx[...] = dy[...].T

    @pl.when(first)
    def _():
        add_column(dvec, GAIN, vacc[0])
        add_column(dvec, SHIFT, vacc[1])
        add_column(dvec, GAIN + 1, vacc[2])
        add_column(dvec, SHIFT + 1, vacc[3])

    @pl.when(jnp.logical_not(first))
    def _():
        add_column(dvec, GAIN, vacc[2])
        add_column(dvec, SHIFT, vacc[3])


def gelu_parts(z):
    root = 0.7978845608028654
    square = z * z
    t = jnp.tanh(z * (root + (root * 0.044715) * square))
    half = 0.5 + 0.5 * t
    act = z * half
    slope = half + act * (1.0 - t) * (root + (3.0 * root * 0.044715) * square)
    return act, slope


def feed_forward(h, units, vec, hb, act, slope, n2, r2, out):
    hb[...] = h[...].astype(BF)
    for c in range(RU):
        rows = slice(c * D, (c + 1) * D)
        a, s = gelu_parts(tn(units[c][...], hb[...]) + column(vec, B1 + c))
        act[rows, :] = a.astype(BF)
        slope[rows, :] = s.astype(BF)
    for c in range(RU):
        rows = slice(c * D, (c + 1) * D)
        h[...] += tn(units[RU + c][...], act[rows, :])

    def leave(lanes):
        normed, inv = norm_parts(h[:, lanes] + column(vec, B2))
        n2[:, lanes] = normed.astype(BF)
        r2[:, lanes] = inv
        out[:, lanes] = normed * column(vec, GAIN + 2) + column(vec, SHIFT + 2)

    lane_loop(h.shape[1], leave)


def feed_backward(dm, units, vec, hb, act, slope, n2, r2, dfb, dz, dunits, dvec, vacc):
    vacc[...] = jnp.zeros(vacc.shape, F32)

    def leave(lanes):
        grad, normed = dm[:, lanes], n2[:, lanes].astype(F32)
        vacc[RU + 1] += grad * normed
        vacc[RU + 2] += grad
        grad = norm_grad(grad, normed, r2[:, lanes], column(vec, GAIN + 2))
        dm[:, lanes] = grad
        short = grad.astype(BF)
        vacc[RU] += short.astype(F32)
        dfb[:, lanes] = short

    lane_loop(dm.shape[1], leave)
    for c in range(RU):
        rows = slice(c * D, (c + 1) * D)
        dz[rows, :] = (nn(units[RU + c][...], dfb[...]) * slope[rows, :].astype(F32)).astype(BF)
        dunits[RU + c][...] += nt(act[rows, :], dfb[...])
    for c in range(RU):
        rows = slice(c * D, (c + 1) * D)
        dm[...] += nn(units[c][...], dz[rows, :])
        dunits[c][...] += nt(hb[...], dz[rows, :])
        for lanes in range(0, dm.shape[1], LANES):
            vacc[c] += dz[rows, lanes : lanes + LANES].astype(F32)
    for index in range(RU):
        add_column(dvec, B1 + index, vacc[index])
    add_column(dvec, B2, vacc[RU])
    add_column(dvec, GAIN + 2, vacc[RU + 1])
    add_column(dvec, SHIFT + 2, vacc[RU + 2])


def cross_forward(a, sq, vec, length, ab, cqt, kt, vt, ot, lse, n1, r1, pair):
    ab[...] = a[...].astype(BF)
    cqt[...] = tn(sq[0][...], ab[...]).astype(BF)
    attend(cqt, kt, vt, None, length, ot, lse, pair)
    a[...] += tn(sq[1][...], ot[...])

    def leave(lanes):
        normed, inv = norm_parts(a[:, lanes])
        n1[:, lanes] = normed.astype(BF)
        r1[:, lanes] = inv
        a[:, lanes] = normed * column(vec, GAIN + 1) + column(vec, SHIFT + 1)

    lane_loop(a.shape[1], leave)


def cross_backward(
    dbq, sq, vec, length, ab, cqt, kt, vt, ot, lse, n1, r1, dca, dot, dqt, dkt, dvt, dsq, dvec, vacc, ready
):
    vacc[0] = jnp.zeros(vacc.shape[1:], F32)
    vacc[1] = jnp.zeros(vacc.shape[1:], F32)

    def leave(lanes):
        grad, normed = dbq[:, lanes], n1[:, lanes].astype(F32)
        vacc[0] += grad * normed
        vacc[1] += grad
        grad = norm_grad(grad, normed, r1[:, lanes], column(vec, GAIN + 1))
        dbq[:, lanes] = grad
        dca[:, lanes] = grad.astype(BF)

    lane_loop(dbq.shape[1], leave)
    dot[...] = nn(sq[1][...], dca[...]).astype(BF)
    dsq[1][...] += nt(ot[...], dca[...])
    attend_back(cqt, kt, vt, None, length, ot, lse, dot, dqt, dkt, dvt)
    ready()
    dsq[0][...] += nt(ab[...], dqt[...])
    dbq[...] += nn(sq[0][...], dqt[...])
    add_column(dvec, GAIN + 1, vacc[0])
    add_column(dvec, SHIFT + 1, vacc[1])


SUB = 256
HOP = 4
HALF = SUB // 2
QUART = SUB // 4
UNITS = 6 + 2 * RU
VEC_ROWS = 256
SUBS = (UNITS * D + VEC_ROWS) // SUB
MESH = pl.DeviceIdType.MESH


class Total:
    def __init__(self, n_dp, order, shorts, other, mine, out, core_in, half, x_in, right_in, left_in, passed, sems):
        self.length = n_dp // 4
        self.last = self.length - 1
        self.section = lax.axis_index("section")
        self.dp = lax.axis_index("dp")
        self.core, self.x, self.z = self.dp % 2, (self.dp // 2) % 2, self.dp // 4
        self.sibling, self.beside = self.dp + 1 - 2 * self.core, self.dp + 2 - 4 * self.x
        self.has_left, self.has_right = self.z > 0, self.z < self.last
        self.order, self.shorts, self.other, self.mine = order, shorts, other, mine
        self.out, self.core_in, self.half, self.x_in = out, core_in, half, x_in
        self.right_in, self.left_in, self.passed, self.sems = right_in, left_in, passed, sems
        far = self.last
        self.ticks = SUBS + HOP * (2 + far + far) + 1

    def greet(self, across=False):
        barrier = pltpu.get_barrier_semaphore()

        def signal(index):
            pl.semaphore_signal(barrier, inc=1, device_id=(self.section, index), device_id_type=MESH)

        signal(self.sibling)
        signal(self.beside)
        pl.when(self.has_left)(lambda: signal(self.dp - 4))
        pl.when(self.has_right)(lambda: signal(self.dp + 4))
        if across:
            pl.semaphore_signal(barrier, inc=1, device_id=(1 - self.section, self.dp), device_id_type=MESH)
        sides = self.has_left.astype(jnp.int32) + self.has_right.astype(jnp.int32)
        pl.semaphore_wait(barrier, 2 + int(across) + sides)

    def short_route(self, t):
        return ((t & 1) == 0) | ((t >= self.shorts[0]) & (t < self.shorts[1]))

    def home(self, t):
        return (t >> 1) & self.last

    def place(self, t, start, size):
        return pl.ds(pl.multiple_of(self.order(t) * SUB + start, QUART), size)

    def send(self, step, t, source, target, index):
        return pltpu.make_async_remote_copy(
            src_ref=source,
            dst_ref=target,
            send_sem=self.sems.at[0, step, t],
            recv_sem=self.sems.at[1, step, t],
            device_id=(self.section, index),
            device_id_type=MESH,
        )

    def part(self, size, index):
        return pl.ds(pl.multiple_of(index * size, size), size)

    def copy_core(self, t):
        source = self.other(t, self.order(t), HALF * (1 - self.core))
        return self.send(0, t, source, self.core_in.at[t], self.sibling)

    def copy_x(self, t):
        rows = self.part(QUART, 1 - self.x)
        return self.send(1, t, self.half.at[t, rows], self.x_in.at[t, pl.ds(0, QUART)], self.beside)

    def copy_x_whole(self, t):
        return self.send(1, t, self.passed.at[t], self.x_in.at[t], self.beside)

    def copy_right(self, t, source):
        return self.send(2, t, source, self.right_in.at[t, pl.ds(0, QUART)], self.dp + 4)

    def copy_left(self, t, source):
        return self.send(3, t, source, self.left_in.at[t, pl.ds(0, QUART)], self.dp - 4)

    def copy_right_whole(self, t, source):
        return self.send(2, t, source, self.right_in.at[t], self.dp + 4)

    def copy_left_whole(self, t, source):
        return self.send(3, t, source, self.left_in.at[t], self.dp - 4)

    def copy_back_x(self, t):
        place = self.place(t, HALF * self.core + QUART * self.x, QUART)
        return self.send(4, t, self.out.at[place], self.out.at[place], self.beside)

    def copy_back_core(self, t):
        place = self.place(t, HALF * self.core, HALF)
        return self.send(5, t, self.out.at[place], self.out.at[place], self.sibling)

    def copy_back_right(self, t):
        place = self.place(t, HALF * self.core, HALF)
        return self.send(4, t, self.out.at[place], self.out.at[place], self.dp + 4)

    def copy_back_left(self, t):
        place = self.place(t, HALF * self.core, HALF)
        return self.send(6, t, self.out.at[place], self.out.at[place], self.dp - 4)

    def add(self, one, two):
        return one + two

    def own_quarter(self, t):
        return self.half.at[t, self.part(QUART, self.x)]

    def short_core(self, t):
        self.copy_core(t).wait_recv()
        self.half[t] = self.add(self.mine(t, self.order(t), HALF * self.core), self.core_in[t])
        self.copy_x(t).start()

    def short_x(self, t):
        self.copy_x(t).wait_recv()
        quart = self.own_quarter(t)
        quart[...] = self.add(quart[...], self.x_in[t, 0:QUART])

        @pl.when(jnp.logical_not(self.has_left) & self.has_right)
        def _():
            self.copy_right(t, quart).start()

        @pl.when(jnp.logical_not(self.has_right) & self.has_left)
        def _():
            self.copy_left(t, quart).start()

    def short_right(self, t):
        @pl.when(self.has_left)
        def _():
            target = self.passed.at[t, pl.ds(0, QUART)]
            self.copy_right(t, target).wait_recv()

            @pl.when(self.has_right)
            def _():
                target[...] = self.add(self.own_quarter(t)[...], self.right_in[t, 0:QUART])
                self.copy_right(t, target).start()

    def short_left(self, t):
        @pl.when(self.has_right)
        def _():
            target = self.passed.at[t, pl.ds(QUART, QUART)]
            self.copy_left(t, target).wait_recv()

            @pl.when(self.has_left)
            def _():
                target[...] = self.add(self.own_quarter(t)[...], self.left_in[t, 0:QUART])
                self.copy_left(t, target).start()

    def short_total(self, t):
        total = self.own_quarter(t)[...].astype(F32)
        total += jnp.where(self.has_left, self.right_in[t, 0:QUART].astype(F32), 0.0)
        total += jnp.where(self.has_right, self.left_in[t, 0:QUART].astype(F32), 0.0)
        self.out[self.place(t, HALF * self.core + QUART * self.x, QUART), :] = total.astype(BF)
        self.copy_back_x(t).start()

    def short_back(self, t):
        self.copy_back_x(t).wait_recv()
        self.copy_back_core(t).start()

    def long_core(self, t):
        self.copy_core(t).wait_recv()
        self.half[t] = self.add(self.mine(t, self.order(t), HALF * self.core), self.core_in[t])
        home = self.home(t)

        @pl.when(jnp.logical_not(self.has_left) & (home > 0))
        def _():
            self.copy_right_whole(t, self.half.at[t]).start()

        @pl.when(jnp.logical_not(self.has_right) & (home < self.last))
        def _():
            self.copy_left_whole(t, self.half.at[t]).start()

    def long_right(self, t):
        @pl.when(self.has_left & (self.z < self.home(t)))
        def _():
            self.copy_right_whole(t, self.passed.at[t]).wait_recv()
            self.passed[t] = self.add(self.half[t], self.right_in[t])
            self.copy_right_whole(t, self.passed.at[t]).start()

    def long_left(self, t):
        @pl.when(self.has_right & (self.z > self.home(t)))
        def _():
            self.copy_left_whole(t, self.passed.at[t]).wait_recv()
            self.passed[t] = self.add(self.half[t], self.left_in[t])
            self.copy_left_whole(t, self.passed.at[t]).start()

    def long_home(self, t):
        @pl.when(self.z == self.home(t))
        def _():
            pl.when(self.has_left)(lambda: self.copy_right_whole(t, self.half.at[t]).wait_recv())
            pl.when(self.has_right)(lambda: self.copy_left_whole(t, self.half.at[t]).wait_recv())
            total = self.half[t].astype(F32)
            total += jnp.where(self.has_left, self.right_in[t].astype(F32), 0.0)
            total += jnp.where(self.has_right, self.left_in[t].astype(F32), 0.0)
            self.passed[t] = total.astype(BF)
            self.copy_x_whole(t).start()

    def long_x(self, t):
        @pl.when(self.z == self.home(t))
        def _():
            self.copy_x_whole(t).wait_recv()
            self.out[self.place(t, HALF * self.core, HALF), :] = self.add(self.passed[t], self.x_in[t])
            pl.when(self.has_left)(lambda: self.copy_back_left(t).start())
            pl.when(self.has_right)(lambda: self.copy_back_right(t).start())
            self.copy_back_core(t).start()

    def long_back(self, t):
        home = self.home(t)

        @pl.when(self.z > home)
        def _():
            self.copy_back_right(t).wait_recv()
            pl.when(self.has_right)(lambda: self.copy_back_right(t).start())

        @pl.when(self.z < home)
        def _():
            self.copy_back_left(t).wait_recv()
            pl.when(self.has_left)(lambda: self.copy_back_left(t).start())

        pl.when(self.z != home)(lambda: self.copy_back_core(t).start())

    def tick(self, now, prepare):
        z, last = self.z, self.last
        far = jnp.maximum(z, last - z)
        prepared = now

        @pl.when(prepared < SUBS)
        def _():
            prepare(prepared)
            self.copy_core(prepared).start()

        def due(step, lag, short):
            t = now - HOP * lag
            fits = (t >= 0) & (t < SUBS)
            kind = self.short_route(t) if short else jnp.logical_not(self.short_route(t))
            pl.when(fits & kind)(lambda: step(t))

        due(self.short_core, 1, True)
        due(self.short_x, 2, True)
        due(self.short_right, 2 + z, True)
        due(self.short_left, 2 + last - z, True)
        due(self.short_total, 2 + far, True)
        due(self.short_back, 3 + far, True)
        due(self.long_core, 1, False)
        due(self.long_right, 1 + z, False)
        due(self.long_left, 1 + last - z, False)
        due(self.long_home, 1 + far, False)
        due(self.long_x, 2 + far, False)
        for home in range(self.length):
            lag = 2 + max(home, last - home) + jnp.abs(z - home)
            t = now - HOP * lag
            fits = (t >= 0) & (t < SUBS) & jnp.logical_not(self.short_route(t)) & (self.home(t) == home)
            pl.when(fits & (z != home))(lambda t=t: self.long_back(t))

    def arrive(self, t):
        self.copy_back_core(t).wait_recv()

    def settle(self, t):
        self.copy_core(t).wait_send()
        self.copy_back_core(t).wait_send()
        home = self.home(t)

        @pl.when(self.short_route(t))
        def _():
            self.copy_x(t).wait_send()
            pl.when(self.has_right)(lambda: self.copy_right(t, self.own_quarter(t)).wait_send())
            pl.when(self.has_left)(lambda: self.copy_left(t, self.own_quarter(t)).wait_send())
            self.copy_back_x(t).wait_send()

        @pl.when(jnp.logical_not(self.short_route(t)))
        def _():
            pl.when(self.z < home)(lambda: self.copy_right_whole(t, self.half.at[t]).wait_send())
            pl.when(self.z > home)(lambda: self.copy_left_whole(t, self.half.at[t]).wait_send())
            pl.when(self.z == home)(lambda: self.copy_x_whole(t).wait_send())
            pl.when(self.has_right & (self.z >= home))(lambda: self.copy_back_right(t).wait_send())
            pl.when(self.has_left & (self.z <= home))(lambda: self.copy_back_left(t).wait_send())


def loop(start, stop, body):
    def step(i, carry):
        body(i)
        return carry

    lax.fori_loop(start, stop, step, 0)


def total_scratch():
    return [pltpu.VMEM((SUBS, HALF, D), BF)] * 6 + [pltpu.SemaphoreType.DMA((2, 7, SUBS))]


def any_space():
    return pl.BlockSpec(memory_space=pl.ANY)


def vmem_space():
    return pl.BlockSpec(memory_space=pltpu.VMEM)


def smem_space():
    return pl.BlockSpec(memory_space=pltpu.SMEM)


def block_spec(*dims):
    return pl.BlockSpec((1,) + dims, lambda b, info: (b,) + (0,) * len(dims))


def shape32(*dims):
    return jax.ShapeDtypeStruct(dims, F32)


def shape16(*dims):
    return jax.ShapeDtypeStruct(dims, BF)


TENSOR_OF = (0, 1, 2, 3, 4, 5) + (6,) * RU + (7,) * RU
TENSOR_SIZE = (1,) * 6 + (RU, RU)
FIRST_UNIT = (0, 1, 2, 3, 4, 5, 6, 6 + RU)
VEC_BLOCKS = VEC_ROWS // SUB
EARLY = 4 * D // SUB + VEC_BLOCKS
LINKED = 6 * D // SUB + VEC_BLOCKS
PIECE = 16


def copies(sources, targets, sems):
    return [pltpu.make_async_copy(s, t, sems.at[i]) for i, (s, t) in enumerate(zip(sources, targets))]


def slot_of(owners, tensor):
    prior = jnp.int32(0)
    for earlier in range(tensor):
        prior += jnp.where(owners[0, earlier] == owners[0, tensor], TENSOR_SIZE[earlier], 0)
    return prior


def start_kernel(n_dp, info, owners, x, slots, pack, out, vec, linked, *refs):
    saved_out, (y_out, stage, *comm), refs = refs[:10], refs[10:19], refs[19:]
    saved, (y, xb, bias, et, pair, places, counter, sems, link_sems) = refs[:10], refs[10:]
    count, tokens = saved_out[0].shape[0], saved_out[0].shape[2]
    first = lax.axis_index("section") == 0
    dp = lax.axis_index("dp")
    for unit in range(UNITS):
        tensor = TENSOR_OF[unit]
        slot = jnp.minimum(slot_of(owners, tensor) + (unit - FIRST_UNIT[tensor]), slots.shape[0] - 1)
        places[0, unit] = slot
        places[1, unit] = (owners[0, tensor] == dp).astype(jnp.int32)

    def own(block, start):
        is_pack = block >= SUBS - VEC_BLOCKS
        unit = jnp.minimum(block * SUB // D, UNITS - 1)
        at = pl.multiple_of((block * SUB) % D + start, HALF)
        value = jnp.where(places[1, unit] == 1, slots[places[0, unit], pl.ds(at, HALF), :], 0.0).astype(BF)
        return jnp.where(is_pack, pack[pl.ds(pl.multiple_of(start, HALF), HALF), :], value)

    def order(t):
        return jnp.where(t < VEC_BLOCKS, t + SUBS - VEC_BLOCKS, t - VEC_BLOCKS)

    total = Total(
        n_dp,
        order,
        (0, LINKED),
        lambda t, block, start: stage.at[t],
        lambda t, block, start: own(block, start),
        out,
        *comm,
    )

    def prepare(t):
        stage[t] = own(order(t), HALF * (1 - total.core))

    def run(ticks):
        begin = counter[0]
        stop = jnp.minimum(begin + ticks, total.ticks)
        loop(begin, stop, lambda now: total.tick(now, prepare))
        counter[0] = stop

    link = pltpu.make_async_remote_copy(
        src_ref=out.at[pl.ds(4 * D, 2 * D)],
        dst_ref=linked,
        send_sem=link_sems.at[0],
        recv_sem=link_sems.at[1],
        device_id=(1 - total.section, dp),
        device_id_type=MESH,
    )
    total.greet(across=True)
    counter[0] = 0
    run(EARLY + HOP * (3 + total.last))
    loop(0, EARLY, total.arrive)
    rows = [out[pl.ds(UNITS * D + i * PIECE, PIECE), :].astype(F32) for i in range(3)]
    whole = jnp.concatenate([rows[0] + rows[1] + rows[2], jnp.zeros((LANES - PIECE, D), F32)], axis=0)
    vec[...] = whole.T
    squares = [out.at[pl.ds(i * D, D)] for i in range(4)]

    def outward(b):
        return copies(saved + (y,), [ref.at[b] for ref in saved_out + (y_out,)], sems)

    def block(b):
        @pl.when(b == 1)
        def _():
            run(jnp.maximum(LINKED + HOP * (3 + total.last) - counter[0], 0))
            loop(EARLY, LINKED, total.arrive)
            pl.when(first)(lambda: link.start())

        load = pltpu.make_async_copy(x.at[pl.ds(pl.multiple_of(b * tokens, tokens), tokens)], xb, sems.at[11])
        load.start()

        @pl.when(b > 0)
        def _():
            for copy in outward(b - 1):
                copy.wait()

        load.wait()
        self_forward(
            xb, squares, vec, first, info[1 + b], *saved, y, bias, et, pair, lambda: run(2)
        )
        for copy in outward(b):
            copy.start()
        run(1)

    loop(0, count, block)
    run(total.ticks)
    for copy in outward(count - 1):
        copy.wait()
    loop(LINKED, SUBS, total.arrive)
    loop(0, SUBS, total.settle)
    pl.when(first)(lambda: link.wait_send())
    pl.when(jnp.logical_not(first))(lambda: link.wait_recv())


def saved_dims(tokens):
    wide, row = ((D, tokens), BF), ((1, tokens), F32)
    return [wide, wide, row, wide, wide, wide, wide, ((HEADS, tokens), F32), wide, row]


def call_start(n_dp, info, owners, x, slots, pack, count):
    tokens = x.shape[0] // count
    kept = saved_dims(tokens)
    scores = pltpu.VMEM((tokens, tokens), F32)
    return pl.pallas_call(
        functools.partial(start_kernel, n_dp),
        name="start",
        out_shape=[shape16(SUBS * SUB, D), shape32(D, LANES), shape16(2 * D, D)]
        + [jax.ShapeDtypeStruct((count,) + dims, kind) for dims, kind in kept]
        + [shape32(count, D, tokens)],
        in_specs=[smem_space(), smem_space(), any_space(), vmem_space(), vmem_space()],
        out_specs=[vmem_space()] * 3 + [any_space()] * 11,
        scratch_shapes=[pltpu.VMEM((SUBS, HALF, D), BF)]
        + total_scratch()
        + [pltpu.VMEM(dims, kind) for dims, kind in kept]
        + [
            pltpu.VMEM((D, tokens), F32),
            pltpu.VMEM((tokens, D), BF),
            scores,
            pltpu.VMEM((D, tokens), F32),
            pltpu.VMEM((2, tokens, tokens), F32),
            pltpu.SMEM((2, UNITS), jnp.int32),
            pltpu.SMEM((1,), jnp.int32),
            pltpu.SemaphoreType.DMA((12,)),
            pltpu.SemaphoreType.DMA((2,)),
        ],
        compiler_params=pltpu.CompilerParams(
            collective_id=0, has_side_effects=True, vmem_limit_bytes=60 * 2**20
        ),
    )(info, owners, x, slots, pack)


def finish_kernel(n_dp, info, dy, sq, vec, late, late_vec, dsq_in, dx_in, *refs):
    saved_in, (dx_out, out), (stage, *comm), refs = refs[:10], refs[10:12], refs[12:20], refs[20:]
    saved, (dys, dx, bias, dsa, dot, dqt, dkt, dvt, dsq, dvec, vacc, pack, counter, sems) = refs[:10], refs[10:]
    count, tokens = dy.shape[0], dy.shape[2]
    first = lax.axis_index("section") == 0
    early = EARLY - VEC_BLOCKS
    others = SUBS - EARLY

    def order(t):
        return jnp.where(t < others, t + early, jnp.where(t < SUBS - VEC_BLOCKS, t - others, t))

    def late_rows(block, start):
        return pl.ds(pl.multiple_of((block - early) * SUB + start, HALF), HALF)

    def own_early(block, start):
        unit = jnp.minimum(block * SUB // D, 3)
        at = pl.multiple_of((block * SUB) % D + start, HALF)
        value = dsq[unit, pl.ds(at, HALF), :].astype(BF)
        return jnp.where(block >= SUBS - VEC_BLOCKS, pack[pl.ds(pl.multiple_of(start, HALF), HALF), :], value)

    def mine(t, block, start):
        at = jnp.clip((block - early) * SUB, 0, (others - 1) * SUB) + start
        return jnp.where(t < others, late[pl.ds(pl.multiple_of(at, HALF), HALF), :], own_early(block, start))

    total = Total(
        n_dp, order, (others, SUBS), lambda t, block, start: stage.at[t], mine, out, *comm
    )

    def prepare(t):
        stage[t] = mine(t, order(t), HALF * (1 - total.core))

    def run(ticks, end):
        begin = counter[0]
        stop = jnp.minimum(begin + ticks, end)
        loop(begin, stop, lambda now: total.tick(now, prepare))
        counter[0] = stop

    total.greet()
    counter[0] = 0
    load_dsq = pltpu.make_async_copy(dsq_in, dsq, sems.at[12])
    load_dsq.start()
    dvec[...] = late_vec[...]
    load_dsq.wait()
    begin = count // 2
    squares = [sq.at[pl.ds(i * D, D)] for i in range(4)]

    def block(b):
        loads = copies([ref.at[b] for ref in saved_in] + [dy.at[b]], saved + (dys,), sems)
        for copy in loads:
            copy.start()
        run(4, others)

        def store(b):
            return pltpu.make_async_copy(
                dx, dx_out.at[pl.ds(pl.multiple_of(b * tokens, tokens), tokens)], sems.at[11]
            )

        pl.when(b > begin)(lambda: store(b - 1).wait())
        for copy in loads:
            copy.wait()
        self_backward(
            dys, squares, vec, first, info[1 + b], *saved, dx,
            bias, dsa, dot, dqt, dkt, dvt, dsq, dvec, vacc, lambda: run(3, others),
        )
        store(b).start()
        pl.when(b == count - 1)(lambda: store(b).wait())

    loop(begin, count, block)
    value = dvec[...].T[:PIECE]
    high = value.astype(BF)
    rest = value - high.astype(F32)
    mid = rest.astype(BF)
    pack[...] = jnp.zeros(pack.shape, BF)
    pack[0:PIECE, :] = high
    pack[PIECE : 2 * PIECE, :] = mid
    pack[2 * PIECE : 3 * PIECE, :] = (rest - mid.astype(F32)).astype(BF)
    run(total.ticks, total.ticks)
    loop(0, SUBS, total.arrive)
    loop(0, SUBS, total.settle)


def call_finish(n_dp, info, dy, weights, vec, late, late_vec, dsq, dx, saved):
    count, tokens = dy.shape[0], dy.shape[2]
    kept = saved_dims(tokens)
    wide16 = pltpu.VMEM((D, tokens), BF)
    wide32 = pltpu.VMEM((D, tokens), F32)
    return pl.pallas_call(
        functools.partial(finish_kernel, n_dp),
        name="finish",
        out_shape=[shape32(count * tokens, D), shape16(SUBS * SUB, D)],
        grid=(1,),
        in_specs=[
            smem_space(),
            any_space(),
            pl.BlockSpec((4 * D, D), lambda i: (0, 0)),
            vmem_space(),
            vmem_space(),
            vmem_space(),
        ]
        + [any_space()] * 12,
        out_specs=[any_space(), vmem_space()],
        input_output_aliases={7: 0},
        scratch_shapes=[pltpu.VMEM((SUBS, HALF, D), BF)]
        + total_scratch()
        + [pltpu.VMEM(dims, kind) for dims, kind in kept]
        + [wide32, pltpu.VMEM((tokens, D), F32), pltpu.VMEM((tokens, tokens), F32)]
        + [wide16] * 5
        + [
            pltpu.VMEM((4, D, D), F32),
            pltpu.VMEM((D, LANES), F32),
            pltpu.VMEM((4, D, LANES), F32),
            pltpu.VMEM((VEC_ROWS, D), BF),
            pltpu.SMEM((1,), jnp.int32),
            pltpu.SemaphoreType.DMA((13,)),
        ],
        compiler_params=pltpu.CompilerParams(
            collective_id=2, has_side_effects=True, vmem_limit_bytes=60 * 2**20
        ),
    )(info, dy, weights, vec, late, late_vec, dsq, dx, *saved)


def middle_kernel(info, vec, y, cot, weights, linked, *refs):
    saved_in, outs, refs = refs[:10], refs[10:16], refs[16:]
    hidden, dy, dx_out, grads, dsq_out, dvec = outs
    saved, refs = refs[:10], refs[10:]
    ut, n0, r0, qt, kt, vt, ot, lse, n1, r1 = saved
    (
        wts, acc, dsq, sent, got, hbuf, mem, hb, act, slope, n2, r2, dfb, dz, vacc,
        bias, dca, dot, dqt, dkt, dvt, pair, cotb, tok, dx, link, swaps, sems, saved_sems, grad_sems,
    ) = refs
    section = lax.axis_index("section")
    first = section == 0
    dp = lax.axis_index("dp")
    count, tokens = y.shape[0], y.shape[2]
    other = 1 - section
    barrier = pltpu.get_barrier_semaphore()
    pl.semaphore_signal(barrier, inc=1, device_id=(other, dp), device_id_type=MESH)
    pl.semaphore_wait(barrier, 1)

    def remote(source, target, step, b):
        return pltpu.make_async_remote_copy(
            src_ref=source,
            dst_ref=target,
            send_sem=swaps.at[step, b],
            recv_sem=swaps.at[step + 1, b],
            device_id=(other, dp),
            device_id_type=MESH,
        )

    def send_memory(b):
        return remote(sent.at[b, 0], got.at[b, 0], 0, b)

    def send_back(b):
        return remote(sent.at[b], got.at[b], 2, b)

    def rows(b):
        return pl.ds(pl.multiple_of(b * tokens, tokens), tokens)

    def load_y(b):
        return pltpu.make_async_copy(y.at[b], hbuf.at[b % 2], sems.at[0])

    def load_cot(b):
        return pltpu.make_async_copy(cot.at[rows(b)], cotb, sems.at[1])

    def store_hidden(b):
        return pltpu.make_async_copy(tok, hidden.at[rows(b)], sems.at[2])

    def store_dy(b):
        return pltpu.make_async_copy(hbuf.at[b % 2], dy.at[b], sems.at[3])

    def load_dy(b):
        return pltpu.make_async_copy(dy.at[b], hbuf.at[b % 2], sems.at[0])

    def store_dx(b):
        return pltpu.make_async_copy(dx, dx_out.at[rows(b)], sems.at[4])

    def load_saved(b):
        return copies([ref.at[b] for ref in saved_in], saved, saved_sems)

    unit = [wts.at[pl.ds(i * D, D)] for i in range(UNITS)]
    part = 6 * D
    load_rest = pltpu.make_async_copy(
        weights.at[pl.ds(part, UNITS * D - part)], wts.at[pl.ds(part, UNITS * D - part)], sems.at[5]
    )
    load_squares = pltpu.make_async_copy(weights.at[pl.ds(0, part)], wts.at[pl.ds(0, part)], sems.at[6])
    load_link = pltpu.make_async_copy(linked, link, sems.at[7])
    load_y(0).start()
    load_rest.start()
    pl.when(jnp.logical_not(first))(lambda: load_link.start())
    load_squares.start()
    s4, s5, ffn = unit[4], unit[5], unit[6:]
    cross_acc = [acc.at[i] for i in range(2)]
    ffn_acc = [acc.at[2 + i] for i in range(2 * RU)]

    def clear():
        acc[...] = jnp.zeros(acc.shape, F32)
        dsq[...] = jnp.zeros(dsq.shape, F32)
        dvec[...] = jnp.zeros(dvec.shape, F32)

    def run_feed_forward(h):
        feed_forward(h, ffn, vec, hb, act, slope, n2, r2, mem)

    def emit_hidden(b):
        pl.when(b > 0)(lambda: store_hidden(b - 1).wait())
        tok[...] = mem[...].T.astype(BF)
        store_hidden(b).start()

    def take_cotangent(b, h):
        load_cot(b).wait()
        token = lax.broadcasted_iota(jnp.int32, (D, tokens), 1)
        h[...] = jnp.where(token < info[1 + b], cotb[...].astype(F32).T, 0.0)

    def run_feed_backward(h):
        feed_backward(h, ffn, vec, hb, act, slope, n2, r2, dfb, dz, ffn_acc, dvec, vacc)

    def run_self_backward(b, h):
        pl.when(b > 0)(lambda: store_dx(b - 1).wait())
        self_backward(
            h, unit[:4], vec, first, info[1 + b], *saved, dx,
            bias, dca, dot, dqt, dkt, dvt, dsq, dvec, vacc.at[pl.ds(0, 4)], lambda: None,
        )
        store_dx(b).start()

    @pl.when(first)
    def _():
        load_rest.wait()

        def ahead(b):
            h = hbuf.at[b % 2]
            load_y(b).wait()
            pl.when(b + 1 < count)(lambda: load_y(b + 1).start())
            run_feed_forward(h)
            sent[b, 0] = mem[...].astype(BF)
            send_memory(b).start()
            emit_hidden(b)

        loop(0, count, ahead)
        store_hidden(count - 1).wait()
        load_squares.wait()
        clear()
        load_y(0).start()

        def back(b):
            h = hbuf.at[b % 2]
            loads = load_saved(b)
            load_cot(b).start()
            load_y(b).wait()
            pl.when(b < count // 2)(lambda: [copy.start() for copy in loads] and None)
            run_feed_forward(h)
            take_cotangent(b, h)
            send_back(b).wait_recv()
            for i, matrix in enumerate((s4, s5)):
                h[...] += nn(matrix[...], got[b, i])
                acc[i] += nt(sent[b, 0], got[b, i])
            run_feed_backward(h)

            @pl.when(b < count // 2)
            def _():
                load_y(b + 1).start()
                for copy in loads:
                    copy.wait()
                run_self_backward(b, h)

            @pl.when(b >= count // 2)
            def _():
                store_dy(b).start()

                @pl.when(b + 1 < count)
                def _():
                    load_y(b + 1).start()
                    store_dy(b).wait()

        loop(0, count, back)
        store_dy(count - 1).wait()
        store_dx(count // 2 - 1).wait()

    @pl.when(jnp.logical_not(first))
    def _():
        clear()
        load_rest.wait()
        load_squares.wait()
        load_link.wait()

        def both(b):
            h = hbuf.at[b % 2]
            load_cot(b).start()
            load_y(b).wait()
            send_memory(b).wait_recv()
            for i, target in enumerate((kt, vt)):
                target[...] = tn(link[pl.ds(i * D, D), :], got[b, 0]).astype(BF)
            cross = (ut, qt, kt, vt, ot, lse, n1, r1)
            cross_forward(h, (s4, s5), vec, info[1 + count + b], *cross, pair)
            run_feed_forward(h)
            emit_hidden(b)
            take_cotangent(b, h)

            pl.when(b > 0)(lambda: store_dy(b - 1).wait())
            pl.when(b + 1 < count)(lambda: load_y(b + 1).start())
            run_feed_backward(h)
            cross_backward(
                h, (s4, s5), vec, info[1 + count + b], *cross, dca, dot, dqt,
                sent.at[b, 0], sent.at[b, 1], cross_acc, dvec, vacc, lambda: send_back(b).start(),
            )
            store_dy(b).start()

        loop(0, count, both)
        store_hidden(count - 1).wait()
        store_dy(count - 1).wait()

        def back(b):
            loads = load_saved(b)
            for copy in loads + [load_dy(b)]:
                copy.start()
            for copy in loads + [load_dy(b)]:
                copy.wait()
            run_self_backward(b, hbuf.at[b % 2])

        loop(0, count // 2, back)
        store_dx(count // 2 - 1).wait()

    @pl.when(first)
    def _():
        loop(0, count, lambda b: send_memory(b).wait_send())

    @pl.when(jnp.logical_not(first))
    def _():
        loop(0, count, lambda b: send_back(b).wait_send())

    out_dsq = pltpu.make_async_copy(dsq, dsq_out, sems.at[6])
    out_dsq.start()
    out_grads = []
    for i in range(10):
        rows_i = pl.ds(i * D, D)
        wts[rows_i, :] = acc[i].astype(BF)
        out_grads.append(pltpu.make_async_copy(wts.at[rows_i], grads.at[rows_i], grad_sems.at[i]))
        out_grads[-1].start()
    for copy in out_grads:
        copy.wait()
    out_dsq.wait()


def call_middle(info, vec, y, cot, weights, linked, saved):
    count, tokens = y.shape[0], y.shape[2]
    kept = saved_dims(tokens)
    wide16 = pltpu.VMEM((D, tokens), BF)
    wide32 = pltpu.VMEM((D, tokens), F32)
    tall16 = pltpu.VMEM((FF, tokens), BF)
    return pl.pallas_call(
        middle_kernel,
        name="middle",
        out_shape=[
            shape16(count * tokens, D),
            shape32(count, D, tokens),
            shape32(count * tokens, D),
            shape16(10 * D, D),
            shape32(4, D, D),
            shape32(D, LANES),
        ],
        in_specs=[smem_space(), vmem_space()] + [any_space()] * 14,
        out_specs=[any_space()] * 5 + [vmem_space()],
        scratch_shapes=[pltpu.VMEM(dims, kind) for dims, kind in kept]
        + [
            pltpu.VMEM((UNITS * D, D), BF),
            pltpu.VMEM((10, D, D), F32),
            pltpu.VMEM((4, D, D), F32),
            pltpu.VMEM((count, 2, D, tokens), BF),
            pltpu.VMEM((count, 2, D, tokens), BF),
            pltpu.VMEM((2, D, tokens), F32),
            wide32, wide16, tall16, tall16, wide16,
            pltpu.VMEM((1, tokens), F32),
            wide16, tall16,
            pltpu.VMEM((RU + 3, D, LANES), F32),
            pltpu.VMEM((tokens, tokens), F32),
            wide16, wide16, wide16, wide16, wide16,
            pltpu.VMEM((2, tokens, tokens), F32),
            pltpu.VMEM((tokens, D), BF),
            pltpu.VMEM((tokens, D), BF),
            pltpu.VMEM((tokens, D), F32),
            pltpu.VMEM((2 * D, D), BF),
            pltpu.SemaphoreType.DMA((4, count)),
            pltpu.SemaphoreType.DMA((8,)),
            pltpu.SemaphoreType.DMA((10,)),
            pltpu.SemaphoreType.DMA((10,)),
        ],
        compiler_params=pltpu.CompilerParams(
            collective_id=1, has_side_effects=True, vmem_limit_bytes=62 * 2**20
        ),
    )(info, vec, y, cot, weights, linked, *saved)


matrix_rate = 0.04
vector_rate = 0.25
matrix_decay = 0.01


def adam_update(weight, moment_old, square_old, gradient, learn_rate, decay_rate):
    moment_one = 0.5 * moment_old + 0.5 * gradient
    moment_two = 0.5 * square_old + 0.5 * gradient * gradient
    correction = 1.0 - 0.5**STEP
    adam_step = moment_one / correction / (jnp.sqrt(moment_two / correction) + 1e-08)
    return (weight - learn_rate * (adam_step + decay_rate * weight), moment_one, moment_two)


def adam_kernel(place, grad, weight, first, second, weight_out, first_out, second_out):
    taken = place[pl.program_id(0)] >= 0
    fresh = adam_update(weight[0], first[0], second[0], grad[...].astype(F32), matrix_rate, matrix_decay)
    for new, old, out in zip(fresh, (weight, first, second), (weight_out, first_out, second_out)):
        out[0] = jnp.where(taken, new, old[0])


def call_adam(place, grads, weight, first, second):
    slots = weight.shape[0]
    spec = block_spec(D, D)
    out = shape32(slots, D, D)
    return pl.pallas_call(
        adam_kernel,
        name="adam",
        out_shape=[out] * 3,
        grid_spec=pltpu.PrefetchScalarGridSpec(
            num_scalar_prefetch=1,
            grid=(slots,),
            in_specs=[pl.BlockSpec((D, D), lambda s, place: (jnp.maximum(place[s], 0), 0))] + [spec] * 3,
            out_specs=[spec] * 3,
        ),
    )(place, grads, weight, first, second)


def unit_tables(owner_row):
    tensor_of = np.array(TENSOR_OF)
    first_unit = np.array(FIRST_UNIT)
    owned_by = owner_row[:8]
    earlier = (owned_by[:, None] == owned_by[None, :]) & jnp.asarray(
        np.arange(8)[None, :] < np.arange(8)[:, None]
    )
    prior = jnp.sum(jnp.where(earlier, jnp.array(TENSOR_SIZE, jnp.int32)[None, :], 0), axis=1)
    unit_owner = owned_by[tensor_of]
    unit_slot = prior[tensor_of] + jnp.asarray(np.arange(UNITS) - first_unit[tensor_of], jnp.int32)
    return unit_owner, unit_slot.astype(jnp.int32)


def slot_units(owner_row, dp, slots):
    unit_owner, unit_slot = unit_tables(owner_row)
    hit = (unit_owner[None, :] == dp) & (unit_slot[None, :] == jnp.arange(slots, dtype=jnp.int32)[:, None])
    return jnp.sum(jnp.where(hit, jnp.arange(UNITS, dtype=jnp.int32)[None, :] + 1, 0), axis=1) - 1


def three_pieces(value):
    high = value.astype(BF)
    rest = value - high.astype(F32)
    mid = rest.astype(BF)
    low = (rest - mid.astype(F32)).astype(BF)
    pad = ((0, PIECE - value.shape[0]), (0, 0))
    parts = jnp.concatenate([jnp.pad(part, pad) for part in (high, mid, low)], axis=0)
    return jnp.pad(parts, ((0, VEC_ROWS - 3 * PIECE), (0, 0)))


def local(n_dp, tokens, cotangent, lengths, owners, master_sq, mom1_sq, mom2_sq, master_vec, mom1_vec, mom2_vec):
    section = lax.axis_index("section")
    dp = lax.axis_index("dp")
    count = lengths.shape[1]
    vec_store = master_vec[0, 0]
    vrows = vec_store.shape[0]
    owns_vector = owners[0, 8] == dp
    pack = three_pieces(jnp.where(owns_vector, vec_store, 0.0))
    own = jnp.where(section == 0, lengths[0], lengths[1])
    info = jnp.concatenate([section[None].astype(jnp.int32), own, lengths[0]])
    weights, vec, linked, *saved = call_start(n_dp, info, owners, tokens[0], master_sq[0, 0], pack, count)
    hidden, dy, dx, late, dsq, late_vec = call_middle(
        info, vec, saved[10], cotangent[0], weights, linked, saved[:10]
    )
    dx, total = call_finish(n_dp, info, dy, weights, vec, late, late_vec, dsq, dx, saved[:10])
    pieces = total[UNITS * D : UNITS * D + 3 * PIECE].astype(F32).reshape(3, PIECE, D)[:, :vrows]
    total_vector = pieces[0] + pieces[1] + pieces[2]
    place = slot_units(owners[0], dp, master_sq.shape[2])
    squares_new = call_adam(place, total, master_sq[0, 0], mom1_sq[0, 0], mom2_sq[0, 0])
    vector_new = adam_update(vec_store, mom1_vec[0, 0], mom2_vec[0, 0], total_vector, vector_rate, 0.0)
    vector_new = [
        jnp.where(owns_vector, new, old)
        for new, old in zip(vector_new, (vec_store, mom1_vec[0, 0], mom2_vec[0, 0]))
    ]
    return (
        hidden[None],
        dx[None],
        *[value[None, None] for value in squares_new],
        *[value[None, None] for value in vector_new],
    )


def solution(mesh):
    n_dp = mesh.shape["dp"]
    slots = P("section", "dp", None, None, None)
    packs = P("section", "dp", None, None)
    rows = P("section", "dp", None)
    return jax.shard_map(
        functools.partial(local, n_dp),
        mesh=mesh,
        in_specs=(rows, rows, P(None, "dp"), P("section", None), slots, slots, slots, packs, packs, packs),
        out_specs=(rows, rows, slots, slots, slots, packs, packs, packs),
        check_vma=False,
    )
```

```python
import functools
import jax
import jax.numpy as jnp
import numpy as np
from jax import lax
from jax.experimental import pallas as pl
from jax.experimental.pallas import tpu as pltpu
from jax.sharding import PartitionSpec as P

D = 512
HEADS = 8
HS = D // HEADS
FF = 2048
RU = FF // D
STEP = 5
LANES = 128
F32 = jnp.float32
BF = jnp.bfloat16
NEG = -1e30


def nn(a, b):
    return jnp.dot(a, b, preferred_element_type=F32)


def nt(a, b):
    return lax.dot_general(a, b, (((1,), (1,)), ((), ())), preferred_element_type=F32)


def tn(a, b):
    return lax.dot_general(a, b, (((0,), (0,)), ((), ())), preferred_element_type=F32)


def lane_loop(count, body):
    def step(i, carry):
        body(pl.ds(pl.multiple_of(i * LANES, LANES), LANES))
        return carry

    lax.fori_loop(0, count // LANES, step, 0, unroll=True)


def norm_parts(value):
    mean = jnp.mean(value, axis=0, keepdims=True)
    centred = value - mean
    inv = lax.rsqrt(jnp.mean(centred * centred, axis=0, keepdims=True) + 1e-05)
    return centred * inv, inv


def norm_grad(grad, normed, inv, gain):
    scaled = grad * gain
    mean_one = jnp.mean(scaled, axis=0, keepdims=True)
    mean_two = jnp.mean(scaled * normed, axis=0, keepdims=True)
    return (scaled - mean_one - normed * mean_two) * inv


def fill_bias(bias, length, causal, key_dim=0):
    rows = bias.shape[0]

    def body(lanes):
        across = lax.broadcasted_iota(jnp.int32, (rows, LANES), 0)
        along = lax.broadcasted_iota(jnp.int32, (rows, LANES), 1) + lanes.start
        key, query = (across, along) if key_dim == 0 else (along, across)
        allowed = key < length
        if causal is not None:
            allowed = allowed & ((key <= query) | jnp.logical_not(causal))
        bias[:, lanes] = jnp.where(allowed, 0.0, NEG)

    lane_loop(bias.shape[1], body)


def head_rows(h):
    return pl.ds(pl.multiple_of(h * HS, HS), HS)


def attend(qt, kt, vt, bias, length, ot, lse, pair):
    width = kt.shape[1]
    index = lax.broadcasted_iota(jnp.int32, (16, width), 0)
    if bias is None:
        masked = (index == 0) & (lax.broadcasted_iota(jnp.int32, index.shape, 1) >= length)
        masks = jnp.where(masked, NEG, 0.0).astype(BF)
        ones = jnp.where(index == 0, 1.0, 0.0).astype(BF)

    def score(h, out):
        rows = head_rows(h)
        keys, queries = kt[rows, :], qt[rows, :] * BF(0.125)
        if bias is None:
            keys = jnp.concatenate([keys, masks], axis=0)
            queries = jnp.concatenate([queries, ones], axis=0)
        out[...] = tn(keys, queries)

    def finish(h, scores):
        rows = head_rows(h)
        biased = scores[...] if bias is None else scores[...] + bias[...]
        top = jnp.max(biased, axis=0, keepdims=True)
        weights = jnp.exp(biased - top).astype(BF)
        values = jnp.concatenate([vt[rows, :], jnp.ones((16, width), BF)], axis=0)
        out = nn(values, weights)
        total = out[HS : HS + 1]
        ot[rows, :] = (out[:HS] * (1.0 / total)).astype(BF)
        lse[pl.ds(h, 1), :] = top + jnp.log(total)

    one, two = pair.at[0], pair.at[1]
    score(0, one)

    def body(i, carry):
        score(2 * i + 1, two)
        finish(2 * i, one)
        score(jnp.minimum(2 * i + 2, HEADS - 1), one)
        finish(2 * i + 1, two)
        return carry

    lax.fori_loop(0, HEADS // 2, body, 0, unroll=True)


def split_rows(row, count):
    high = row.astype(BF)
    rest = row - high.astype(F32)
    mid = rest.astype(BF)
    low = (rest - mid.astype(F32)).astype(BF)
    index = lax.broadcasted_iota(jnp.int32, (16, row.shape[1]), 0)
    parts = jnp.where(index == 0, high, jnp.where(index == 1, mid, low))
    return jnp.where(index < 3, parts, BF(count))


def attend_back(qt, kt, vt, bias, length, ot, lse, dot, dqt, dkt, dvt):
    index = lax.broadcasted_iota(jnp.int32, (16, kt.shape[1]), 0)
    ones = jnp.where(index < 3, 1.0, 0.0).astype(BF)
    masks = ones
    if bias is None:
        masked = (index == 3) & (lax.broadcasted_iota(jnp.int32, index.shape, 1) >= length)
        masks = jnp.where(masked, NEG, ones.astype(F32)).astype(BF)

    def head(h, carry):
        rows = head_rows(h)
        keys, grads = kt[rows, :], dot[rows, :]
        queries = qt[rows, :] * BF(0.125)
        delta = jnp.sum(grads.astype(F32) * ot[rows, :].astype(F32), axis=0, keepdims=True)
        left = jnp.concatenate([queries, split_rows(-lse[pl.ds(h, 1), :], 1)], axis=0)
        scores = tn(left, jnp.concatenate([keys, masks], axis=0))
        probs = jnp.exp(scores if bias is None else scores + bias[...])
        left = jnp.concatenate([grads, split_rows(-delta, 0)], axis=0)
        dscores = (probs * tn(left, jnp.concatenate([vt[rows, :], ones], axis=0))).astype(BF)
        dvt[rows, :] = nn(grads, probs.astype(BF)).astype(BF)
        dkt[rows, :] = nn(queries, dscores).astype(BF)
        dqt[rows, :] = (nt(keys, dscores) * 0.125).astype(BF)
        return carry

    lax.fori_loop(0, HEADS, head, 0, unroll=True)


GAIN, SHIFT, B2, B1 = 0, 3, 6, 7


def column(vec, index):
    return vec[:, index : index + 1]


def self_column(vec, first, row):
    return jnp.where(first, column(vec, row + 1), column(vec, row))


def add_column(dvec, index, acc):
    dvec[:, index : index + 1] += jnp.sum(acc, axis=1, keepdims=True)


def self_forward(x, sq, vec, first, length, ut, n0, r0, qt, kt, vt, ot, lse, n1, r1, y, bias, et, pair, pause):
    tokens = x.shape[0]
    et[...] = x[...].astype(F32).T

    def entry(lanes):
        value = et[:, lanes]
        normed, inv = norm_parts(value)
        n0[:, lanes] = normed.astype(BF)
        r0[:, lanes] = inv
        value = jnp.where(first, normed * column(vec, GAIN) + column(vec, SHIFT), value)
        et[:, lanes] = value
        ut[:, lanes] = value.astype(BF)

    lane_loop(tokens, entry)
    fill_bias(bias, length, jnp.logical_not(first))
    for index, out in enumerate((qt, kt, vt)):
        out[...] = tn(sq[index][...], ut[...]).astype(BF)
    pause()
    attend(qt, kt, vt, bias, length, ot, lse, pair)
    pause()
    et[...] += tn(sq[3][...], ot[...])
    gain, shift = self_column(vec, first, GAIN), self_column(vec, first, SHIFT)

    def leave(lanes):
        normed, inv = norm_parts(et[:, lanes])
        n1[:, lanes] = normed.astype(BF)
        r1[:, lanes] = inv
        y[:, lanes] = normed * gain + shift

    lane_loop(tokens, leave)


def self_backward(
    dy, sq, vec, first, length, ut, n0, r0, qt, kt, vt, ot, lse, n1, r1, dx,
    bias, dsa, dot, dqt, dkt, dvt, dsq, dvec, vacc, pause,
):
    tokens = dy.shape[1]
    vacc[...] = jnp.zeros(vacc.shape, F32)
    gain = self_column(vec, first, GAIN)

    def leave(lanes):
        grad, normed = dy[:, lanes], n1[:, lanes].astype(F32)
        vacc[2] += grad * normed
        vacc[3] += grad
        grad = norm_grad(grad, normed, r1[:, lanes], gain)
        dy[:, lanes] = grad
        dsa[:, lanes] = grad.astype(BF)

    lane_loop(tokens, leave)
    fill_bias(bias, length, jnp.logical_not(first), 1)
    dot[...] = nn(sq[3][...], dsa[...]).astype(BF)
    dsq[3] += nt(ot[...], dsa[...])
    pause()
    attend_back(qt, kt, vt, bias, length, ot, lse, dot, dqt, dkt, dvt)
    for index, grad in enumerate((dqt, dkt, dvt)):
        dsq[index] += nt(ut[...], grad[...])
        dy[...] += nn(sq[index][...], grad[...])
    pause()
    entry_gain = column(vec, GAIN)

    def entry(lanes):
        grad, normed = dy[:, lanes], n0[:, lanes].astype(F32)
        vacc[0] += grad * normed
        vacc[1] += grad
        dy[:, lanes] = jnp.where(first, norm_grad(grad, normed, r0[:, lanes], entry_gain), grad)

    lane_loop(tokens, entry)
    dx[...] = dy[...].T

    @pl.when(first)
    def _():
        add_column(dvec, GAIN, vacc[0])
        add_column(dvec, SHIFT, vacc[1])
        add_column(dvec, GAIN + 1, vacc[2])
        add_column(dvec, SHIFT + 1, vacc[3])

    @pl.when(jnp.logical_not(first))
    def _():
        add_column(dvec, GAIN, vacc[2])
        add_column(dvec, SHIFT, vacc[3])


def gelu_parts(z):
    root = 0.7978845608028654
    square = z * z
    t = jnp.tanh(z * (root + (root * 0.044715) * square))
    half = 0.5 + 0.5 * t
    act = z * half
    slope = half + act * (1.0 - t) * (root + (3.0 * root * 0.044715) * square)
    return act, slope


def feed_forward(h, units, vec, hb, act, slope, n2, r2, out):
    hb[...] = h[...].astype(BF)
    for c in range(RU):
        rows = slice(c * D, (c + 1) * D)
        a, s = gelu_parts(tn(units[c][...], hb[...]) + column(vec, B1 + c))
        act[rows, :] = a.astype(BF)
        slope[rows, :] = s.astype(BF)
    for c in range(RU):
        rows = slice(c * D, (c + 1) * D)
        h[...] += tn(units[RU + c][...], act[rows, :])

    def leave(lanes):
        normed, inv = norm_parts(h[:, lanes] + column(vec, B2))
        n2[:, lanes] = normed.astype(BF)
        r2[:, lanes] = inv
        out[:, lanes] = normed * column(vec, GAIN + 2) + column(vec, SHIFT + 2)

    lane_loop(h.shape[1], leave)


def feed_backward(dm, units, vec, hb, act, slope, n2, r2, dfb, dz, dunits, dvec, vacc):
    vacc[...] = jnp.zeros(vacc.shape, F32)

    def leave(lanes):
        grad, normed = dm[:, lanes], n2[:, lanes].astype(F32)
        vacc[RU + 1] += grad * normed
        vacc[RU + 2] += grad
        grad = norm_grad(grad, normed, r2[:, lanes], column(vec, GAIN + 2))
        dm[:, lanes] = grad
        short = grad.astype(BF)
        vacc[RU] += short.astype(F32)
        dfb[:, lanes] = short

    lane_loop(dm.shape[1], leave)
    for c in range(RU):
        rows = slice(c * D, (c + 1) * D)
        dz[rows, :] = (nn(units[RU + c][...], dfb[...]) * slope[rows, :].astype(F32)).astype(BF)
        dunits[RU + c][...] += nt(act[rows, :], dfb[...])
    for c in range(RU):
        rows = slice(c * D, (c + 1) * D)
        dm[...] += nn(units[c][...], dz[rows, :])
        dunits[c][...] += nt(hb[...], dz[rows, :])
        for lanes in range(0, dm.shape[1], LANES):
            vacc[c] += dz[rows, lanes : lanes + LANES].astype(F32)
    for index in range(RU):
        add_column(dvec, B1 + index, vacc[index])
    add_column(dvec, B2, vacc[RU])
    add_column(dvec, GAIN + 2, vacc[RU + 1])
    add_column(dvec, SHIFT + 2, vacc[RU + 2])


def cross_forward(a, sq, vec, length, ab, cqt, kt, vt, ot, lse, n1, r1, pair):
    ab[...] = a[...].astype(BF)
    cqt[...] = tn(sq[0][...], ab[...]).astype(BF)
    attend(cqt, kt, vt, None, length, ot, lse, pair)
    a[...] += tn(sq[1][...], ot[...])

    def leave(lanes):
        normed, inv = norm_parts(a[:, lanes])
        n1[:, lanes] = normed.astype(BF)
        r1[:, lanes] = inv
        a[:, lanes] = normed * column(vec, GAIN + 1) + column(vec, SHIFT + 1)

    lane_loop(a.shape[1], leave)


def cross_backward(
    dbq, sq, vec, length, ab, cqt, kt, vt, ot, lse, n1, r1, dca, dot, dqt, dkt, dvt, dsq, dvec, vacc, ready
):
    vacc[0] = jnp.zeros(vacc.shape[1:], F32)
    vacc[1] = jnp.zeros(vacc.shape[1:], F32)

    def leave(lanes):
        grad, normed = dbq[:, lanes], n1[:, lanes].astype(F32)
        vacc[0] += grad * normed
        vacc[1] += grad
        grad = norm_grad(grad, normed, r1[:, lanes], column(vec, GAIN + 1))
        dbq[:, lanes] = grad
        dca[:, lanes] = grad.astype(BF)

    lane_loop(dbq.shape[1], leave)
    dot[...] = nn(sq[1][...], dca[...]).astype(BF)
    dsq[1][...] += nt(ot[...], dca[...])
    attend_back(cqt, kt, vt, None, length, ot, lse, dot, dqt, dkt, dvt)
    ready()
    dsq[0][...] += nt(ab[...], dqt[...])
    dbq[...] += nn(sq[0][...], dqt[...])
    add_column(dvec, GAIN + 1, vacc[0])
    add_column(dvec, SHIFT + 1, vacc[1])


SUB = 256
HOP = 3
HALF = SUB // 2
QUART = SUB // 4
UNITS = 6 + 2 * RU
VEC_ROWS = 256
SUBS = (UNITS * D + VEC_ROWS) // SUB
MESH = pl.DeviceIdType.MESH


class Total:
    def __init__(self, n_dp, order, shorts, other, mine, out, core_in, half, x_in, right_in, left_in, passed, sems):
        self.length = n_dp // 4
        self.last = self.length - 1
        self.section = lax.axis_index("section")
        self.dp = lax.axis_index("dp")
        self.core, self.x, self.z = self.dp % 2, (self.dp // 2) % 2, self.dp // 4
        self.sibling, self.beside = self.dp + 1 - 2 * self.core, self.dp + 2 - 4 * self.x
        self.has_left, self.has_right = self.z > 0, self.z < self.last
        self.order, self.shorts, self.other, self.mine = order, shorts, other, mine
        self.out, self.core_in, self.half, self.x_in = out, core_in, half, x_in
        self.right_in, self.left_in, self.passed, self.sems = right_in, left_in, passed, sems
        far = self.last
        self.ticks = SUBS + HOP * (2 + far + far) + 1

    def greet(self, across=False):
        barrier = pltpu.get_barrier_semaphore()

        def signal(index):
            pl.semaphore_signal(barrier, inc=1, device_id=(self.section, index), device_id_type=MESH)

        signal(self.sibling)
        signal(self.beside)
        pl.when(self.has_left)(lambda: signal(self.dp - 4))
        pl.when(self.has_right)(lambda: signal(self.dp + 4))
        if across:
            pl.semaphore_signal(barrier, inc=1, device_id=(1 - self.section, self.dp), device_id_type=MESH)
        sides = self.has_left.astype(jnp.int32) + self.has_right.astype(jnp.int32)
        pl.semaphore_wait(barrier, 2 + int(across) + sides)

    def short_route(self, t):
        return ((t & 1) == 0) | ((t >= self.shorts[0]) & (t < self.shorts[1]))

    def home(self, t):
        return (t >> 1) & self.last

    def place(self, t, start, size):
        return pl.ds(pl.multiple_of(self.order(t) * SUB + start, QUART), size)

    def send(self, step, t, source, target, index):
        return pltpu.make_async_remote_copy(
            src_ref=source,
            dst_ref=target,
            send_sem=self.sems.at[0, step, t],
            recv_sem=self.sems.at[1, step, t],
            device_id=(self.section, index),
            device_id_type=MESH,
        )

    def part(self, size, index):
        return pl.ds(pl.multiple_of(index * size, size), size)

    def copy_core(self, t):
        source = self.other(t, self.order(t), HALF * (1 - self.core))
        return self.send(0, t, source, self.core_in.at[t], self.sibling)

    def copy_x(self, t):
        rows = self.part(QUART, 1 - self.x)
        return self.send(1, t, self.half.at[t, rows], self.x_in.at[t, pl.ds(0, QUART)], self.beside)

    def copy_x_whole(self, t):
        return self.send(1, t, self.passed.at[t], self.x_in.at[t], self.beside)

    def copy_right(self, t, source):
        return self.send(2, t, source, self.right_in.at[t, pl.ds(0, QUART)], self.dp + 4)

    def copy_left(self, t, source):
        return self.send(3, t, source, self.left_in.at[t, pl.ds(0, QUART)], self.dp - 4)

    def copy_right_whole(self, t, source):
        return self.send(2, t, source, self.right_in.at[t], self.dp + 4)

    def copy_left_whole(self, t, source):
        return self.send(3, t, source, self.left_in.at[t], self.dp - 4)

    def copy_back_x(self, t):
        place = self.place(t, HALF * self.core + QUART * self.x, QUART)
        return self.send(4, t, self.out.at[place], self.out.at[place], self.beside)

    def copy_back_core(self, t):
        place = self.place(t, HALF * self.core, HALF)
        return self.send(5, t, self.out.at[place], self.out.at[place], self.sibling)

    def copy_back_right(self, t):
        place = self.place(t, HALF * self.core, HALF)
        return self.send(4, t, self.out.at[place], self.out.at[place], self.dp + 4)

    def copy_back_left(self, t):
        place = self.place(t, HALF * self.core, HALF)
        return self.send(6, t, self.out.at[place], self.out.at[place], self.dp - 4)

    def add(self, one, two):
        return one + two

    def own_quarter(self, t):
        return self.half.at[t, self.part(QUART, self.x)]

    def short_core(self, t):
        self.copy_core(t).wait_recv()
        self.half[t] = self.add(self.mine(t, self.order(t), HALF * self.core), self.core_in[t])
        self.copy_x(t).start()

    def short_x(self, t):
        self.copy_x(t).wait_recv()
        quart = self.own_quarter(t)
        quart[...] = self.add(quart[...], self.x_in[t, 0:QUART])

        @pl.when(jnp.logical_not(self.has_left) & self.has_right)
        def _():
            self.copy_right(t, quart).start()

        @pl.when(jnp.logical_not(self.has_right) & self.has_left)
        def _():
            self.copy_left(t, quart).start()

    def short_right(self, t):
        @pl.when(self.has_left)
        def _():
            target = self.passed.at[t, pl.ds(0, QUART)]
            self.copy_right(t, target).wait_recv()

            @pl.when(self.has_right)
            def _():
                target[...] = self.add(self.own_quarter(t)[...], self.right_in[t, 0:QUART])
                self.copy_right(t, target).start()

    def short_left(self, t):
        @pl.when(self.has_right)
        def _():
            target = self.passed.at[t, pl.ds(QUART, QUART)]
            self.copy_left(t, target).wait_recv()

            @pl.when(self.has_left)
            def _():
                target[...] = self.add(self.own_quarter(t)[...], self.left_in[t, 0:QUART])
                self.copy_left(t, target).start()

    def short_total(self, t):
        total = self.own_quarter(t)[...].astype(F32)
        total += jnp.where(self.has_left, self.right_in[t, 0:QUART].astype(F32), 0.0)
        total += jnp.where(self.has_right, self.left_in[t, 0:QUART].astype(F32), 0.0)
        self.out[self.place(t, HALF * self.core + QUART * self.x, QUART), :] = total.astype(BF)
        self.copy_back_x(t).start()

    def short_back(self, t):
        self.copy_back_x(t).wait_recv()
        self.copy_back_core(t).start()

    def long_core(self, t):
        self.copy_core(t).wait_recv()
        self.half[t] = self.add(self.mine(t, self.order(t), HALF * self.core), self.core_in[t])
        home = self.home(t)

        @pl.when(jnp.logical_not(self.has_left) & (home > 0))
        def _():
            self.copy_right_whole(t, self.half.at[t]).start()

        @pl.when(jnp.logical_not(self.has_right) & (home < self.last))
        def _():
            self.copy_left_whole(t, self.half.at[t]).start()

    def long_right(self, t):
        @pl.when(self.has_left & (self.z < self.home(t)))
        def _():
            self.copy_right_whole(t, self.passed.at[t]).wait_recv()
            self.passed[t] = self.add(self.half[t], self.right_in[t])
            self.copy_right_whole(t, self.passed.at[t]).start()

    def long_left(self, t):
        @pl.when(self.has_right & (self.z > self.home(t)))
        def _():
            self.copy_left_whole(t, self.passed.at[t]).wait_recv()
            self.passed[t] = self.add(self.half[t], self.left_in[t])
            self.copy_left_whole(t, self.passed.at[t]).start()

    def long_home(self, t):
        @pl.when(self.z == self.home(t))
        def _():
            pl.when(self.has_left)(lambda: self.copy_right_whole(t, self.half.at[t]).wait_recv())
            pl.when(self.has_right)(lambda: self.copy_left_whole(t, self.half.at[t]).wait_recv())
            total = self.half[t].astype(F32)
            total += jnp.where(self.has_left, self.right_in[t].astype(F32), 0.0)
            total += jnp.where(self.has_right, self.left_in[t].astype(F32), 0.0)
            self.passed[t] = total.astype(BF)
            self.copy_x_whole(t).start()

    def long_x(self, t):
        @pl.when(self.z == self.home(t))
        def _():
            self.copy_x_whole(t).wait_recv()
            self.out[self.place(t, HALF * self.core, HALF), :] = self.add(self.passed[t], self.x_in[t])
            pl.when(self.has_left)(lambda: self.copy_back_left(t).start())
            pl.when(self.has_right)(lambda: self.copy_back_right(t).start())
            self.copy_back_core(t).start()

    def long_back(self, t):
        home = self.home(t)

        @pl.when(self.z > home)
        def _():
            self.copy_back_right(t).wait_recv()
            pl.when(self.has_right)(lambda: self.copy_back_right(t).start())

        @pl.when(self.z < home)
        def _():
            self.copy_back_left(t).wait_recv()
            pl.when(self.has_left)(lambda: self.copy_back_left(t).start())

        pl.when(self.z != home)(lambda: self.copy_back_core(t).start())

    def tick(self, now, prepare):
        z, last = self.z, self.last
        far = jnp.maximum(z, last - z)
        prepared = now

        @pl.when(prepared < SUBS)
        def _():
            prepare(prepared)
            self.copy_core(prepared).start()

        def due(step, lag, short):
            t = now - HOP * lag
            fits = (t >= 0) & (t < SUBS)
            kind = self.short_route(t) if short else jnp.logical_not(self.short_route(t))
            pl.when(fits & kind)(lambda: step(t))

        due(self.short_core, 1, True)
        due(self.short_x, 2, True)
        due(self.short_right, 2 + z, True)
        due(self.short_left, 2 + last - z, True)
        due(self.short_total, 2 + far, True)
        due(self.short_back, 3 + far, True)
        due(self.long_core, 1, False)
        due(self.long_right, 1 + z, False)
        due(self.long_left, 1 + last - z, False)
        due(self.long_home, 1 + far, False)
        due(self.long_x, 2 + far, False)
        for home in range(self.length):
            lag = 2 + max(home, last - home) + jnp.abs(z - home)
            t = now - HOP * lag
            fits = (t >= 0) & (t < SUBS) & jnp.logical_not(self.short_route(t)) & (self.home(t) == home)
            pl.when(fits & (z != home))(lambda t=t: self.long_back(t))

    def arrive(self, t):
        self.copy_back_core(t).wait_recv()

    def settle(self, t):
        self.copy_core(t).wait_send()
        self.copy_back_core(t).wait_send()
        home = self.home(t)

        @pl.when(self.short_route(t))
        def _():
            self.copy_x(t).wait_send()
            pl.when(self.has_right)(lambda: self.copy_right(t, self.own_quarter(t)).wait_send())
            pl.when(self.has_left)(lambda: self.copy_left(t, self.own_quarter(t)).wait_send())
            self.copy_back_x(t).wait_send()

        @pl.when(jnp.logical_not(self.short_route(t)))
        def _():
            pl.when(self.z < home)(lambda: self.copy_right_whole(t, self.half.at[t]).wait_send())
            pl.when(self.z > home)(lambda: self.copy_left_whole(t, self.half.at[t]).wait_send())
            pl.when(self.z == home)(lambda: self.copy_x_whole(t).wait_send())
            pl.when(self.has_right & (self.z >= home))(lambda: self.copy_back_right(t).wait_send())
            pl.when(self.has_left & (self.z <= home))(lambda: self.copy_back_left(t).wait_send())


def loop(start, stop, body):
    def step(i, carry):
        body(i)
        return carry

    lax.fori_loop(start, stop, step, 0)


def total_scratch():
    return [pltpu.VMEM((SUBS, HALF, D), BF)] * 6 + [pltpu.SemaphoreType.DMA((2, 7, SUBS))]


def any_space():
    return pl.BlockSpec(memory_space=pl.ANY)


def vmem_space():
    return pl.BlockSpec(memory_space=pltpu.VMEM)


def smem_space():
    return pl.BlockSpec(memory_space=pltpu.SMEM)


def block_spec(*dims):
    return pl.BlockSpec((1,) + dims, lambda b, info: (b,) + (0,) * len(dims))


def shape32(*dims):
    return jax.ShapeDtypeStruct(dims, F32)


def shape16(*dims):
    return jax.ShapeDtypeStruct(dims, BF)


TENSOR_OF = (0, 1, 2, 3, 4, 5) + (6,) * RU + (7,) * RU
TENSOR_SIZE = (1,) * 6 + (RU, RU)
FIRST_UNIT = (0, 1, 2, 3, 4, 5, 6, 6 + RU)
VEC_BLOCKS = VEC_ROWS // SUB
EARLY = 4 * D // SUB + VEC_BLOCKS
LINKED = 6 * D // SUB + VEC_BLOCKS
PIECE = 16


def copies(sources, targets, sems):
    return [pltpu.make_async_copy(s, t, sems.at[i]) for i, (s, t) in enumerate(zip(sources, targets))]


def slot_of(owners, tensor):
    prior = jnp.int32(0)
    for earlier in range(tensor):
        prior += jnp.where(owners[0, earlier] == owners[0, tensor], TENSOR_SIZE[earlier], 0)
    return prior


def start_kernel(n_dp, info, owners, x, slots, pack, out, vec, linked, *refs):
    saved_out, (y_out, stage, *comm), refs = refs[:10], refs[10:19], refs[19:]
    saved, (y, xb, bias, et, pair, places, counter, sems, link_sems) = refs[:10], refs[10:]
    count, tokens = saved_out[0].shape[0], saved_out[0].shape[2]
    first = lax.axis_index("section") == 0
    dp = lax.axis_index("dp")
    for unit in range(UNITS):
        tensor = TENSOR_OF[unit]
        slot = jnp.minimum(slot_of(owners, tensor) + (unit - FIRST_UNIT[tensor]), slots.shape[0] - 1)
        places[0, unit] = slot
        places[1, unit] = (owners[0, tensor] == dp).astype(jnp.int32)

    def own(block, start):
        is_pack = block >= SUBS - VEC_BLOCKS
        unit = jnp.minimum(block * SUB // D, UNITS - 1)
        at = pl.multiple_of((block * SUB) % D + start, HALF)
        value = jnp.where(places[1, unit] == 1, slots[places[0, unit], pl.ds(at, HALF), :], 0.0).astype(BF)
        return jnp.where(is_pack, pack[pl.ds(pl.multiple_of(start, HALF), HALF), :], value)

    def order(t):
        return jnp.where(t < VEC_BLOCKS, t + SUBS - VEC_BLOCKS, t - VEC_BLOCKS)

    total = Total(
        n_dp,
        order,
        (0, LINKED),
        lambda t, block, start: stage.at[t],
        lambda t, block, start: own(block, start),
        out,
        *comm,
    )

    def prepare(t):
        stage[t] = own(order(t), HALF * (1 - total.core))

    def run(ticks):
        begin = counter[0]
        stop = jnp.minimum(begin + ticks, total.ticks)
        loop(begin, stop, lambda now: total.tick(now, prepare))
        counter[0] = stop

    link = pltpu.make_async_remote_copy(
        src_ref=out.at[pl.ds(4 * D, 2 * D)],
        dst_ref=linked,
        send_sem=link_sems.at[0],
        recv_sem=link_sems.at[1],
        device_id=(1 - total.section, dp),
        device_id_type=MESH,
    )
    total.greet(across=True)
    counter[0] = 0
    run(EARLY + HOP * (3 + total.last))
    loop(0, EARLY, total.arrive)
    rows = [out[pl.ds(UNITS * D + i * PIECE, PIECE), :].astype(F32) for i in range(3)]
    whole = jnp.concatenate([rows[0] + rows[1] + rows[2], jnp.zeros((LANES - PIECE, D), F32)], axis=0)
    vec[...] = whole.T
    squares = [out.at[pl.ds(i * D, D)] for i in range(4)]

    def outward(b):
        return copies(saved + (y,), [ref.at[b] for ref in saved_out + (y_out,)], sems)

    def block(b):
        @pl.when(b == 1)
        def _():
            run(jnp.maximum(LINKED + HOP * (3 + total.last) - counter[0], 0))
            loop(EARLY, LINKED, total.arrive)
            pl.when(first)(lambda: link.start())

        load = pltpu.make_async_copy(x.at[pl.ds(pl.multiple_of(b * tokens, tokens), tokens)], xb, sems.at[11])
        load.start()

        @pl.when(b > 0)
        def _():
            for copy in outward(b - 1):
                copy.wait()

        load.wait()
        self_forward(
            xb, squares, vec, first, info[1 + b], *saved, y, bias, et, pair, lambda: run(2)
        )
        for copy in outward(b):
            copy.start()
        run(1)

    loop(0, count, block)
    run(total.ticks)
    for copy in outward(count - 1):
        copy.wait()
    loop(LINKED, SUBS, total.arrive)
    loop(0, SUBS, total.settle)
    pl.when(first)(lambda: link.wait_send())
    pl.when(jnp.logical_not(first))(lambda: link.wait_recv())


def saved_dims(tokens):
    wide, row = ((D, tokens), BF), ((1, tokens), F32)
    return [wide, wide, row, wide, wide, wide, wide, ((HEADS, tokens), F32), wide, row]


def call_start(n_dp, info, owners, x, slots, pack, count):
    tokens = x.shape[0] // count
    kept = saved_dims(tokens)
    scores = pltpu.VMEM((tokens, tokens), F32)
    return pl.pallas_call(
        functools.partial(start_kernel, n_dp),
        name="start",
        out_shape=[shape16(SUBS * SUB, D), shape32(D, LANES), shape16(2 * D, D)]
        + [jax.ShapeDtypeStruct((count,) + dims, kind) for dims, kind in kept]
        + [shape32(count, D, tokens)],
        in_specs=[smem_space(), smem_space(), any_space(), vmem_space(), vmem_space()],
        out_specs=[vmem_space()] * 3 + [any_space()] * 11,
        scratch_shapes=[pltpu.VMEM((SUBS, HALF, D), BF)]
        + total_scratch()
        + [pltpu.VMEM(dims, kind) for dims, kind in kept]
        + [
            pltpu.VMEM((D, tokens), F32),
            pltpu.VMEM((tokens, D), BF),
            scores,
            pltpu.VMEM((D, tokens), F32),
            pltpu.VMEM((2, tokens, tokens), F32),
            pltpu.SMEM((2, UNITS), jnp.int32),
            pltpu.SMEM((1,), jnp.int32),
            pltpu.SemaphoreType.DMA((12,)),
            pltpu.SemaphoreType.DMA((2,)),
        ],
        compiler_params=pltpu.CompilerParams(
            collective_id=0, has_side_effects=True, vmem_limit_bytes=60 * 2**20
        ),
    )(info, owners, x, slots, pack)


def finish_kernel(n_dp, info, dy, sq, vec, late_in, late_vec, dsq_in, dx_in, *refs):
    saved_in, (dx_out, out), (late, stage, *comm), refs = refs[:10], refs[10:12], refs[12:21], refs[21:]
    saved, (dys, dx, bias, dsa, dot, dqt, dkt, dvt, dsq, dvec, vacc, pack, counter, sems, link_sems) = refs[:10], refs[10:]
    count, tokens = dy.shape[0], dy.shape[2]
    first = lax.axis_index("section") == 0
    early = EARLY - VEC_BLOCKS
    others = SUBS - EARLY

    mixed = 2 * D // SUB
    plain = others - mixed

    def order(t):
        block = jnp.where(t < plain, t + early + mixed, t - plain + early)
        return jnp.where(t < others, block, jnp.where(t < SUBS - VEC_BLOCKS, t - others, t))

    def own_early(block, start):
        unit = jnp.minimum(block * SUB // D, 3)
        at = pl.multiple_of((block * SUB) % D + start, HALF)
        value = dsq[unit, pl.ds(at, HALF), :].astype(BF)
        return jnp.where(block >= SUBS - VEC_BLOCKS, pack[pl.ds(pl.multiple_of(start, HALF), HALF), :], value)

    def own_late(block, start):
        return late[pl.ds(pl.multiple_of((block - early) * SUB + start, HALF), HALF), :]

    def mine(t, block, start):
        return lax.cond(t < others, lambda: own_late(block, start), lambda: own_early(block, start))

    total = Total(
        n_dp, order, (others, SUBS), lambda t, block, start: stage.at[t], mine, out, *comm
    )

    def prepare(t):
        pl.when((t == plain) & first)(lambda: link.wait_recv())
        stage[t] = mine(t, order(t), HALF * (1 - total.core))

    def run(ticks, end):
        begin = counter[0]
        stop = jnp.minimum(begin + ticks, end)
        loop(begin, stop, lambda now: total.tick(now, prepare))
        counter[0] = stop

    link = pltpu.make_async_remote_copy(
        src_ref=late_in.at[pl.ds(10 * D, 2 * D)],
        dst_ref=late.at[pl.ds(0, 2 * D)],
        send_sem=link_sems.at[0],
        recv_sem=link_sems.at[1],
        device_id=(1 - total.section, total.dp),
        device_id_type=MESH,
    )
    counter[0] = 0
    load_dsq = pltpu.make_async_copy(dsq_in, dsq, sems.at[12])
    load_dsq.start()
    load_late = pltpu.make_async_copy(late_in.at[pl.ds(2 * D, 8 * D)], late.at[pl.ds(2 * D, 8 * D)], sems.at[13])
    load_mixed = pltpu.make_async_copy(late_in.at[pl.ds(0, 2 * D)], late.at[pl.ds(0, 2 * D)], sems.at[14])
    load_late.start()
    pl.when(jnp.logical_not(first))(lambda: load_mixed.start())
    dvec[...] = late_vec[...]
    total.greet(across=True)
    pl.when(jnp.logical_not(first))(lambda: link.start())
    load_dsq.wait()
    load_late.wait()
    pl.when(jnp.logical_not(first))(lambda: load_mixed.wait())
    begin = count // 2
    squares = [sq.at[pl.ds(i * D, D)] for i in range(4)]

    def block(b):
        loads = copies([ref.at[b] for ref in saved_in] + [dy.at[b]], saved + (dys,), sems)
        for copy in loads:
            copy.start()
        run(4, others)

        def store(b):
            return pltpu.make_async_copy(
                dx, dx_out.at[pl.ds(pl.multiple_of(b * tokens, tokens), tokens)], sems.at[11]
            )

        pl.when(b > begin)(lambda: store(b - 1).wait())
        for copy in loads:
            copy.wait()
        self_backward(
            dys, squares, vec, first, info[1 + b], *saved, dx,
            bias, dsa, dot, dqt, dkt, dvt, dsq, dvec, vacc, lambda: run(3, others),
        )
        store(b).start()
        pl.when(b == count - 1)(lambda: store(b).wait())

    loop(begin, count, block)
    value = dvec[...].T[:PIECE]
    high = value.astype(BF)
    rest = value - high.astype(F32)
    mid = rest.astype(BF)
    pack[...] = jnp.zeros(pack.shape, BF)
    pack[0:PIECE, :] = high
    pack[PIECE : 2 * PIECE, :] = mid
    pack[2 * PIECE : 3 * PIECE, :] = (rest - mid.astype(F32)).astype(BF)
    run(total.ticks, total.ticks)
    loop(0, SUBS, total.arrive)
    loop(0, SUBS, total.settle)
    pl.when(jnp.logical_not(first))(lambda: link.wait_send())


def call_finish(n_dp, info, dy, weights, vec, late, late_vec, dsq, dx, saved):
    count, tokens = dy.shape[0], dy.shape[2]
    kept = saved_dims(tokens)
    wide16 = pltpu.VMEM((D, tokens), BF)
    wide32 = pltpu.VMEM((D, tokens), F32)
    return pl.pallas_call(
        functools.partial(finish_kernel, n_dp),
        name="finish",
        out_shape=[shape32(count * tokens, D), shape16(SUBS * SUB, D)],
        grid=(1,),
        in_specs=[
            smem_space(),
            any_space(),
            pl.BlockSpec((4 * D, D), lambda i: (0, 0)),
            vmem_space(),
            any_space(),
            vmem_space(),
        ]
        + [any_space()] * 12,
        out_specs=[any_space(), vmem_space()],
        input_output_aliases={7: 0},
        scratch_shapes=[pltpu.VMEM((10 * D, D), BF), pltpu.VMEM((SUBS, HALF, D), BF)]
        + total_scratch()
        + [pltpu.VMEM(dims, kind) for dims, kind in kept]
        + [wide32, pltpu.VMEM((tokens, D), F32), pltpu.VMEM((tokens, tokens), F32)]
        + [wide16] * 5
        + [
            pltpu.VMEM((4, D, D), F32),
            pltpu.VMEM((D, LANES), F32),
            pltpu.VMEM((4, D, LANES), F32),
            pltpu.VMEM((VEC_ROWS, D), BF),
            pltpu.SMEM((1,), jnp.int32),
            pltpu.SemaphoreType.DMA((15,)),
            pltpu.SemaphoreType.DMA((2,)),
        ],
        compiler_params=pltpu.CompilerParams(
            collective_id=2, has_side_effects=True, vmem_limit_bytes=60 * 2**20
        ),
    )(info, dy, weights, vec, late, late_vec, dsq, dx, *saved)


def middle_kernel(info, vec, y, cot, weights, linked, *refs):
    saved_in, outs, refs = refs[:10], refs[10:16], refs[16:]
    hidden, dy, dx_out, grads, dsq_out, dvec = outs
    saved, refs = refs[:10], refs[10:]
    ut, n0, r0, qt, kt, vt, ot, lse, n1, r1 = saved
    (
        wts, acc, dsq, sent, got, hbuf, mem, hb, act, slope, n2, r2, dfb, dz, vacc,
        bias, dca, dot, dqt, dkt, dvt, pair, cotb, tok, dx, link, swaps, sems, saved_sems, grad_sems,
    ) = refs
    section = lax.axis_index("section")
    first = section == 0
    dp = lax.axis_index("dp")
    count, tokens = y.shape[0], y.shape[2]
    other = 1 - section
    barrier = pltpu.get_barrier_semaphore()
    pl.semaphore_signal(barrier, inc=1, device_id=(other, dp), device_id_type=MESH)
    pl.semaphore_wait(barrier, 1)

    def remote(source, target, step, b):
        return pltpu.make_async_remote_copy(
            src_ref=source,
            dst_ref=target,
            send_sem=swaps.at[step, b],
            recv_sem=swaps.at[step + 1, b],
            device_id=(other, dp),
            device_id_type=MESH,
        )

    def send_memory(b):
        return remote(sent.at[b], got.at[b], 0, b)

    def send_back(b):
        return remote(sent.at[b], got.at[b], 2, b)

    def rows(b):
        return pl.ds(pl.multiple_of(b * tokens, tokens), tokens)

    def load_y(b):
        return pltpu.make_async_copy(y.at[b], hbuf.at[b % 2], sems.at[0])

    def load_cot(b):
        return pltpu.make_async_copy(cot.at[rows(b)], cotb, sems.at[1])

    def store_hidden(b):
        return pltpu.make_async_copy(tok, hidden.at[rows(b)], sems.at[2])

    def store_dy(b):
        return pltpu.make_async_copy(hbuf.at[b % 2], dy.at[b], sems.at[3])

    def load_dy(b):
        return pltpu.make_async_copy(dy.at[b], hbuf.at[b % 2], sems.at[0])

    def store_dx(b):
        return pltpu.make_async_copy(dx, dx_out.at[rows(b)], sems.at[4])

    def load_saved(b):
        return copies([ref.at[b] for ref in saved_in], saved, saved_sems)

    unit = [wts.at[pl.ds(i * D, D)] for i in range(UNITS)]
    part = 6 * D
    load_rest = pltpu.make_async_copy(
        weights.at[pl.ds(part, UNITS * D - part)], wts.at[pl.ds(part, UNITS * D - part)], sems.at[5]
    )
    load_squares = pltpu.make_async_copy(weights.at[pl.ds(0, part)], wts.at[pl.ds(0, part)], sems.at[6])
    load_link = pltpu.make_async_copy(linked, link, sems.at[7])
    load_y(0).start()
    load_rest.start()
    pl.when(jnp.logical_not(first))(lambda: load_link.start())
    load_squares.start()
    s4, s5, ffn = unit[4], unit[5], unit[6:]
    cross_acc = [acc.at[i] for i in range(2)]
    link_acc = acc.at[pl.ds(10, 2)]
    ffn_acc = [acc.at[2 + i] for i in range(2 * RU)]

    out_dsq = pltpu.make_async_copy(dsq, dsq_out, sems.at[6])

    def clear():
        acc[...] = jnp.zeros(acc.shape, F32)
        dsq[...] = jnp.zeros(dsq.shape, F32)
        dvec[...] = jnp.zeros(dvec.shape, F32)

    def run_feed_forward(h):
        feed_forward(h, ffn, vec, hb, act, slope, n2, r2, mem)

    def emit_hidden(b):
        pl.when(b > 0)(lambda: store_hidden(b - 1).wait())
        tok[...] = mem[...].T.astype(BF)
        store_hidden(b).start()

    def take_cotangent(b, h):
        load_cot(b).wait()
        token = lax.broadcasted_iota(jnp.int32, (D, tokens), 1)
        h[...] = jnp.where(token < info[1 + b], cotb[...].astype(F32).T, 0.0)

    def run_feed_backward(h):
        feed_backward(h, ffn, vec, hb, act, slope, n2, r2, dfb, dz, ffn_acc, dvec, vacc)

    def run_self_backward(b, h):
        pl.when(b > 0)(lambda: store_dx(b - 1).wait())
        self_backward(
            h, unit[:4], vec, first, info[1 + b], *saved, dx,
            bias, dca, dot, dqt, dkt, dvt, dsq, dvec, vacc.at[pl.ds(0, 4)], lambda: None,
        )
        store_dx(b).start()

    @pl.when(first)
    def _():
        load_rest.wait()

        def ahead(b):
            h = hbuf.at[b % 2]
            load_y(b).wait()
            pl.when(b + 1 < count)(lambda: load_y(b + 1).start())
            run_feed_forward(h)
            sent[b] = mem[...].astype(BF)
            send_memory(b).start()
            emit_hidden(b)

        loop(0, count, ahead)
        store_hidden(count - 1).wait()
        load_squares.wait()
        clear()
        load_y(0).start()

        def back(b):
            h = hbuf.at[b % 2]
            loads = load_saved(b)
            load_cot(b).start()
            load_y(b).wait()
            pl.when(b < count // 2)(lambda: [copy.start() for copy in loads] and None)
            run_feed_forward(h)
            take_cotangent(b, h)
            send_back(b).wait_recv()
            h[...] += got[b].astype(F32)
            run_feed_backward(h)

            @pl.when(b < count // 2)
            def _():
                load_y(b + 1).start()
                for copy in loads:
                    copy.wait()
                run_self_backward(b, h)
                pl.when(b == count // 2 - 1)(lambda: out_dsq.start())

            @pl.when(b >= count // 2)
            def _():
                store_dy(b).start()

                @pl.when(b + 1 < count)
                def _():
                    load_y(b + 1).start()
                    store_dy(b).wait()

        loop(0, count, back)
        store_dy(count - 1).wait()
        store_dx(count // 2 - 1).wait()

    @pl.when(jnp.logical_not(first))
    def _():
        clear()
        load_rest.wait()
        load_squares.wait()
        load_link.wait()

        def give_back(b):
            grad = nn(link[0:D, :], dkt[...]) + nn(link[D : 2 * D, :], dvt[...])
            sent[b] = grad.astype(BF)
            send_back(b).start()

        def both(b):
            h = hbuf.at[b % 2]
            load_cot(b).start()
            load_y(b).wait()
            send_memory(b).wait_recv()
            for i, target in enumerate((kt, vt)):
                target[...] = tn(link[pl.ds(i * D, D), :], got[b]).astype(BF)
            cross = (ut, qt, kt, vt, ot, lse, n1, r1)
            cross_forward(h, (s4, s5), vec, info[1 + count + b], *cross, pair)
            run_feed_forward(h)
            emit_hidden(b)
            take_cotangent(b, h)

            pl.when(b > 0)(lambda: store_dy(b - 1).wait())
            pl.when(b + 1 < count)(lambda: load_y(b + 1).start())
            run_feed_backward(h)
            cross_backward(
                h, (s4, s5), vec, info[1 + count + b], *cross, dca, dot, dqt,
                dkt, dvt, cross_acc, dvec, vacc, lambda: give_back(b),
            )
            for i, grad in enumerate((dkt, dvt)):
                link_acc[i] += nt(got[b], grad[...])
            store_dy(b).start()

        loop(0, count, both)
        store_hidden(count - 1).wait()
        store_dy(count - 1).wait()

        def back(b):
            loads = load_saved(b)
            for copy in loads + [load_dy(b)]:
                copy.start()
            for copy in loads + [load_dy(b)]:
                copy.wait()
            run_self_backward(b, hbuf.at[b % 2])

        loop(0, count // 2, back)
        out_dsq.start()
        store_dx(count // 2 - 1).wait()

    @pl.when(first)
    def _():
        loop(0, count, lambda b: send_memory(b).wait_send())

    @pl.when(jnp.logical_not(first))
    def _():
        loop(0, count, lambda b: send_back(b).wait_send())

    out_grads = []
    for i in range(12):
        rows_i = pl.ds(i * D, D)
        wts[rows_i, :] = acc[i].astype(BF)
        out_grads.append(pltpu.make_async_copy(wts.at[rows_i], grads.at[rows_i], grad_sems.at[i]))
        out_grads[-1].start()
    for copy in out_grads:
        copy.wait()
    out_dsq.wait()


def call_middle(info, vec, y, cot, weights, linked, saved):
    count, tokens = y.shape[0], y.shape[2]
    kept = saved_dims(tokens)
    wide16 = pltpu.VMEM((D, tokens), BF)
    wide32 = pltpu.VMEM((D, tokens), F32)
    tall16 = pltpu.VMEM((FF, tokens), BF)
    return pl.pallas_call(
        middle_kernel,
        name="middle",
        out_shape=[
            shape16(count * tokens, D),
            shape32(count, D, tokens),
            shape32(count * tokens, D),
            shape16(12 * D, D),
            shape32(4, D, D),
            shape32(D, LANES),
        ],
        in_specs=[smem_space(), vmem_space()] + [any_space()] * 14,
        out_specs=[any_space()] * 5 + [vmem_space()],
        scratch_shapes=[pltpu.VMEM(dims, kind) for dims, kind in kept]
        + [
            pltpu.VMEM((UNITS * D, D), BF),
            pltpu.VMEM((12, D, D), F32),
            pltpu.VMEM((4, D, D), F32),
            pltpu.VMEM((count, D, tokens), BF),
            pltpu.VMEM((count, D, tokens), BF),
            pltpu.VMEM((2, D, tokens), F32),
            wide32, wide16, tall16, tall16, wide16,
            pltpu.VMEM((1, tokens), F32),
            wide16, tall16,
            pltpu.VMEM((RU + 3, D, LANES), F32),
            pltpu.VMEM((tokens, tokens), F32),
            wide16, wide16, wide16, wide16, wide16,
            pltpu.VMEM((2, tokens, tokens), F32),
            pltpu.VMEM((tokens, D), BF),
            pltpu.VMEM((tokens, D), BF),
            pltpu.VMEM((tokens, D), F32),
            pltpu.VMEM((2 * D, D), BF),
            pltpu.SemaphoreType.DMA((4, count)),
            pltpu.SemaphoreType.DMA((8,)),
            pltpu.SemaphoreType.DMA((10,)),
            pltpu.SemaphoreType.DMA((12,)),
        ],
        compiler_params=pltpu.CompilerParams(
            collective_id=1, has_side_effects=True, vmem_limit_bytes=62 * 2**20
        ),
    )(info, vec, y, cot, weights, linked, *saved)


matrix_rate = 0.04
vector_rate = 0.25
matrix_decay = 0.01


def adam_update(weight, moment_old, square_old, gradient, learn_rate, decay_rate):
    moment_one = 0.5 * moment_old + 0.5 * gradient
    moment_two = 0.5 * square_old + 0.5 * gradient * gradient
    correction = 1.0 - 0.5**STEP
    adam_step = moment_one / correction / (jnp.sqrt(moment_two / correction) + 1e-08)
    return (weight - learn_rate * (adam_step + decay_rate * weight), moment_one, moment_two)


def adam_kernel(place, grad, weight, first, second, weight_out, first_out, second_out):
    taken = place[pl.program_id(0)] >= 0
    fresh = adam_update(weight[0], first[0], second[0], grad[...].astype(F32), matrix_rate, matrix_decay)
    for new, old, out in zip(fresh, (weight, first, second), (weight_out, first_out, second_out)):
        out[0] = jnp.where(taken, new, old[0])


def call_adam(place, grads, weight, first, second):
    slots = weight.shape[0]
    spec = block_spec(D, D)
    out = shape32(slots, D, D)
    return pl.pallas_call(
        adam_kernel,
        name="adam",
        out_shape=[out] * 3,
        grid_spec=pltpu.PrefetchScalarGridSpec(
            num_scalar_prefetch=1,
            grid=(slots,),
            in_specs=[pl.BlockSpec((D, D), lambda s, place: (jnp.maximum(place[s], 0), 0))] + [spec] * 3,
            out_specs=[spec] * 3,
        ),
    )(place, grads, weight, first, second)


def unit_tables(owner_row):
    tensor_of = np.array(TENSOR_OF)
    first_unit = np.array(FIRST_UNIT)
    owned_by = owner_row[:8]
    earlier = (owned_by[:, None] == owned_by[None, :]) & jnp.asarray(
        np.arange(8)[None, :] < np.arange(8)[:, None]
    )
    prior = jnp.sum(jnp.where(earlier, jnp.array(TENSOR_SIZE, jnp.int32)[None, :], 0), axis=1)
    unit_owner = owned_by[tensor_of]
    unit_slot = prior[tensor_of] + jnp.asarray(np.arange(UNITS) - first_unit[tensor_of], jnp.int32)
    return unit_owner, unit_slot.astype(jnp.int32)


def slot_units(owner_row, dp, slots):
    unit_owner, unit_slot = unit_tables(owner_row)
    hit = (unit_owner[None, :] == dp) & (unit_slot[None, :] == jnp.arange(slots, dtype=jnp.int32)[:, None])
    return jnp.sum(jnp.where(hit, jnp.arange(UNITS, dtype=jnp.int32)[None, :] + 1, 0), axis=1) - 1


def three_pieces(value):
    high = value.astype(BF)
    rest = value - high.astype(F32)
    mid = rest.astype(BF)
    low = (rest - mid.astype(F32)).astype(BF)
    pad = ((0, PIECE - value.shape[0]), (0, 0))
    parts = jnp.concatenate([jnp.pad(part, pad) for part in (high, mid, low)], axis=0)
    return jnp.pad(parts, ((0, VEC_ROWS - 3 * PIECE), (0, 0)))


def local(n_dp, tokens, cotangent, lengths, owners, master_sq, mom1_sq, mom2_sq, master_vec, mom1_vec, mom2_vec):
    section = lax.axis_index("section")
    dp = lax.axis_index("dp")
    count = lengths.shape[1]
    vec_store = master_vec[0, 0]
    vrows = vec_store.shape[0]
    owns_vector = owners[0, 8] == dp
    pack = three_pieces(jnp.where(owns_vector, vec_store, 0.0))
    own = jnp.where(section == 0, lengths[0], lengths[1])
    info = jnp.concatenate([section[None].astype(jnp.int32), own, lengths[0]])
    weights, vec, linked, *saved = call_start(n_dp, info, owners, tokens[0], master_sq[0, 0], pack, count)
    hidden, dy, dx, late, dsq, late_vec = call_middle(
        info, vec, saved[10], cotangent[0], weights, linked, saved[:10]
    )
    dx, total = call_finish(n_dp, info, dy, weights, vec, late, late_vec, dsq, dx, saved[:10])
    pieces = total[UNITS * D : UNITS * D + 3 * PIECE].astype(F32).reshape(3, PIECE, D)[:, :vrows]
    total_vector = pieces[0] + pieces[1] + pieces[2]
    place = slot_units(owners[0], dp, master_sq.shape[2])
    squares_new = call_adam(place, total, master_sq[0, 0], mom1_sq[0, 0], mom2_sq[0, 0])
    vector_new = adam_update(vec_store, mom1_vec[0, 0], mom2_vec[0, 0], total_vector, vector_rate, 0.0)
    vector_new = [
        jnp.where(owns_vector, new, old)
        for new, old in zip(vector_new, (vec_store, mom1_vec[0, 0], mom2_vec[0, 0]))
    ]
    return (
        hidden[None],
        dx[None],
        *[value[None, None] for value in squares_new],
        *[value[None, None] for value in vector_new],
    )


def solution(mesh):
    n_dp = mesh.shape["dp"]
    slots = P("section", "dp", None, None, None)
    packs = P("section", "dp", None, None)
    rows = P("section", "dp", None)
    return jax.shard_map(
        functools.partial(local, n_dp),
        mesh=mesh,
        in_specs=(rows, rows, P(None, "dp"), P("section", None), slots, slots, slots, packs, packs, packs),
        out_specs=(rows, rows, slots, slots, slots, packs, packs, packs),
        check_vma=False,
    )
```

```python
import functools
import jax
import jax.numpy as jnp
import numpy as np
from jax import lax
from jax.experimental import pallas as pl
from jax.experimental.pallas import tpu as pltpu
from jax.sharding import PartitionSpec as P

D = 512
HEADS = 8
HS = D // HEADS
FF = 2048
RU = FF // D
STEP = 5
LANES = 128
F32 = jnp.float32
BF = jnp.bfloat16
NEG = -1e30


def nn(a, b):
    return jnp.dot(a, b, preferred_element_type=F32)


def nt(a, b):
    return lax.dot_general(a, b, (((1,), (1,)), ((), ())), preferred_element_type=F32)


def tn(a, b):
    return lax.dot_general(a, b, (((0,), (0,)), ((), ())), preferred_element_type=F32)


def lane_loop(count, body):
    def step(i, carry):
        body(pl.ds(pl.multiple_of(i * LANES, LANES), LANES))
        return carry

    lax.fori_loop(0, count // LANES, step, 0, unroll=True)


def norm_parts(value):
    mean = jnp.mean(value, axis=0, keepdims=True)
    centred = value - mean
    inv = lax.rsqrt(jnp.mean(centred * centred, axis=0, keepdims=True) + 1e-05)
    return centred * inv, inv


def norm_grad(grad, normed, inv, gain):
    scaled = grad * gain
    mean_one = jnp.mean(scaled, axis=0, keepdims=True)
    mean_two = jnp.mean(scaled * normed, axis=0, keepdims=True)
    return (scaled - mean_one - normed * mean_two) * inv


def fill_bias(bias, length, causal, key_dim=0):
    rows = bias.shape[0]

    def body(lanes):
        across = lax.broadcasted_iota(jnp.int32, (rows, LANES), 0)
        along = lax.broadcasted_iota(jnp.int32, (rows, LANES), 1) + lanes.start
        key, query = (across, along) if key_dim == 0 else (along, across)
        allowed = key < length
        if causal is not None:
            allowed = allowed & ((key <= query) | jnp.logical_not(causal))
        bias[:, lanes] = jnp.where(allowed, 0.0, NEG)

    lane_loop(bias.shape[1], body)


def head_rows(h):
    return pl.ds(pl.multiple_of(h * HS, HS), HS)


def attend(qt, kt, vt, bias, length, ot, lse, pair):
    width = kt.shape[1]
    index = lax.broadcasted_iota(jnp.int32, (16, width), 0)
    if bias is None:
        masked = (index == 0) & (lax.broadcasted_iota(jnp.int32, index.shape, 1) >= length)
        masks = jnp.where(masked, NEG, 0.0).astype(BF)
        ones = jnp.where(index == 0, 1.0, 0.0).astype(BF)

    def score(h, out):
        rows = head_rows(h)
        keys, queries = kt[rows, :], qt[rows, :] * BF(0.125)
        if bias is None:
            keys = jnp.concatenate([keys, masks], axis=0)
            queries = jnp.concatenate([queries, ones], axis=0)
        out[...] = tn(keys, queries)

    def finish(h, scores):
        rows = head_rows(h)
        biased = scores[...] if bias is None else scores[...] + bias[...]
        top = jnp.max(biased, axis=0, keepdims=True)
        weights = jnp.exp(biased - top).astype(BF)
        values = jnp.concatenate([vt[rows, :], jnp.ones((16, width), BF)], axis=0)
        out = nn(values, weights)
        total = out[HS : HS + 1]
        ot[rows, :] = (out[:HS] * (1.0 / total)).astype(BF)
        lse[pl.ds(h, 1), :] = top + jnp.log(total)

    one, two = pair.at[0], pair.at[1]
    score(0, one)

    def body(i, carry):
        score(2 * i + 1, two)
        finish(2 * i, one)
        score(jnp.minimum(2 * i + 2, HEADS - 1), one)
        finish(2 * i + 1, two)
        return carry

    lax.fori_loop(0, HEADS // 2, body, 0, unroll=True)


def split_rows(row, count):
    high = row.astype(BF)
    rest = row - high.astype(F32)
    mid = rest.astype(BF)
    low = (rest - mid.astype(F32)).astype(BF)
    index = lax.broadcasted_iota(jnp.int32, (16, row.shape[1]), 0)
    parts = jnp.where(index == 0, high, jnp.where(index == 1, mid, low))
    return jnp.where(index < 3, parts, BF(count))


def attend_back(qt, kt, vt, bias, length, ot, lse, dot, dqt, dkt, dvt):
    index = lax.broadcasted_iota(jnp.int32, (16, kt.shape[1]), 0)
    ones = jnp.where(index < 3, 1.0, 0.0).astype(BF)
    masks = ones
    if bias is None:
        masked = (index == 3) & (lax.broadcasted_iota(jnp.int32, index.shape, 1) >= length)
        masks = jnp.where(masked, NEG, ones.astype(F32)).astype(BF)

    def head(h, carry):
        rows = head_rows(h)
        keys, grads = kt[rows, :], dot[rows, :]
        queries = qt[rows, :] * BF(0.125)
        delta = jnp.sum(grads.astype(F32) * ot[rows, :].astype(F32), axis=0, keepdims=True)
        left = jnp.concatenate([queries, split_rows(-lse[pl.ds(h, 1), :], 1)], axis=0)
        scores = tn(left, jnp.concatenate([keys, masks], axis=0))
        probs = jnp.exp(scores if bias is None else scores + bias[...])
        left = jnp.concatenate([grads, split_rows(-delta, 0)], axis=0)
        dscores = (probs * tn(left, jnp.concatenate([vt[rows, :], ones], axis=0))).astype(BF)
        dvt[rows, :] = nn(grads, probs.astype(BF)).astype(BF)
        dkt[rows, :] = nn(queries, dscores).astype(BF)
        dqt[rows, :] = (nt(keys, dscores) * 0.125).astype(BF)
        return carry

    lax.fori_loop(0, HEADS, head, 0, unroll=True)


GAIN, SHIFT, B2, B1 = 0, 3, 6, 7


def column(vec, index):
    return vec[:, index : index + 1]


def self_column(vec, first, row):
    return jnp.where(first, column(vec, row + 1), column(vec, row))


def add_column(dvec, index, acc):
    dvec[:, index : index + 1] += jnp.sum(acc, axis=1, keepdims=True)


def self_forward(x, sq, vec, first, length, ut, n0, r0, qt, kt, vt, ot, lse, n1, r1, y, bias, et, pair, pause):
    tokens = x.shape[0]
    et[...] = x[...].astype(F32).T

    def entry(lanes):
        value = et[:, lanes]
        normed, inv = norm_parts(value)
        n0[:, lanes] = normed.astype(BF)
        r0[:, lanes] = inv
        value = jnp.where(first, normed * column(vec, GAIN) + column(vec, SHIFT), value)
        et[:, lanes] = value
        ut[:, lanes] = value.astype(BF)

    lane_loop(tokens, entry)
    fill_bias(bias, length, jnp.logical_not(first))
    for index, out in enumerate((qt, kt, vt)):
        out[...] = tn(sq[index][...], ut[...]).astype(BF)
    pause()
    attend(qt, kt, vt, bias, length, ot, lse, pair)
    pause()
    et[...] += tn(sq[3][...], ot[...])
    gain, shift = self_column(vec, first, GAIN), self_column(vec, first, SHIFT)

    def leave(lanes):
        normed, inv = norm_parts(et[:, lanes])
        n1[:, lanes] = normed.astype(BF)
        r1[:, lanes] = inv
        y[:, lanes] = normed * gain + shift

    lane_loop(tokens, leave)


def self_backward(
    dy, sq, vec, first, length, ut, n0, r0, qt, kt, vt, ot, lse, n1, r1, dx,
    bias, dsa, dot, dqt, dkt, dvt, dsq, dvec, vacc, pause,
):
    tokens = dy.shape[1]
    vacc[...] = jnp.zeros(vacc.shape, F32)
    gain = self_column(vec, first, GAIN)

    def leave(lanes):
        grad, normed = dy[:, lanes], n1[:, lanes].astype(F32)
        vacc[2] += grad * normed
        vacc[3] += grad
        grad = norm_grad(grad, normed, r1[:, lanes], gain)
        dy[:, lanes] = grad
        dsa[:, lanes] = grad.astype(BF)

    lane_loop(tokens, leave)
    fill_bias(bias, length, jnp.logical_not(first), 1)
    dot[...] = nn(sq[3][...], dsa[...]).astype(BF)
    dsq[3] += nt(ot[...], dsa[...])
    pause()
    attend_back(qt, kt, vt, bias, length, ot, lse, dot, dqt, dkt, dvt)
    for index, grad in enumerate((dqt, dkt, dvt)):
        dsq[index] += nt(ut[...], grad[...])
        dy[...] += nn(sq[index][...], grad[...])
    pause()
    entry_gain = column(vec, GAIN)

    def entry(lanes):
        grad, normed = dy[:, lanes], n0[:, lanes].astype(F32)
        vacc[0] += grad * normed
        vacc[1] += grad
        dy[:, lanes] = jnp.where(first, norm_grad(grad, normed, r0[:, lanes], entry_gain), grad)

    lane_loop(tokens, entry)
    dx[...] = dy[...].T

    @pl.when(first)
    def _():
        add_column(dvec, GAIN, vacc[0])
        add_column(dvec, SHIFT, vacc[1])
        add_column(dvec, GAIN + 1, vacc[2])
        add_column(dvec, SHIFT + 1, vacc[3])

    @pl.when(jnp.logical_not(first))
    def _():
        add_column(dvec, GAIN, vacc[2])
        add_column(dvec, SHIFT, vacc[3])


def gelu_parts(z):
    root = 0.7978845608028654
    square = z * z
    t = jnp.tanh(z * (root + (root * 0.044715) * square))
    half = 0.5 + 0.5 * t
    act = z * half
    slope = half + act * (1.0 - t) * (root + (3.0 * root * 0.044715) * square)
    return act, slope


def feed_forward(h, units, vec, hb, act, slope, n2, r2, out):
    hb[...] = h[...].astype(BF)
    for c in range(RU):
        rows = slice(c * D, (c + 1) * D)
        a, s = gelu_parts(tn(units[c][...], hb[...]) + column(vec, B1 + c))
        act[rows, :] = a.astype(BF)
        if slope is not None:
            slope[rows, :] = s.astype(BF)
    for c in range(RU):
        rows = slice(c * D, (c + 1) * D)
        h[...] += tn(units[RU + c][...], act[rows, :])

    def leave(lanes):
        normed, inv = norm_parts(h[:, lanes] + column(vec, B2))
        n2[:, lanes] = normed.astype(BF)
        r2[:, lanes] = inv
        out[:, lanes] = normed * column(vec, GAIN + 2) + column(vec, SHIFT + 2)

    lane_loop(h.shape[1], leave)


def feed_backward(dm, units, vec, hb, act, slope, n2, r2, dfb, dz, dunits, dvec, vacc):
    vacc[...] = jnp.zeros(vacc.shape, F32)

    def leave(lanes):
        grad, normed = dm[:, lanes], n2[:, lanes].astype(F32)
        vacc[RU + 1] += grad * normed
        vacc[RU + 2] += grad
        grad = norm_grad(grad, normed, r2[:, lanes], column(vec, GAIN + 2))
        dm[:, lanes] = grad
        short = grad.astype(BF)
        vacc[RU] += short.astype(F32)
        dfb[:, lanes] = short

    lane_loop(dm.shape[1], leave)
    for c in range(RU):
        rows = slice(c * D, (c + 1) * D)
        dz[rows, :] = (nn(units[RU + c][...], dfb[...]) * slope[rows, :].astype(F32)).astype(BF)
        dunits[RU + c][...] += nt(act[rows, :], dfb[...])
    for c in range(RU):
        rows = slice(c * D, (c + 1) * D)
        dm[...] += nn(units[c][...], dz[rows, :])
        dunits[c][...] += nt(hb[...], dz[rows, :])
        for lanes in range(0, dm.shape[1], LANES):
            vacc[c] += dz[rows, lanes : lanes + LANES].astype(F32)
    for index in range(RU):
        add_column(dvec, B1 + index, vacc[index])
    add_column(dvec, B2, vacc[RU])
    add_column(dvec, GAIN + 2, vacc[RU + 1])
    add_column(dvec, SHIFT + 2, vacc[RU + 2])


def cross_forward(a, sq, vec, length, ab, cqt, kt, vt, ot, lse, n1, r1, pair):
    ab[...] = a[...].astype(BF)
    cqt[...] = tn(sq[0][...], ab[...]).astype(BF)
    attend(cqt, kt, vt, None, length, ot, lse, pair)
    a[...] += tn(sq[1][...], ot[...])

    def leave(lanes):
        normed, inv = norm_parts(a[:, lanes])
        n1[:, lanes] = normed.astype(BF)
        r1[:, lanes] = inv
        a[:, lanes] = normed * column(vec, GAIN + 1) + column(vec, SHIFT + 1)

    lane_loop(a.shape[1], leave)


def cross_backward(
    dbq, sq, vec, length, ab, cqt, kt, vt, ot, lse, n1, r1, dca, dot, dqt, dkt, dvt, dsq, dvec, vacc, ready
):
    vacc[0] = jnp.zeros(vacc.shape[1:], F32)
    vacc[1] = jnp.zeros(vacc.shape[1:], F32)

    def leave(lanes):
        grad, normed = dbq[:, lanes], n1[:, lanes].astype(F32)
        vacc[0] += grad * normed
        vacc[1] += grad
        grad = norm_grad(grad, normed, r1[:, lanes], column(vec, GAIN + 1))
        dbq[:, lanes] = grad
        dca[:, lanes] = grad.astype(BF)

    lane_loop(dbq.shape[1], leave)
    dot[...] = nn(sq[1][...], dca[...]).astype(BF)
    dsq[1][...] += nt(ot[...], dca[...])
    attend_back(cqt, kt, vt, None, length, ot, lse, dot, dqt, dkt, dvt)
    ready()
    dsq[0][...] += nt(ab[...], dqt[...])
    dbq[...] += nn(sq[0][...], dqt[...])
    add_column(dvec, GAIN + 1, vacc[0])
    add_column(dvec, SHIFT + 1, vacc[1])


SUB = 256
HALF = SUB // 2
QUART = SUB // 4
UNITS = 6 + 2 * RU
VEC_ROWS = 256
SUBS = (UNITS * D + VEC_ROWS) // SUB
MESH = pl.DeviceIdType.MESH


class Total:
    def __init__(self, n_dp, hop, order, shorts, other, mine, out, core_in, half, x_in, right_in, left_in, passed, sems):
        self.length = n_dp // 4
        self.hop = hop
        self.last = self.length - 1
        self.section = lax.axis_index("section")
        self.dp = lax.axis_index("dp")
        self.core, self.x, self.z = self.dp % 2, (self.dp // 2) % 2, self.dp // 4
        self.sibling, self.beside = self.dp + 1 - 2 * self.core, self.dp + 2 - 4 * self.x
        self.has_left, self.has_right = self.z > 0, self.z < self.last
        self.order, self.shorts, self.other, self.mine = order, shorts, other, mine
        self.out, self.core_in, self.half, self.x_in = out, core_in, half, x_in
        self.right_in, self.left_in, self.passed, self.sems = right_in, left_in, passed, sems
        far = self.last
        self.ticks = SUBS + self.hop * (2 + far + far) + 1

    def greet(self, across=False):
        barrier = pltpu.get_barrier_semaphore()

        def signal(index):
            pl.semaphore_signal(barrier, inc=1, device_id=(self.section, index), device_id_type=MESH)

        signal(self.sibling)
        signal(self.beside)
        pl.when(self.has_left)(lambda: signal(self.dp - 4))
        pl.when(self.has_right)(lambda: signal(self.dp + 4))
        if across:
            pl.semaphore_signal(barrier, inc=1, device_id=(1 - self.section, self.dp), device_id_type=MESH)
        sides = self.has_left.astype(jnp.int32) + self.has_right.astype(jnp.int32)
        pl.semaphore_wait(barrier, 2 + int(across) + sides)

    def short_route(self, t):
        return ((t & 1) == 0) | ((t >= self.shorts[0]) & (t < self.shorts[1]))

    def home(self, t):
        return (t >> 1) & self.last

    def place(self, t, start, size):
        return pl.ds(pl.multiple_of(self.order(t) * SUB + start, QUART), size)

    def send(self, step, t, source, target, index):
        return pltpu.make_async_remote_copy(
            src_ref=source,
            dst_ref=target,
            send_sem=self.sems.at[0, step, t],
            recv_sem=self.sems.at[1, step, t],
            device_id=(self.section, index),
            device_id_type=MESH,
        )

    def part(self, size, index):
        return pl.ds(pl.multiple_of(index * size, size), size)

    def copy_core(self, t):
        source = self.other(t, self.order(t), HALF * (1 - self.core))
        return self.send(0, t, source, self.core_in.at[t], self.sibling)

    def copy_x(self, t):
        rows = self.part(QUART, 1 - self.x)
        return self.send(1, t, self.half.at[t, rows], self.x_in.at[t, pl.ds(0, QUART)], self.beside)

    def copy_x_whole(self, t):
        return self.send(1, t, self.passed.at[t], self.x_in.at[t], self.beside)

    def copy_right(self, t, source):
        return self.send(2, t, source, self.right_in.at[t, pl.ds(0, QUART)], self.dp + 4)

    def copy_left(self, t, source):
        return self.send(3, t, source, self.left_in.at[t, pl.ds(0, QUART)], self.dp - 4)

    def copy_right_whole(self, t, source):
        return self.send(2, t, source, self.right_in.at[t], self.dp + 4)

    def copy_left_whole(self, t, source):
        return self.send(3, t, source, self.left_in.at[t], self.dp - 4)

    def copy_back_x(self, t):
        place = self.place(t, HALF * self.core + QUART * self.x, QUART)
        return self.send(4, t, self.out.at[place], self.out.at[place], self.beside)

    def copy_back_core(self, t):
        place = self.place(t, HALF * self.core, HALF)
        return self.send(5, t, self.out.at[place], self.out.at[place], self.sibling)

    def copy_back_right(self, t):
        place = self.place(t, HALF * self.core, HALF)
        return self.send(4, t, self.out.at[place], self.out.at[place], self.dp + 4)

    def copy_back_left(self, t):
        place = self.place(t, HALF * self.core, HALF)
        return self.send(6, t, self.out.at[place], self.out.at[place], self.dp - 4)

    def add(self, one, two):
        return one + two

    def own_quarter(self, t):
        return self.half.at[t, self.part(QUART, self.x)]

    def short_core(self, t):
        self.copy_core(t).wait_recv()
        self.half[t] = self.add(self.mine(t, self.order(t), HALF * self.core), self.core_in[t])
        self.copy_x(t).start()

    def short_x(self, t):
        self.copy_x(t).wait_recv()
        quart = self.own_quarter(t)
        quart[...] = self.add(quart[...], self.x_in[t, 0:QUART])

        @pl.when(jnp.logical_not(self.has_left) & self.has_right)
        def _():
            self.copy_right(t, quart).start()

        @pl.when(jnp.logical_not(self.has_right) & self.has_left)
        def _():
            self.copy_left(t, quart).start()

    def short_right(self, t):
        @pl.when(self.has_left)
        def _():
            target = self.passed.at[t, pl.ds(0, QUART)]
            self.copy_right(t, target).wait_recv()

            @pl.when(self.has_right)
            def _():
                target[...] = self.add(self.own_quarter(t)[...], self.right_in[t, 0:QUART])
                self.copy_right(t, target).start()

    def short_left(self, t):
        @pl.when(self.has_right)
        def _():
            target = self.passed.at[t, pl.ds(QUART, QUART)]
            self.copy_left(t, target).wait_recv()

            @pl.when(self.has_left)
            def _():
                target[...] = self.add(self.own_quarter(t)[...], self.left_in[t, 0:QUART])
                self.copy_left(t, target).start()

    def short_total(self, t):
        total = self.own_quarter(t)[...].astype(F32)
        total += jnp.where(self.has_left, self.right_in[t, 0:QUART].astype(F32), 0.0)
        total += jnp.where(self.has_right, self.left_in[t, 0:QUART].astype(F32), 0.0)
        self.out[self.place(t, HALF * self.core + QUART * self.x, QUART), :] = total.astype(BF)
        self.copy_back_x(t).start()

    def short_back(self, t):
        self.copy_back_x(t).wait_recv()
        self.copy_back_core(t).start()

    def long_core(self, t):
        self.copy_core(t).wait_recv()
        self.half[t] = self.add(self.mine(t, self.order(t), HALF * self.core), self.core_in[t])
        home = self.home(t)

        @pl.when(jnp.logical_not(self.has_left) & (home > 0))
        def _():
            self.copy_right_whole(t, self.half.at[t]).start()

        @pl.when(jnp.logical_not(self.has_right) & (home < self.last))
        def _():
            self.copy_left_whole(t, self.half.at[t]).start()

    def long_right(self, t):
        @pl.when(self.has_left & (self.z < self.home(t)))
        def _():
            self.copy_right_whole(t, self.passed.at[t]).wait_recv()
            self.passed[t] = self.add(self.half[t], self.right_in[t])
            self.copy_right_whole(t, self.passed.at[t]).start()

    def long_left(self, t):
        @pl.when(self.has_right & (self.z > self.home(t)))
        def _():
            self.copy_left_whole(t, self.passed.at[t]).wait_recv()
            self.passed[t] = self.add(self.half[t], self.left_in[t])
            self.copy_left_whole(t, self.passed.at[t]).start()

    def long_home(self, t):
        @pl.when(self.z == self.home(t))
        def _():
            pl.when(self.has_left)(lambda: self.copy_right_whole(t, self.half.at[t]).wait_recv())
            pl.when(self.has_right)(lambda: self.copy_left_whole(t, self.half.at[t]).wait_recv())
            total = self.half[t].astype(F32)
            total += jnp.where(self.has_left, self.right_in[t].astype(F32), 0.0)
            total += jnp.where(self.has_right, self.left_in[t].astype(F32), 0.0)
            self.passed[t] = total.astype(BF)
            self.copy_x_whole(t).start()

    def long_x(self, t):
        @pl.when(self.z == self.home(t))
        def _():
            self.copy_x_whole(t).wait_recv()
            self.out[self.place(t, HALF * self.core, HALF), :] = self.add(self.passed[t], self.x_in[t])
            pl.when(self.has_left)(lambda: self.copy_back_left(t).start())
            pl.when(self.has_right)(lambda: self.copy_back_right(t).start())
            self.copy_back_core(t).start()

    def long_back(self, t):
        home = self.home(t)

        @pl.when(self.z > home)
        def _():
            self.copy_back_right(t).wait_recv()
            pl.when(self.has_right)(lambda: self.copy_back_right(t).start())

        @pl.when(self.z < home)
        def _():
            self.copy_back_left(t).wait_recv()
            pl.when(self.has_left)(lambda: self.copy_back_left(t).start())

        pl.when(self.z != home)(lambda: self.copy_back_core(t).start())

    def tick(self, now, prepare):
        z, last = self.z, self.last
        far = jnp.maximum(z, last - z)
        prepared = now

        @pl.when(prepared < SUBS)
        def _():
            prepare(prepared)
            self.copy_core(prepared).start()

        def due(step, lag, short):
            t = now - self.hop * lag
            fits = (t >= 0) & (t < SUBS)
            kind = self.short_route(t) if short else jnp.logical_not(self.short_route(t))
            pl.when(fits & kind)(lambda: step(t))

        due(self.short_core, 1, True)
        due(self.short_x, 2, True)
        due(self.short_right, 2 + z, True)
        due(self.short_left, 2 + last - z, True)
        due(self.short_total, 2 + far, True)
        due(self.short_back, 3 + far, True)
        due(self.long_core, 1, False)
        due(self.long_right, 1 + z, False)
        due(self.long_left, 1 + last - z, False)
        due(self.long_home, 1 + far, False)
        due(self.long_x, 2 + far, False)
        for home in range(self.length):
            lag = 2 + max(home, last - home) + jnp.abs(z - home)
            t = now - self.hop * lag
            fits = (t >= 0) & (t < SUBS) & jnp.logical_not(self.short_route(t)) & (self.home(t) == home)
            pl.when(fits & (z != home))(lambda t=t: self.long_back(t))

    def arrive(self, t):
        self.copy_back_core(t).wait_recv()

    def settle(self, t):
        self.copy_core(t).wait_send()
        self.copy_back_core(t).wait_send()
        home = self.home(t)

        @pl.when(self.short_route(t))
        def _():
            self.copy_x(t).wait_send()
            pl.when(self.has_right)(lambda: self.copy_right(t, self.own_quarter(t)).wait_send())
            pl.when(self.has_left)(lambda: self.copy_left(t, self.own_quarter(t)).wait_send())
            self.copy_back_x(t).wait_send()

        @pl.when(jnp.logical_not(self.short_route(t)))
        def _():
            pl.when(self.z < home)(lambda: self.copy_right_whole(t, self.half.at[t]).wait_send())
            pl.when(self.z > home)(lambda: self.copy_left_whole(t, self.half.at[t]).wait_send())
            pl.when(self.z == home)(lambda: self.copy_x_whole(t).wait_send())
            pl.when(self.has_right & (self.z >= home))(lambda: self.copy_back_right(t).wait_send())
            pl.when(self.has_left & (self.z <= home))(lambda: self.copy_back_left(t).wait_send())


def loop(start, stop, body):
    def step(i, carry):
        body(i)
        return carry

    lax.fori_loop(start, stop, step, 0)


def total_scratch():
    return [pltpu.VMEM((SUBS, HALF, D), BF)] * 6 + [pltpu.SemaphoreType.DMA((2, 7, SUBS))]


def any_space():
    return pl.BlockSpec(memory_space=pl.ANY)


def vmem_space():
    return pl.BlockSpec(memory_space=pltpu.VMEM)


def smem_space():
    return pl.BlockSpec(memory_space=pltpu.SMEM)


def block_spec(*dims):
    return pl.BlockSpec((1,) + dims, lambda b, info: (b,) + (0,) * len(dims))


def shape32(*dims):
    return jax.ShapeDtypeStruct(dims, F32)


def shape16(*dims):
    return jax.ShapeDtypeStruct(dims, BF)


TENSOR_OF = (0, 1, 2, 3, 4, 5) + (6,) * RU + (7,) * RU
TENSOR_SIZE = (1,) * 6 + (RU, RU)
FIRST_UNIT = (0, 1, 2, 3, 4, 5, 6, 6 + RU)
VEC_BLOCKS = VEC_ROWS // SUB
EARLY = 4 * D // SUB + VEC_BLOCKS
LINKED = 6 * D // SUB + VEC_BLOCKS
PIECE = 16


def copies(sources, targets, sems):
    return [pltpu.make_async_copy(s, t, sems.at[i]) for i, (s, t) in enumerate(zip(sources, targets))]


def slot_of(owners, tensor):
    prior = jnp.int32(0)
    for earlier in range(tensor):
        prior += jnp.where(owners[0, earlier] == owners[0, tensor], TENSOR_SIZE[earlier], 0)
    return prior


def start_kernel(n_dp, info, owners, x, slots, pack, out, vec, linked, *refs):
    saved_out, (y_out, stage, *comm), refs = refs[:10], refs[10:19], refs[19:]
    saved, (y, xb, bias, et, pair, places, counter, sems, link_sems) = refs[:10], refs[10:]
    count, tokens = saved_out[0].shape[0], saved_out[0].shape[2]
    first = lax.axis_index("section") == 0
    dp = lax.axis_index("dp")
    for unit in range(UNITS):
        tensor = TENSOR_OF[unit]
        slot = jnp.minimum(slot_of(owners, tensor) + (unit - FIRST_UNIT[tensor]), slots.shape[0] - 1)
        places[0, unit] = slot
        places[1, unit] = (owners[0, tensor] == dp).astype(jnp.int32)

    def own(block, start):
        is_pack = block >= SUBS - VEC_BLOCKS
        unit = jnp.minimum(block * SUB // D, UNITS - 1)
        at = pl.multiple_of((block * SUB) % D + start, HALF)
        value = jnp.where(places[1, unit] == 1, slots[places[0, unit], pl.ds(at, HALF), :], 0.0).astype(BF)
        return jnp.where(is_pack, pack[pl.ds(pl.multiple_of(start, HALF), HALF), :], value)

    def order(t):
        return jnp.where(t < VEC_BLOCKS, t + SUBS - VEC_BLOCKS, t - VEC_BLOCKS)

    total = Total(
        n_dp,
        4,
        order,
        (0, LINKED),
        lambda t, block, start: stage.at[t],
        lambda t, block, start: own(block, start),
        out,
        *comm,
    )

    def prepare(t):
        stage[t] = own(order(t), HALF * (1 - total.core))

    def run(ticks):
        begin = counter[0]
        stop = jnp.minimum(begin + ticks, total.ticks)
        loop(begin, stop, lambda now: total.tick(now, prepare))
        counter[0] = stop

    link = pltpu.make_async_remote_copy(
        src_ref=out.at[pl.ds(4 * D, 2 * D)],
        dst_ref=linked,
        send_sem=link_sems.at[0],
        recv_sem=link_sems.at[1],
        device_id=(1 - total.section, dp),
        device_id_type=MESH,
    )
    total.greet(across=True)
    counter[0] = 0
    run(EARLY + total.hop * (3 + total.last))
    loop(0, EARLY, total.arrive)
    rows = [out[pl.ds(UNITS * D + i * PIECE, PIECE), :].astype(F32) for i in range(3)]
    whole = jnp.concatenate([rows[0] + rows[1] + rows[2], jnp.zeros((LANES - PIECE, D), F32)], axis=0)
    vec[...] = whole.T
    squares = [out.at[pl.ds(i * D, D)] for i in range(4)]

    def outward(b):
        return copies(saved + (y,), [ref.at[b] for ref in saved_out + (y_out,)], sems)

    def block(b):
        @pl.when(b == 1)
        def _():
            run(jnp.maximum(LINKED + total.hop * (3 + total.last) - counter[0], 0))
            loop(EARLY, LINKED, total.arrive)
            pl.when(first)(lambda: link.start())

        load = pltpu.make_async_copy(x.at[pl.ds(pl.multiple_of(b * tokens, tokens), tokens)], xb, sems.at[11])
        load.start()

        @pl.when(b > 0)
        def _():
            for copy in outward(b - 1):
                copy.wait()

        load.wait()
        self_forward(
            xb, squares, vec, first, info[1 + b], *saved, y, bias, et, pair, lambda: run(2)
        )
        for copy in outward(b):
            copy.start()
        run(1)

    loop(0, count, block)
    run(total.ticks)
    for copy in outward(count - 1):
        copy.wait()
    loop(LINKED, SUBS, total.arrive)
    loop(0, SUBS, total.settle)
    pl.when(first)(lambda: link.wait_send())
    pl.when(jnp.logical_not(first))(lambda: link.wait_recv())


def saved_dims(tokens):
    wide, row = ((D, tokens), BF), ((1, tokens), F32)
    return [wide, wide, row, wide, wide, wide, wide, ((HEADS, tokens), F32), wide, row]


def call_start(n_dp, info, owners, x, slots, pack, count):
    tokens = x.shape[0] // count
    kept = saved_dims(tokens)
    scores = pltpu.VMEM((tokens, tokens), F32)
    return pl.pallas_call(
        functools.partial(start_kernel, n_dp),
        name="start",
        out_shape=[shape16(SUBS * SUB, D), shape32(D, LANES), shape16(2 * D, D)]
        + [jax.ShapeDtypeStruct((count,) + dims, kind) for dims, kind in kept]
        + [shape32(count, D, tokens)],
        in_specs=[smem_space(), smem_space(), any_space(), vmem_space(), vmem_space()],
        out_specs=[vmem_space()] * 3 + [any_space()] * 11,
        scratch_shapes=[pltpu.VMEM((SUBS, HALF, D), BF)]
        + total_scratch()
        + [pltpu.VMEM(dims, kind) for dims, kind in kept]
        + [
            pltpu.VMEM((D, tokens), F32),
            pltpu.VMEM((tokens, D), BF),
            scores,
            pltpu.VMEM((D, tokens), F32),
            pltpu.VMEM((2, tokens, tokens), F32),
            pltpu.SMEM((2, UNITS), jnp.int32),
            pltpu.SMEM((1,), jnp.int32),
            pltpu.SemaphoreType.DMA((12,)),
            pltpu.SemaphoreType.DMA((2,)),
        ],
        compiler_params=pltpu.CompilerParams(
            collective_id=0, has_side_effects=True, vmem_limit_bytes=60 * 2**20
        ),
    )(info, owners, x, slots, pack)


def finish_kernel(n_dp, info, dy, sq, vec, late_in, late_vec, dsq_in, dx_in, *refs):
    saved_in, (dx_out, out), (late, stage, *comm), refs = refs[:10], refs[10:12], refs[12:21], refs[21:]
    saved, (dys, dx, bias, dsa, dot, dqt, dkt, dvt, dsq, dvec, vacc, pack, counter, sems, link_sems) = refs[:10], refs[10:]
    count, tokens = dy.shape[0], dy.shape[2]
    first = lax.axis_index("section") == 0
    early = EARLY - VEC_BLOCKS
    others = SUBS - EARLY

    mixed = 2 * D // SUB
    plain = others - mixed

    def order(t):
        block = jnp.where(t < plain, t + early + mixed, t - plain + early)
        return jnp.where(t < others, block, jnp.where(t < SUBS - VEC_BLOCKS, t - others, t))

    def own_early(block, start):
        unit = jnp.minimum(block * SUB // D, 3)
        at = pl.multiple_of((block * SUB) % D + start, HALF)
        value = dsq[unit, pl.ds(at, HALF), :].astype(BF)
        return jnp.where(block >= SUBS - VEC_BLOCKS, pack[pl.ds(pl.multiple_of(start, HALF), HALF), :], value)

    def own_late(block, start):
        return late[pl.ds(pl.multiple_of((block - early) * SUB + start, HALF), HALF), :]

    def mine(t, block, start):
        return lax.cond(t < others, lambda: own_late(block, start), lambda: own_early(block, start))

    total = Total(
        n_dp, 3, order, (others, SUBS), lambda t, block, start: stage.at[t], mine, out, *comm
    )

    def prepare(t):
        pl.when((t == plain) & first)(lambda: link.wait_recv())
        stage[t] = mine(t, order(t), HALF * (1 - total.core))

    def run(ticks, end):
        begin = counter[0]
        stop = jnp.minimum(begin + ticks, end)
        loop(begin, stop, lambda now: total.tick(now, prepare))
        counter[0] = stop

    link = pltpu.make_async_remote_copy(
        src_ref=late_in.at[pl.ds(10 * D, 2 * D)],
        dst_ref=late.at[pl.ds(0, 2 * D)],
        send_sem=link_sems.at[0],
        recv_sem=link_sems.at[1],
        device_id=(1 - total.section, total.dp),
        device_id_type=MESH,
    )
    counter[0] = 0
    load_dsq = pltpu.make_async_copy(dsq_in, dsq, sems.at[12])
    load_late = pltpu.make_async_copy(late_in.at[pl.ds(2 * D, 8 * D)], late.at[pl.ds(2 * D, 8 * D)], sems.at[13])
    load_mixed = pltpu.make_async_copy(late_in.at[pl.ds(0, 2 * D)], late.at[pl.ds(0, 2 * D)], sems.at[14])
    load_late.start()
    pl.when(jnp.logical_not(first))(lambda: load_mixed.start())
    load_dsq.start()
    dvec[...] = late_vec[...]
    total.greet(across=True)
    pl.when(jnp.logical_not(first))(lambda: link.start())
    load_late.wait()
    pl.when(jnp.logical_not(first))(lambda: load_mixed.wait())
    begin = count // 2
    squares = [sq.at[pl.ds(i * D, D)] for i in range(4)]

    def block(b):
        loads = copies([ref.at[b] for ref in saved_in] + [dy.at[b]], saved + (dys,), sems)
        for copy in loads:
            copy.start()
        run(4, others)

        def store(b):
            return pltpu.make_async_copy(
                dx, dx_out.at[pl.ds(pl.multiple_of(b * tokens, tokens), tokens)], sems.at[11]
            )

        pl.when(b == begin)(lambda: load_dsq.wait())
        pl.when(b > begin)(lambda: store(b - 1).wait())
        for copy in loads:
            copy.wait()
        self_backward(
            dys, squares, vec, first, info[1 + b], *saved, dx,
            bias, dsa, dot, dqt, dkt, dvt, dsq, dvec, vacc, lambda: run(3, others),
        )
        store(b).start()
        pl.when(b == count - 1)(lambda: store(b).wait())

    loop(begin, count, block)
    value = dvec[...].T[:PIECE]
    high = value.astype(BF)
    rest = value - high.astype(F32)
    mid = rest.astype(BF)
    pack[...] = jnp.zeros(pack.shape, BF)
    pack[0:PIECE, :] = high
    pack[PIECE : 2 * PIECE, :] = mid
    pack[2 * PIECE : 3 * PIECE, :] = (rest - mid.astype(F32)).astype(BF)
    run(total.ticks, total.ticks)
    loop(0, SUBS, total.arrive)
    loop(0, SUBS, total.settle)
    pl.when(jnp.logical_not(first))(lambda: link.wait_send())


def call_finish(n_dp, info, dy, weights, vec, late, late_vec, dsq, dx, saved):
    count, tokens = dy.shape[0], dy.shape[2]
    kept = saved_dims(tokens)
    wide16 = pltpu.VMEM((D, tokens), BF)
    wide32 = pltpu.VMEM((D, tokens), F32)
    return pl.pallas_call(
        functools.partial(finish_kernel, n_dp),
        name="finish",
        out_shape=[shape32(count * tokens, D), shape16(SUBS * SUB, D)],
        grid=(1,),
        in_specs=[
            smem_space(),
            any_space(),
            pl.BlockSpec((4 * D, D), lambda i: (0, 0)),
            vmem_space(),
            any_space(),
            vmem_space(),
        ]
        + [any_space()] * 12,
        out_specs=[any_space(), vmem_space()],
        input_output_aliases={7: 0},
        scratch_shapes=[pltpu.VMEM((10 * D, D), BF), pltpu.VMEM((SUBS, HALF, D), BF)]
        + total_scratch()
        + [pltpu.VMEM(dims, kind) for dims, kind in kept]
        + [wide32, pltpu.VMEM((tokens, D), F32), pltpu.VMEM((tokens, tokens), F32)]
        + [wide16] * 5
        + [
            pltpu.VMEM((4, D, D), F32),
            pltpu.VMEM((D, LANES), F32),
            pltpu.VMEM((4, D, LANES), F32),
            pltpu.VMEM((VEC_ROWS, D), BF),
            pltpu.SMEM((1,), jnp.int32),
            pltpu.SemaphoreType.DMA((15,)),
            pltpu.SemaphoreType.DMA((2,)),
        ],
        compiler_params=pltpu.CompilerParams(
            collective_id=2, has_side_effects=True, vmem_limit_bytes=60 * 2**20
        ),
    )(info, dy, weights, vec, late, late_vec, dsq, dx, *saved)


def middle_kernel(info, vec, y, cot, weights, linked, *refs):
    saved_in, outs, refs = refs[:10], refs[10:16], refs[16:]
    hidden, dy, dx_out, grads, dsq_out, dvec = outs
    saved, refs = refs[:10], refs[10:]
    ut, n0, r0, qt, kt, vt, ot, lse, n1, r1 = saved
    (
        wts, acc, dsq, sent, got, hbuf, mem, hb, act, slope, n2, r2, dfb, dz, vacc,
        bias, dca, dot, dqt, dkt, dvt, pair, cotb, tok, dx, link, swaps, sems, saved_sems, grad_sems,
    ) = refs
    section = lax.axis_index("section")
    first = section == 0
    dp = lax.axis_index("dp")
    count, tokens = y.shape[0], y.shape[2]
    other = 1 - section
    barrier = pltpu.get_barrier_semaphore()
    pl.semaphore_signal(barrier, inc=1, device_id=(other, dp), device_id_type=MESH)
    pl.semaphore_wait(barrier, 1)

    def remote(source, target, step, b):
        return pltpu.make_async_remote_copy(
            src_ref=source,
            dst_ref=target,
            send_sem=swaps.at[step, b],
            recv_sem=swaps.at[step + 1, b],
            device_id=(other, dp),
            device_id_type=MESH,
        )

    def send_memory(b):
        return remote(sent.at[b], got.at[b], 0, b)

    def send_back(b):
        return remote(sent.at[b], got.at[b], 2, b)

    def rows(b):
        return pl.ds(pl.multiple_of(b * tokens, tokens), tokens)

    def load_y(b):
        return pltpu.make_async_copy(y.at[b], hbuf.at[b % 2], sems.at[0])

    def load_cot(b):
        return pltpu.make_async_copy(cot.at[rows(b)], cotb, sems.at[1])

    def store_hidden(b):
        return pltpu.make_async_copy(tok, hidden.at[rows(b)], sems.at[2])

    def store_dy(b):
        return pltpu.make_async_copy(hbuf.at[b % 2], dy.at[b], sems.at[3])

    def load_dy(b):
        return pltpu.make_async_copy(dy.at[b], hbuf.at[b % 2], sems.at[0])

    def store_dx(b):
        return pltpu.make_async_copy(dx, dx_out.at[rows(b)], sems.at[4])

    def load_saved(b):
        return copies([ref.at[b] for ref in saved_in], saved, saved_sems)

    unit = [wts.at[pl.ds(i * D, D)] for i in range(UNITS)]
    part = 6 * D
    load_rest = pltpu.make_async_copy(
        weights.at[pl.ds(part, UNITS * D - part)], wts.at[pl.ds(part, UNITS * D - part)], sems.at[5]
    )
    load_squares = pltpu.make_async_copy(weights.at[pl.ds(0, part)], wts.at[pl.ds(0, part)], sems.at[6])
    load_link = pltpu.make_async_copy(linked, link, sems.at[7])
    load_y(0).start()
    load_rest.start()
    pl.when(jnp.logical_not(first))(lambda: load_link.start())
    load_squares.start()
    s4, s5, ffn = unit[4], unit[5], unit[6:]
    cross_acc = [acc.at[i] for i in range(2)]
    link_acc = acc.at[pl.ds(10, 2)]
    ffn_acc = [acc.at[2 + i] for i in range(2 * RU)]

    out_dsq = pltpu.make_async_copy(dsq, dsq_out, sems.at[6])

    def clear():
        acc[...] = jnp.zeros(acc.shape, F32)
        dsq[...] = jnp.zeros(dsq.shape, F32)
        dvec[...] = jnp.zeros(dvec.shape, F32)

    def run_feed_forward(h, kept=slope):
        feed_forward(h, ffn, vec, hb, act, kept, n2, r2, mem)

    def emit_hidden(b):
        pl.when(b > 0)(lambda: store_hidden(b - 1).wait())
        tok[...] = mem[...].T.astype(BF)
        store_hidden(b).start()

    def take_cotangent(b, h):
        load_cot(b).wait()
        token = lax.broadcasted_iota(jnp.int32, (D, tokens), 1)
        h[...] = jnp.where(token < info[1 + b], cotb[...].astype(F32).T, 0.0)

    def run_feed_backward(h):
        feed_backward(h, ffn, vec, hb, act, slope, n2, r2, dfb, dz, ffn_acc, dvec, vacc)

    def run_self_backward(b, h):
        pl.when(b > 0)(lambda: store_dx(b - 1).wait())
        self_backward(
            h, unit[:4], vec, first, info[1 + b], *saved, dx,
            bias, dca, dot, dqt, dkt, dvt, dsq, dvec, vacc.at[pl.ds(0, 4)], lambda: None,
        )
        store_dx(b).start()

    @pl.when(first)
    def _():
        load_rest.wait()

        def ahead(b):
            h = hbuf.at[b % 2]
            load_y(b).wait()
            pl.when(b + 1 < count)(lambda: load_y(b + 1).start())
            run_feed_forward(h, None)
            sent[b] = mem[...].astype(BF)
            send_memory(b).start()
            emit_hidden(b)

        loop(0, count, ahead)
        store_hidden(count - 1).wait()
        load_squares.wait()
        clear()
        load_y(0).start()

        def back(b):
            h = hbuf.at[b % 2]
            loads = load_saved(b)
            load_cot(b).start()
            load_y(b).wait()
            pl.when(b < count // 2)(lambda: [copy.start() for copy in loads] and None)
            run_feed_forward(h)
            take_cotangent(b, h)
            send_back(b).wait_recv()
            h[...] += got[b].astype(F32)
            run_feed_backward(h)

            @pl.when(b < count // 2)
            def _():
                load_y(b + 1).start()
                for copy in loads:
                    copy.wait()
                run_self_backward(b, h)
                pl.when(b == count // 2 - 1)(lambda: out_dsq.start())

            @pl.when(b >= count // 2)
            def _():
                store_dy(b).start()

                @pl.when(b + 1 < count)
                def _():
                    load_y(b + 1).start()
                    store_dy(b).wait()

        loop(0, count, back)
        store_dy(count - 1).wait()
        store_dx(count // 2 - 1).wait()

    @pl.when(jnp.logical_not(first))
    def _():
        clear()
        load_rest.wait()
        load_squares.wait()
        load_link.wait()

        def give_back(b):
            grad = nn(link[0:D, :], dkt[...]) + nn(link[D : 2 * D, :], dvt[...])
            sent[b] = grad.astype(BF)
            send_back(b).start()

        def both(b):
            h = hbuf.at[b % 2]
            load_cot(b).start()
            load_y(b).wait()
            send_memory(b).wait_recv()
            for i, target in enumerate((kt, vt)):
                target[...] = tn(link[pl.ds(i * D, D), :], got[b]).astype(BF)
            cross = (ut, qt, kt, vt, ot, lse, n1, r1)
            cross_forward(h, (s4, s5), vec, info[1 + count + b], *cross, pair)
            run_feed_forward(h)
            emit_hidden(b)
            take_cotangent(b, h)

            pl.when(b > 0)(lambda: store_dy(b - 1).wait())
            pl.when(b + 1 < count)(lambda: load_y(b + 1).start())
            run_feed_backward(h)
            cross_backward(
                h, (s4, s5), vec, info[1 + count + b], *cross, dca, dot, dqt,
                dkt, dvt, cross_acc, dvec, vacc, lambda: give_back(b),
            )
            for i, grad in enumerate((dkt, dvt)):
                link_acc[i] += nt(got[b], grad[...])
            store_dy(b).start()

        loop(0, count, both)
        store_hidden(count - 1).wait()
        store_dy(count - 1).wait()

        def back(b):
            loads = load_saved(b)
            for copy in loads + [load_dy(b)]:
                copy.start()
            for copy in loads + [load_dy(b)]:
                copy.wait()
            run_self_backward(b, hbuf.at[b % 2])

        loop(0, count // 2, back)
        out_dsq.start()
        store_dx(count // 2 - 1).wait()

    @pl.when(first)
    def _():
        loop(0, count, lambda b: send_memory(b).wait_send())

    @pl.when(jnp.logical_not(first))
    def _():
        loop(0, count, lambda b: send_back(b).wait_send())

    def out_grad(i):
        place = pl.ds(i * D, D)
        return pltpu.make_async_copy(wts.at[place], grads.at[place], grad_sems.at[i])

    def emit(i):
        wts[pl.ds(i * D, D), :] = acc[i].astype(BF)
        out_grad(i).start()

    crossed = (0, 1, 10, 11)

    @pl.when(jnp.logical_not(first))
    def _():
        for i in crossed:
            emit(i)

    for i in range(2, 10):
        emit(i)

    @pl.when(jnp.logical_not(first))
    def _():
        for i in crossed:
            out_grad(i).wait()

    for i in range(2, 10):
        out_grad(i).wait()
    out_dsq.wait()


def call_middle(info, vec, y, cot, weights, linked, saved):
    count, tokens = y.shape[0], y.shape[2]
    kept = saved_dims(tokens)
    wide16 = pltpu.VMEM((D, tokens), BF)
    wide32 = pltpu.VMEM((D, tokens), F32)
    tall16 = pltpu.VMEM((FF, tokens), BF)
    return pl.pallas_call(
        middle_kernel,
        name="middle",
        out_shape=[
            shape16(count * tokens, D),
            shape32(count, D, tokens),
            shape32(count * tokens, D),
            shape16(12 * D, D),
            shape32(4, D, D),
            shape32(D, LANES),
        ],
        in_specs=[smem_space(), vmem_space()] + [any_space()] * 14,
        out_specs=[any_space()] * 5 + [vmem_space()],
        scratch_shapes=[pltpu.VMEM(dims, kind) for dims, kind in kept]
        + [
            pltpu.VMEM((UNITS * D, D), BF),
            pltpu.VMEM((12, D, D), F32),
            pltpu.VMEM((4, D, D), F32),
            pltpu.VMEM((count, D, tokens), BF),
            pltpu.VMEM((count, D, tokens), BF),
            pltpu.VMEM((2, D, tokens), F32),
            wide32, wide16, tall16, tall16, wide16,
            pltpu.VMEM((1, tokens), F32),
            wide16, tall16,
            pltpu.VMEM((RU + 3, D, LANES), F32),
            pltpu.VMEM((tokens, tokens), F32),
            wide16, wide16, wide16, wide16, wide16,
            pltpu.VMEM((2, tokens, tokens), F32),
            pltpu.VMEM((tokens, D), BF),
            pltpu.VMEM((tokens, D), BF),
            pltpu.VMEM((tokens, D), F32),
            pltpu.VMEM((2 * D, D), BF),
            pltpu.SemaphoreType.DMA((4, count)),
            pltpu.SemaphoreType.DMA((8,)),
            pltpu.SemaphoreType.DMA((10,)),
            pltpu.SemaphoreType.DMA((12,)),
        ],
        compiler_params=pltpu.CompilerParams(
            collective_id=1, has_side_effects=True, vmem_limit_bytes=62 * 2**20
        ),
    )(info, vec, y, cot, weights, linked, *saved)


matrix_rate = 0.04
vector_rate = 0.25
matrix_decay = 0.01


def adam_update(weight, moment_old, square_old, gradient, learn_rate, decay_rate):
    moment_one = 0.5 * moment_old + 0.5 * gradient
    moment_two = 0.5 * square_old + 0.5 * gradient * gradient
    correction = 1.0 - 0.5**STEP
    adam_step = moment_one / correction / (jnp.sqrt(moment_two / correction) + 1e-08)
    return (weight - learn_rate * (adam_step + decay_rate * weight), moment_one, moment_two)


def adam_kernel(place, grad, weight, first, second, weight_out, first_out, second_out):
    taken = place[pl.program_id(0)] >= 0
    fresh = adam_update(weight[0], first[0], second[0], grad[...].astype(F32), matrix_rate, matrix_decay)
    for new, old, out in zip(fresh, (weight, first, second), (weight_out, first_out, second_out)):
        out[0] = jnp.where(taken, new, old[0])


def call_adam(place, grads, weight, first, second):
    slots = weight.shape[0]
    spec = block_spec(D, D)
    out = shape32(slots, D, D)
    return pl.pallas_call(
        adam_kernel,
        name="adam",
        out_shape=[out] * 3,
        grid_spec=pltpu.PrefetchScalarGridSpec(
            num_scalar_prefetch=1,
            grid=(slots,),
            in_specs=[pl.BlockSpec((D, D), lambda s, place: (jnp.maximum(place[s], 0), 0))] + [spec] * 3,
            out_specs=[spec] * 3,
        ),
    )(place, grads, weight, first, second)


def unit_tables(owner_row):
    tensor_of = np.array(TENSOR_OF)
    first_unit = np.array(FIRST_UNIT)
    owned_by = owner_row[:8]
    earlier = (owned_by[:, None] == owned_by[None, :]) & jnp.asarray(
        np.arange(8)[None, :] < np.arange(8)[:, None]
    )
    prior = jnp.sum(jnp.where(earlier, jnp.array(TENSOR_SIZE, jnp.int32)[None, :], 0), axis=1)
    unit_owner = owned_by[tensor_of]
    unit_slot = prior[tensor_of] + jnp.asarray(np.arange(UNITS) - first_unit[tensor_of], jnp.int32)
    return unit_owner, unit_slot.astype(jnp.int32)


def slot_units(owner_row, dp, slots):
    unit_owner, unit_slot = unit_tables(owner_row)
    hit = (unit_owner[None, :] == dp) & (unit_slot[None, :] == jnp.arange(slots, dtype=jnp.int32)[:, None])
    return jnp.sum(jnp.where(hit, jnp.arange(UNITS, dtype=jnp.int32)[None, :] + 1, 0), axis=1) - 1


def three_pieces(value):
    high = value.astype(BF)
    rest = value - high.astype(F32)
    mid = rest.astype(BF)
    low = (rest - mid.astype(F32)).astype(BF)
    pad = ((0, PIECE - value.shape[0]), (0, 0))
    parts = jnp.concatenate([jnp.pad(part, pad) for part in (high, mid, low)], axis=0)
    return jnp.pad(parts, ((0, VEC_ROWS - 3 * PIECE), (0, 0)))


def local(n_dp, tokens, cotangent, lengths, owners, master_sq, mom1_sq, mom2_sq, master_vec, mom1_vec, mom2_vec):
    section = lax.axis_index("section")
    dp = lax.axis_index("dp")
    count = lengths.shape[1]
    vec_store = master_vec[0, 0]
    vrows = vec_store.shape[0]
    owns_vector = owners[0, 8] == dp
    pack = three_pieces(jnp.where(owns_vector, vec_store, 0.0))
    own = jnp.where(section == 0, lengths[0], lengths[1])
    info = jnp.concatenate([section[None].astype(jnp.int32), own, lengths[0]])
    weights, vec, linked, *saved = call_start(n_dp, info, owners, tokens[0], master_sq[0, 0], pack, count)
    hidden, dy, dx, late, dsq, late_vec = call_middle(
        info, vec, saved[10], cotangent[0], weights, linked, saved[:10]
    )
    dx, total = call_finish(n_dp, info, dy, weights, vec, late, late_vec, dsq, dx, saved[:10])
    pieces = total[UNITS * D : UNITS * D + 3 * PIECE].astype(F32).reshape(3, PIECE, D)[:, :vrows]
    total_vector = pieces[0] + pieces[1] + pieces[2]
    place = slot_units(owners[0], dp, master_sq.shape[2])
    squares_new = call_adam(place, total, master_sq[0, 0], mom1_sq[0, 0], mom2_sq[0, 0])
    vector_new = adam_update(vec_store, mom1_vec[0, 0], mom2_vec[0, 0], total_vector, vector_rate, 0.0)
    vector_new = [
        jnp.where(owns_vector, new, old)
        for new, old in zip(vector_new, (vec_store, mom1_vec[0, 0], mom2_vec[0, 0]))
    ]
    return (
        hidden[None],
        dx[None],
        *[value[None, None] for value in squares_new],
        *[value[None, None] for value in vector_new],
    )


def solution(mesh):
    n_dp = mesh.shape["dp"]
    slots = P("section", "dp", None, None, None)
    packs = P("section", "dp", None, None)
    rows = P("section", "dp", None)
    return jax.shard_map(
        functools.partial(local, n_dp),
        mesh=mesh,
        in_specs=(rows, rows, P(None, "dp"), P("section", None), slots, slots, slots, packs, packs, packs),
        out_specs=(rows, rows, slots, slots, slots, packs, packs, packs),
        check_vma=False,
    )
```
